32 devices in a mesh: dom: 8 (over z, x), bin: 4 (over y, core).
Axes of the slice: x: 2, y: 2, z: 4, core: 2. Of those that a mesh axis runs over, the one named last changes fastest.
Arguments:
- displacement: float32 [3, 64, 64, 512], P(None, 'dom', 'bin'), may hold values from -0.3 to 0.3
- velocity: float32 [3, 64, 64, 512], P(None, 'dom', 'bin'), may hold values from -0.3 to 0.3
- moduli: float32 [2, 64, 64, 512], P(None, 'dom', 'bin'), may hold values from 0.2 to 2
- nodal_mass: float32 [64, 64, 512], P('dom', 'bin'), may hold values from 0.5 to 2
- segment_node: int32 [32768], P(('dom', 'bin')), may hold values from 0 to 65535
- segment_base: float32 [3, 32768], P(None, ('dom', 'bin')), may hold values from 0 to 1
- contact_bin: int32 [4, 256, 1], P(None, ('dom', 'bin')), may hold values from 0 to 3; in each aligned block of 8 rows (0 to 7, 8 to 15, ..., all dimensions but the last counted through in order) at most 4 rows name the same one
- element_tile: int32 [64, 64, 512], P('dom', 'bin'), may hold values from 0 to 8191, as said below
Outputs:
- new_displacement: float32 [3, 64, 64, 512], P(None, 'dom', 'bin')
- new_velocity: float32 [3, 64, 64, 512], P(None, 'dom', 'bin')
- tile_heat: float32 [8192], P(('dom', 'bin'))
The draws below stay inside these ranges and needn't reach their ends.
Inputs may be any that keep to these rules, and one draw needn't show every extreme that they name: `contact_bin`: in each substep no device sends more than 4 of its blocks to one bin, and at least one device sends exactly 4. `segment_node`: A node of the holding device's own block, numbered row-major over (8, 16, 512). `element_tile`: tiles are numbered device-major (256 to a device, devices in the order dom, then bin). An element's tile belongs to the device that holds it, except that elements of a device's first or last layer along the first dimension may take a tile of the device one step lower or higher along dom (same bin index).
All inputs are finite; a program needn't handle non-finite values.
Results may differ from the reference program's by a relative error of at most 0.0003.
Values sent between devices are 32-bit elements; how exact they have to be, the bound alone decides.
No kernel may reach another device: no remote copies, remote signals or barrier semaphores. Data moves between devices by JAX's collectives and lax.ppermute only.
A program may use at most 128 MiB of HBM per device.

```python
import math
import jax
import jax.numpy as jnp
import numpy as np
from jax import lax

CX = 8
CY = 16
NZ = 512
SUB = 4
SEG = 128
BLK_DEV = 8
TILE_DEV = 256
CAP = 4
NX = 64
NY = 64
BLOCKS = 256
SEGS = 32768
TILES = 8192
N_DOM = 8
N_BIN = 4


def draw_element_tile(key, part):
    pos_x = jnp.arange(NX, dtype=jnp.int32)[:, None, None]
    pos_y = jnp.arange(NY, dtype=jnp.int32)[None, :, None]
    pos_z = jnp.arange(NZ, dtype=jnp.int32)[None, None, :]
    dom_index = pos_x // CX
    bin_index = pos_y // CY
    local_x = pos_x % CX
    local_y = pos_y % CY
    local_order = (local_x * CY + local_y) * NZ + pos_z
    local_tile = local_order * TILE_DEV // (CX * CY * NZ)
    moving = jax.random.randint(jax.random.fold_in(key, 11), (NX, NY, NZ), 0, 2)
    down = jnp.logical_and(local_x == 0, dom_index > 0).astype(jnp.int32) * moving
    up = jnp.logical_and(local_x == CX - 1, dom_index < N_DOM - 1).astype(jnp.int32) * moving
    target_dom = dom_index - down + up
    device = target_dom * N_BIN + bin_index
    return (device * TILE_DEV + local_tile).astype(jnp.int32)


def place_ends(values, own_key, low, largest):
    index_at = [jax.random.randint(jax.random.fold_in(own_key, axis), (), 0, length) for axis, length in enumerate(values.shape)]
    longest = values.shape.index(max(values.shape))
    beside = index_at[:longest] + [(index_at[longest] + 1) % values.shape[longest]] + index_at[longest + 1:]
    return values.at[tuple(index_at)].set(low).at[tuple(beside)].set(largest)


def block_scale(rng, dims, cuts, low, top_value):
    def one(dim, parts):
        steps = jax.random.uniform(jax.random.fold_in(jax.random.fold_in(rng, 6), dim), (parts,), jnp.float32, low / len(cuts), top_value / len(cuts))
        return jnp.repeat(jnp.exp(steps), dims[dim] // parts).reshape((-1,) + (1,) * (len(dims) - dim - 1))

    factor_of = one(*cuts[0])
    for cut in cuts[1:]:
        factor_of = factor_of * one(*cut)
    return factor_of


def assign_block(own_key, own, number, rows, number_of, top, most, slope):
    order = jax.random.permutation(own_key, number_of)
    crowded, ordinary = load_shares(number_of, rows * top, most, slope, True), load_shares(number_of, rows * top, most, slope, False)
    places = jnp.arange(number_of)

    def named(lengths, rotation):
        used = int((lengths > 0).sum())
        fixed = max(1, used // 4)
        moved = fixed + (places - fixed + rotation * (used - fixed)) % max(1, number_of - fixed)
        return jnp.zeros((number_of,), jnp.int32).at[order[jnp.where(places < fixed, places, moved)]].set(jnp.asarray(lengths, jnp.int32))

    lengths = jnp.where(number % 4 == 0, named(crowded, number // 4), named(ordinary, number - number // 4 - 1))
    mixed = jax.random.permutation(jax.random.fold_in(own, 3), number_of)
    donor, taker = mixed[0:number_of // 2 * 2:2], mixed[1:number_of // 2 * 2:2]
    slack = jnp.minimum(lengths[donor] - 1, most - lengths[taker]) // 2
    slack = jnp.where((donor == order[0]) | (taker == order[0]) | (lengths[taker] == 0), 0, jnp.maximum(slack, 0))
    moved = jax.random.randint(jax.random.fold_in(own, 4), (number_of // 2,), 0, 1 << 20) % (slack + 1)
    lengths = lengths.at[donor].add(-moved).at[taker].add(moved)
    items = jnp.searchsorted(jnp.cumsum(lengths), jnp.arange(rows * top), side="right").astype(jnp.int32)
    grid = items.reshape(top, rows).T
    grid = grid[jax.random.permutation(jax.random.fold_in(own, 1), rows)]
    rotation = jax.random.randint(jax.random.fold_in(own, 2), (rows, 1), 0, top)
    return jnp.take_along_axis(grid, (jnp.arange(top)[None, :] + rotation) % top, axis=1)


def load_shares(count, total, most, slope, full):
    portions = [(1 << 20) // math.isqrt(rank ** slope) + 1 for rank in range(1, count + 1)]
    largest = most if full else min(most, max(-(-total // count), total * portions[0] // sum(portions)))
    least = 1 if total - largest >= count - 1 else 0
    counts, spare = [largest] + [least] * (count - 1), total - largest - least * (count - 1)
    while spare > 0:
        candidates = [i for i in range(1, count) if counts[i] < largest] or [i for i in range(1, count) if counts[i] < most]
        whole, remaining = sum([portions[i] for i in candidates]), spare
        for i in candidates:
            addition = min(most - counts[i], max(1, remaining * portions[i] // whole), spare)
            counts[i] = counts[i] + addition
            spare = spare - addition
    return np.array(counts)


def noise(rng, shape, width, limit, shards=(), held_as=jnp.bfloat16):
    result = jax.random.normal(rng, shape, jnp.float32) * width
    if len(shards) > 0:
        result = block_scale(rng, shape, shards, -0.22, 0.18) * result
    return jnp.clip(result, min=-limit, max=limit).astype(held_as)


def setup_inputs(seed: int = 0) -> dict:
    arg_keys = jax.random.split(jax.random.key(seed), 9)
    displacement = noise(arg_keys[0], (3, NX, NY, NZ), 0.05, 0.3, ((1, 8), (2, 4)), jnp.float32)
    velocity = noise(arg_keys[1], (3, NX, NY, NZ), 0.05, 0.3, ((1, 8), (2, 4)), jnp.float32)
    moduli = jnp.clip(jnp.exp(math.log(2.0) - 2.3025851 * jax.random.uniform(arg_keys[2], (2, NX, NY, NZ), jnp.float32) ** block_scale(arg_keys[2], (2, NX, NY, NZ), ((1, 8), (2, 4)), -0.2, 0.2)), 0.2, 2.0)
    nodal_mass = jnp.clip(jnp.exp(math.log(2.0) - 1.3862944 * jax.random.uniform(arg_keys[3], (NX, NY, NZ), jnp.float32) ** block_scale(arg_keys[3], (NX, NY, NZ), ((0, 8), (1, 4)), -0.2, 0.2)), 0.5, 2.0)
    segment_node = place_ends(jax.random.randint(arg_keys[4], (SEGS,), 0, CX * CY * NZ), jax.random.fold_in(arg_keys[4], 1), 0, (CX * CY * NZ) - 1).astype(jnp.int32)
    segment_base = jnp.clip(1.0 * jax.random.uniform(arg_keys[5], (3, SEGS), jnp.float32) ** block_scale(arg_keys[5], (3, SEGS), ((1, 32),), -0.2, 0.2), 0.0, 1.0)
    contact_bin_keys = jax.random.split(jax.random.fold_in(arg_keys[6], 1), SUB * BLOCKS // BLK_DEV)
    contact_bin_turns = jax.random.permutation(jax.random.fold_in(arg_keys[6], 3), SUB * BLOCKS // BLK_DEV)
    contact_bin = jax.vmap(lambda own, number: assign_block(jax.random.fold_in(arg_keys[6], 2), own, number, BLK_DEV, N_BIN, 1, CAP, 2))(contact_bin_keys, contact_bin_turns).reshape((SUB, BLOCKS, 1))
    element_tile = draw_element_tile(jax.random.fold_in(arg_keys[8], 71), 0)
    return {"displacement": displacement, "velocity": velocity, "moduli": moduli, "nodal_mass": nodal_mass, "segment_node": segment_node, "segment_base": segment_base, "contact_bin": contact_bin, "element_tile": element_tile}


RADIUS = 0.09
PENALTY = 4.0
SHORT_GAIN = 100.0
TIME_STEP = 0.2
CORNERS = ((0, 0, 0), (0, 0, 1), (0, 1, 0), (0, 1, 1), (1, 0, 0), (1, 0, 1), (1, 1, 0), (1, 1, 1))

def corner_forces(padded, moduli_used, extent_x, extent_y):
    pieces = []
    for a, b, c in CORNERS:
        piece = padded[:, a:a + extent_x, b:b + extent_y]
        if c == 1:
            piece = jnp.roll(piece, -1, axis=3)
        pieces.append(piece)
    corner_signs = [[2 * bit - 1 for bit in corner] for corner in CORNERS]
    gradient = [[0.25 * sum((corner_signs[k][q] * pieces[k][p] for k in range(8))) for q in range(3)] for p in range(3)]
    volume_strain = gradient[0][0] + gradient[1][1] + gradient[2][2]
    stress = [[moduli_used[1] * (gradient[p][q] + gradient[q][p]) + (moduli_used[0] * volume_strain if p == q else 0.0) for q in range(3)] for p in range(3)]
    corner_list = []
    for k in range(8):
        corner_list.append(jnp.stack([-0.25 * sum((corner_signs[k][q] * stress[p][q] for q in range(3))) for p in range(3)]))
    return corner_list

def spread_corners(corner_list):
    nodal = 0.0
    for k in range(8):
        a, b, c = CORNERS[k]
        moved = jnp.roll(corner_list[k], c, axis=3)
        nodal = nodal + jnp.pad(moved, ((0, 0), (a, 1 - a), (b, 1 - b), (0, 0)))
    return nodal

def contact_terms(segment_pool, alive_mask):
    row_blocks = segment_pool.reshape(3, -1, SEG).transpose(1, 0, 2)

    def one_block(target):
        offsets = target[:, :, None] - segment_pool[:, None, :]
        distance = jnp.sqrt(lax.optimization_barrier(jnp.sum(offsets * offsets, axis=0)))
        pressure = jnp.maximum(RADIUS - distance, 0.0) * alive_mask[None, :]
        pushing = PENALTY * lax.optimization_barrier(jnp.sum(offsets * (pressure / jnp.maximum(distance, 0.25 * RADIUS))[None], axis=2))
        heating = SHORT_GAIN * lax.optimization_barrier(jnp.sum(pressure * pressure, axis=1))
        return (pushing, heating)
    return lax.map(one_block, row_blocks)

def reference(displacement, velocity, moduli, nodal_mass, segment_node, segment_base, contact_bin, element_tile):
    devices = N_DOM * N_BIN
    owner = jnp.arange(SEGS, dtype=jnp.int32) // (BLK_DEV * SEG)
    grid_x = owner // N_BIN * CX + segment_node // (CY * NZ)
    grid_y = owner % N_BIN * CY + segment_node // NZ % CY
    grid_z = segment_node % NZ
    segment_tile = element_tile[grid_x, grid_y, grid_z]
    block_owner = jnp.arange(BLOCKS, dtype=jnp.int32) // BLK_DEV
    source = block_owner % N_BIN
    tile_heat = jnp.zeros((TILES,), jnp.float32)
    for step in range(SUB):
        points = segment_base + displacement[:, grid_x, grid_y, grid_z]
        target_bin = contact_bin[step, :, 0]
        onehot = (target_bin.reshape(devices, BLK_DEV)[:, :, None] == jnp.arange(N_BIN, dtype=jnp.int32)[None, None, :]).astype(jnp.int32)
        slot_rank = jnp.cumsum(onehot, axis=1) - onehot
        slot_index = lax.optimization_barrier(jnp.sum(slot_rank * onehot, axis=2)).reshape(BLOCKS)
        group = block_owner // N_BIN * N_BIN + target_bin
        blocks = points.reshape(3, BLOCKS, SEG).transpose(1, 0, 2)
        buffers = jnp.zeros((devices, N_BIN, CAP, 3, SEG), jnp.float32).at[group, source, slot_index].set(blocks)
        alive = jnp.zeros((devices, N_BIN, CAP), jnp.float32).at[group, source, slot_index].set(1.0)

        def per_group(pair):
            group_buffer, group_alive = pair
            segment_pool = group_buffer.transpose(2, 0, 1, 3).reshape(3, -1)
            alive_mask = jnp.repeat(group_alive.reshape(-1), SEG)
            pushing, heating = contact_terms(segment_pool, alive_mask)
            return (pushing.reshape(N_BIN, CAP, 3, SEG), heating.reshape(N_BIN, CAP, SEG))
        push_all, heat_all = lax.map(per_group, (buffers, alive))
        segment_push = push_all[group, source, slot_index].transpose(1, 0, 2).reshape(3, SEGS)
        segment_heat = heat_all[group, source, slot_index].reshape(SEGS)
        tile_heat = tile_heat + jax.ops.segment_sum(segment_heat, segment_tile, num_segments=TILES)
        contact = jnp.zeros((3, NX, NY, NZ), jnp.float32).at[:, grid_x, grid_y, grid_z].add(segment_push)
        padded = jnp.pad(displacement, ((0, 0), (0, 1), (0, 1), (0, 0)))
        internal = spread_corners(corner_forces(padded, moduli, NX, NY))[:, :NX, :NY]
        velocity = velocity + TIME_STEP * (internal + contact) / nodal_mass[None]
        displacement = displacement + TIME_STEP * velocity
    return (displacement, velocity, tile_heat)
```

```python
import functools
import jax
import jax.numpy as jnp
from jax import lax
from jax.experimental import pallas as pl
from jax.experimental.pallas import tpu as pltpu
from jax.sharding import PartitionSpec as P

SEG = 128
TILE_DEV = 256
RADIUS = 0.09
PENALTY = 4.0
SHORT_GAIN = 100.0
TIME_STEP = 0.2
VMEM_BYTES = 40 * 1024 * 1024
F32 = jnp.float32
BF16 = jnp.bfloat16
WHOLE = pl.BlockSpec(memory_space=pltpu.VMEM)
SCALARS = pl.BlockSpec(memory_space=pltpu.SMEM)
NT = (((1,), (1,)), ((), ()))


def shifted(value, axis, steps):
    count = lax.axis_size(axis)
    first, last = (max(0, -steps), min(count, count - steps))
    return lax.ppermute(value, axis, [(source, source + steps) for source in range(first, last)])


def cycled(value, axis, steps):
    count = lax.axis_size(axis)
    return lax.ppermute(value, axis, [(source, (source + steps) % count) for source in range(count)])


def call(body, outs, scratch=(), flops=1_000_000, specs=None):
    return functools.partial(
        pl.pallas_call,
        body,
        out_shape=outs,
        out_specs=[WHOLE] * len(outs),
        scratch_shapes=list(scratch),
        compiler_params=pltpu.CompilerParams(vmem_limit_bytes=VMEM_BYTES),
        cost_estimate=pl.CostEstimate(flops=flops, bytes_accessed=4_000_000, transcendentals=0),
    )(in_specs=specs)


def split_two(value):
    high = value.astype(BF16)
    return high, (value - high.astype(F32)).astype(BF16)


def node_split(node_ref, extent_z):
    node = jnp.concatenate([node_ref[j : j + 1, :] for j in range(node_ref.shape[0])], axis=1)
    return lax.div(node, jnp.int32(extent_z)), lax.rem(node, jnp.int32(extent_z))


def one_hot_z(column, extent_z):
    depth = lax.broadcasted_iota(jnp.int32, (extent_z, column.shape[1]), 0)
    return jnp.where(depth == column, 1.0, 0.0).astype(BF16)


def gather_nodes(pieces, row, hot):
    rows = pieces[0].shape[0]
    picked = sum(jnp.dot(piece, hot, preferred_element_type=F32) for piece in pieces)
    at_row = lax.broadcasted_iota(jnp.int32, (rows, row.shape[1]), 0) == row
    return jnp.sum(jnp.where(at_row, picked, 0.0), axis=0, keepdims=True)


def store_positions(disp_ref, base_ref, node_ref, targets):
    extent_x, extent_y, extent_z = disp_ref.shape[1:]
    rows = extent_x * extent_y
    blocks = node_ref.shape[0]
    row, column = node_split(node_ref, extent_z)
    hot = one_hot_z(column, extent_z)
    for p in range(3):
        plane = disp_ref[p].reshape(rows, extent_z)
        points = base_ref[p : p + 1, :] + gather_nodes(split_two(plane), row, hot)
        tile = jnp.concatenate([points[:, j * SEG : (j + 1) * SEG] for j in range(blocks)], axis=0)
        for ref, lane in targets:
            ref[p * blocks : (p + 1) * blocks, lane : lane + SEG] = tile


def store_column(source_ref, at, target_ref, first):
    count, extent_x, _, extent_z = source_ref.shape
    for p in range(count):
        tile = jnp.concatenate([source_ref[p, x, at : at + 1, :] for x in range(extent_x)], axis=0)
        target_ref[first + p * extent_x : first + (p + 1) * extent_x, 0:extent_z] = tile


def store_messages(disp_ref, base_ref, node_ref, up_ref, down_ref, far_ref):
    extent_y, extent_z = disp_ref.shape[2:]
    store_column(disp_ref, extent_y - 1, up_ref, 0)
    store_column(disp_ref, 0, down_ref, 0)
    store_positions(disp_ref, base_ref, node_ref, [(up_ref, extent_z), (down_ref, extent_z), (far_ref, 0)])


def first_body(disp_ref, base_ref, node_ref, moduli_ref, bins_ref, up_ref, down_ref, far_ref):
    _, extent_x, extent_y, extent_z = disp_ref.shape
    store_messages(disp_ref, base_ref, node_ref, up_ref, down_ref, far_ref)
    rows = 3 * extent_x
    store_column(moduli_ref, extent_y - 1, up_ref, rows)
    bins = bins_ref[...]
    zeros = jnp.zeros((8, SEG), F32)
    up_ref[rows : rows + 8, extent_z:] = bins
    up_ref[rows + 8 : rows + 16, extent_z:] = zeros
    down_ref[rows : rows + 8, 0:extent_z] = jnp.zeros((8, extent_z), F32)
    down_ref[rows : rows + 8, extent_z:] = bins
    far_ref[rows : rows + 8, :] = bins


def layer_body(with_moduli, *refs):
    if with_moduli:
        flag_ref, first_ref, last_ref, lower_ref, upper_ref, moduli_ref, up_ref, down_ref = refs
    else:
        flag_ref, first_ref, last_ref, lower_ref, upper_ref, up_ref, down_ref = refs
    extent_y, extent_z = first_ref.shape[2:]
    extent_x = 8
    has_lower, has_upper = flag_ref[0], flag_ref[1]
    main = 3 * extent_y
    for x, source_ref, target_ref in ((0, first_ref, down_ref), (extent_x - 1, last_ref, up_ref)):
        for p in range(3):
            target_ref[p * extent_y : (p + 1) * extent_y, :] = source_ref[p, 0]
        above = [upper_ref[p * extent_x + x : p * extent_x + x + 1, 0:extent_z] * has_upper for p in range(3)]
        below = [lower_ref[p * extent_x + x : p * extent_x + x + 1, 0:extent_z] * has_lower for p in range(3)]
        if with_moduli and x > 0:
            first = 3 * extent_x + x
            rest = [lower_ref[first + m * extent_x : first + m * extent_x + 1, 0:extent_z] * has_lower for m in range(2)]
        else:
            rest = [jnp.zeros((2, extent_z), F32)]
        target_ref[main : main + 8, :] = jnp.concatenate(above + below + rest, axis=0)
    if with_moduli:
        for m in range(2):
            up_ref[main + 8 + m * extent_y : main + 8 + (m + 1) * extent_y, :] = moduli_ref[m, 0]


def pair_body(blocks, bin_count, last, *refs):
    if last:
        (bins_ref, own_ref, lower_ref, upper_ref, far_ref, node_ref, heat_ref, tile_ref,
         contact_ref, partial_ref, spread, listed, push) = refs
    else:
        (bins_ref, own_ref, lower_ref, upper_ref, far_ref, node_ref, heat_ref,
         contact_ref, total_ref, spread, listed, push) = refs
    total_blocks = blocks * bin_count
    extent_z = contact_ref.shape[1]
    rows = contact_ref.shape[0] // 3
    counts = [jnp.int32(0)] * bin_count
    for i in range(total_blocks):
        named = bins_ref[i]
        taken = counts[0]
        for b in range(1, bin_count):
            taken = jnp.where(named == b, counts[b], taken)
        listed[named * total_blocks + taken] = i
        counts = [count + (named == b).astype(jnp.int32) for b, count in enumerate(counts)]
    sources = [own_ref[...], lower_ref[...], upper_ref[...]] + [far_ref[s] for s in range(far_ref.shape[0])]
    for d, source in enumerate(sources):
        turned = source.T
        for p in range(3):
            for j in range(blocks):
                at = p * blocks + j
                spread[d * blocks + j, p] = jnp.broadcast_to(turned[:, at : at + 1], (SEG, SEG))
    heats = []
    for j in range(blocks):
        named = bins_ref[j]
        count = counts[0]
        for b in range(1, bin_count):
            count = jnp.where(named == b, counts[b], count)
        point = [jnp.broadcast_to(own_ref[p * blocks + j : p * blocks + j + 1, :], (8, SEG)) for p in range(3)]

        def against(i, sums):
            other = listed[named * total_blocks + i]
            sums = list(sums)
            for g in range(SEG // 8):
                delta = [point[p] - spread[other, p, g * 8 : (g + 1) * 8, :] for p in range(3)]
                square = delta[0] * delta[0] + delta[1] * delta[1] + delta[2] * delta[2]
                inverse = lax.rsqrt(jnp.maximum(square, 1e-30))
                pressure = jnp.maximum(RADIUS - square * inverse, 0.0)
                factor = pressure * jnp.minimum(inverse, 1.0 / (0.25 * RADIUS))
                for p in range(3):
                    sums[p] = sums[p] + factor * delta[p]
                sums[3] = sums[3] + pressure * pressure
            return tuple(sums)

        sums = lax.fori_loop(0, count, against, (jnp.zeros((8, SEG), F32),) * 4)
        for p in range(3):
            push[p : p + 1, j * SEG : (j + 1) * SEG] = PENALTY * jnp.sum(sums[p], axis=0, keepdims=True)
        heats.append(SHORT_GAIN * jnp.sum(sums[3], axis=0, keepdims=True))
    row, column = node_split(node_ref, extent_z)
    hot = one_hot_z(column, extent_z)
    at_row = lax.broadcasted_iota(jnp.int32, (rows, row.shape[1]), 0) == row
    for p in range(3):
        placed = jnp.where(at_row, push[p : p + 1, :], 0.0)
        contact_ref[p * rows : (p + 1) * rows, :] = sum(
            lax.dot_general(piece, hot, NT, preferred_element_type=F32) for piece in split_two(placed)
        )
    total = heat_ref[...] + jnp.concatenate(heats, axis=0)
    if not last:
        total_ref[...] = total
        return
    flat = jnp.concatenate([total[j : j + 1, :] for j in range(blocks)], axis=1)
    side, slot = tile_ref[0:1, :], tile_ref[1:2, :]
    hot_slot = one_hot_z(slot, TILE_DEV)
    at_side = lax.broadcasted_iota(jnp.int32, (8, flat.shape[1]), 0) == side
    placed = jnp.where(at_side, flat, 0.0)
    high, low = split_two(placed)
    lowest = (placed - high.astype(F32) - low.astype(F32)).astype(BF16)
    partial_ref[...] = sum(
        lax.dot_general(piece, hot_slot, NT, preferred_element_type=F32) for piece in (high, low, lowest)
    )


def tile_body(own_ref, bin_count, tiles_ref, node_ref, out_ref):
    extent_x, extent_y, extent_z = tiles_ref.shape
    row, column = node_split(node_ref, extent_z)
    hot = one_hot_z(column, extent_z)
    tiles = tiles_ref[...].reshape(extent_x * extent_y, extent_z)
    device = lax.div(tiles, jnp.int32(TILE_DEV))
    slot = tiles - device * TILE_DEV
    offset = (device - own_ref[0]).astype(F32).astype(BF16)
    found = gather_nodes([offset], row, hot)
    side = jnp.where(found < -0.5, 0, jnp.where(found > 0.5, 2, 1))
    found_slot = gather_nodes([slot.astype(F32).astype(BF16)], row, hot).astype(jnp.int32)
    rest = jnp.zeros((6, row.shape[1]), jnp.int32)
    out_ref[...] = jnp.concatenate([side, found_slot, rest], axis=0)


def update_body(first, last, *refs):
    refs = list(refs)
    take = lambda count: [refs.pop(0) for _ in range(count)]
    flag_ref, disp_ref, vel_ref, mass_ref, moduli_ref, contact_ref, lower_ref, upper_ref, back_ref, front_ref = take(10)
    if not last:
        base_ref, node_ref = take(2)
    new_disp_ref, new_vel_ref = take(2)
    if not last:
        up_ref, down_ref, far_ref = take(3)
    if first:
        (scaled,) = take(1)
    else:
        scaled = moduli_ref
    field, feature, stress = take(3)
    _, extent_x, extent_y, extent_z = disp_ref.shape
    padded_y = extent_y + 8
    has_lower, has_upper = flag_ref[0], flag_ref[1]
    place = lax.broadcasted_iota(jnp.int32, (8, extent_z), 0)

    def halo_tile(above, below):
        return jnp.where(place == 0, above, jnp.where(place == 7, below, 0.0))

    for p in range(3):
        for x in range(extent_x):
            at = p * extent_x + x
            field[p, x + 1, 0:extent_y, :] = disp_ref[p, x]
            field[p, x + 1, extent_y:padded_y, :] = halo_tile(
                upper_ref[at : at + 1, 0:extent_z] * has_upper, lower_ref[at : at + 1, 0:extent_z] * has_lower
            )
        for x, layer_ref in ((0, back_ref), (extent_x + 1, front_ref)):
            main = 3 * extent_y
            field[p, x, 0:extent_y, :] = layer_ref[p * extent_y : (p + 1) * extent_y, :]
            field[p, x, extent_y:padded_y, :] = halo_tile(
                layer_ref[main + p : main + p + 1, :], layer_ref[main + 3 + p : main + 4 + p, :]
            )
    if first:
        scale = -1.0 / 16.0
        main = 3 * extent_y
        for m in range(2):
            for x in range(extent_x):
                at = (3 + m) * extent_x + x
                scaled[m, x + 1, 0:extent_y, :] = moduli_ref[m, x] * scale
                below = lower_ref[at : at + 1, 0:extent_z] * (has_lower * scale)
                scaled[m, x + 1, extent_y:padded_y, :] = jnp.where(place == 7, below, 0.0)
            begin = main + 8 + m * extent_y
            scaled[m, 0, 0:extent_y, :] = back_ref[begin : begin + extent_y, :] * scale
            below = back_ref[main + 6 + m : main + 7 + m, :] * scale
            scaled[m, 0, extent_y:padded_y, :] = jnp.where(place == 7, below, 0.0)

    def features(x, carry):
        for p in range(3):
            value = field[p, x]
            ahead = pltpu.roll(value, padded_y - 1, 0)
            total, change = value + ahead, ahead - value
            total_z, change_z = pltpu.roll(total, extent_z - 1, 1), pltpu.roll(change, extent_z - 1, 1)
            feature[x, p] = total + total_z
            feature[x, 3 + p] = change + change_z
            feature[x, 6 + p] = total_z - total
        return carry

    lax.fori_loop(0, extent_x + 2, features, 0)

    def stresses(x, carry):
        for t in range(padded_y // 8):
            rows = slice(t * 8, t * 8 + 8)
            along_x = [feature[x + 1, p, rows] - feature[x, p, rows] for p in range(3)]
            along_y = [feature[x + 1, 3 + p, rows] + feature[x, 3 + p, rows] for p in range(3)]
            along_z = [feature[x + 1, 6 + p, rows] + feature[x, 6 + p, rows] for p in range(3)]
            volume = scaled[0, x, rows] * (along_x[0] + along_y[1] + along_z[2])
            shear = scaled[1, x, rows]
            twice = shear + shear
            stress[x, 0, rows] = twice * along_x[0] + volume
            stress[x, 1, rows] = twice * along_y[1] + volume
            stress[x, 2, rows] = twice * along_z[2] + volume
            stress[x, 3, rows] = shear * (along_y[0] + along_x[1])
            stress[x, 4, rows] = shear * (along_z[0] + along_x[2])
            stress[x, 5, rows] = shear * (along_z[1] + along_y[2])
        return carry

    lax.fori_loop(0, extent_x + 1, stresses, 0)
    which = ((0, 3, 4), (3, 1, 5), (4, 5, 2))

    def forces(x, carry):
        step_mass = TIME_STEP / mass_ref[x]
        for p in range(3):
            of_x, of_y, of_z = which[p]
            part_x = stress[x, of_x] - stress[x + 1, of_x]
            part_y = stress[x, of_y] + stress[x + 1, of_y]
            part_z = stress[x, of_z] + stress[x + 1, of_z]
            plain = (part_x - part_y)[:extent_y] + pltpu.roll(part_x + part_y, 1, 0)[:extent_y]
            slope = part_z[:extent_y] + pltpu.roll(part_z, 1, 0)[:extent_y]
            internal = (plain - slope) + pltpu.roll(plain + slope, 1, 1)
            at = pl.ds(pl.multiple_of((p * extent_x + x) * extent_y, 8), extent_y)
            speed = vel_ref[p, x] + step_mass * (internal + contact_ref[at, :])
            new_vel_ref[p, x] = speed
            new_disp_ref[p, x] = disp_ref[p, x] + TIME_STEP * speed
        return carry

    lax.fori_loop(0, extent_x, forces, 0)
    if not last:
        store_messages(new_disp_ref, base_ref, node_ref, up_ref, down_ref, far_ref)


def per_device(displacement, velocity, moduli, nodal_mass, segment_node, segment_base, contact_bin, element_tile):
    shape = displacement.shape
    _, extent_x, extent_y, extent_z = shape
    steps = contact_bin.shape[0]
    segments = segment_node.shape[0]
    blocks = segments // SEG
    bin_count = lax.axis_size("bin")
    bin_at = lax.axis_index("bin")
    own_device = lax.axis_index("dom") * bin_count + bin_at
    flags = jnp.stack([bin_at > 0, bin_at < bin_count - 1]).astype(F32)
    node = segment_node.reshape(blocks, SEG)
    bins = contact_bin[:, :, 0].astype(F32)
    bins = jnp.pad(bins, ((0, 8 - steps), (0, SEG - blocks)))
    rows = 3 * extent_x
    wide = extent_z + SEG
    struct = lambda *dims: jax.ShapeDtypeStruct(dims, F32)
    padded_y = extent_y + 8
    layer_rows = 3 * extent_y + 8

    up, down, far = call(first_body, [struct(rows + 16, wide), struct(rows + 8, wide), struct(rows + 8, SEG)], specs=[WHOLE] * 5)(
        displacement, segment_base, node, moduli, bins
    )
    tile_places = pl.pallas_call(
        lambda own, tiles, nodes, out: tile_body(own, bin_count, tiles, nodes, out),
        out_shape=jax.ShapeDtypeStruct((8, segments), jnp.int32),
        in_specs=[SCALARS, WHOLE, WHOLE],
        out_specs=WHOLE,
        compiler_params=pltpu.CompilerParams(vmem_limit_bytes=VMEM_BYTES),
        cost_estimate=pl.CostEstimate(flops=1_000_000, bytes_accessed=4_000_000, transcendentals=0),
    )(own_device[None].astype(jnp.int32), element_tile, node)
    heat = jnp.zeros((blocks, SEG), F32)
    scaled = None
    for step in range(steps):
        lower = cycled(up, "bin", 1)
        upper = cycled(down, "bin", -1)
        others = [cycled(far, "bin", shift) for shift in range(2, bin_count - 1)]
        first, last = step == 0, step == steps - 1
        if first:
            of_bins = [bins[:steps, :blocks]]
            of_bins += [v[rows : rows + steps, extent_z : extent_z + blocks] for v in (lower, upper)]
            of_bins += [v[rows : rows + steps, :blocks] for v in others]
            all_bins = jnp.concatenate(of_bins, axis=1).astype(jnp.int32)
        layer = lambda at: pl.BlockSpec((3, 1, extent_y, extent_z), lambda i: (0, at, 0, 0))
        full = lambda v: pl.BlockSpec(v.shape, lambda i: (0,) * v.ndim)
        up_rows = layer_rows + (2 * extent_y if first else 0)
        layer_args = [flags, displacement, displacement, lower, upper]
        layer_specs = [SCALARS, layer(0), layer(extent_x - 1), full(lower), full(upper)]
        if first:
            layer_args.append(moduli)
            layer_specs.append(pl.BlockSpec((2, 1, extent_y, extent_z), lambda i: (0, extent_x - 1, 0, 0)))
        to_front, to_back = pl.pallas_call(
            functools.partial(layer_body, first),
            grid=(1,),
            out_shape=[struct(up_rows, extent_z), struct(layer_rows, extent_z)],
            in_specs=layer_specs,
            out_specs=[pl.BlockSpec((up_rows, extent_z), lambda i: (0, 0)), pl.BlockSpec((layer_rows, extent_z), lambda i: (0, 0))],
            compiler_params=pltpu.CompilerParams(vmem_limit_bytes=VMEM_BYTES),
            cost_estimate=pl.CostEstimate(flops=100_000, bytes_accessed=500_000, transcendentals=0),
        )(*layer_args)
        back = shifted(to_front, "dom", 1)
        front = shifted(to_back, "dom", -1)
        pair_args = [
            all_bins[step],
            far[:rows],
            lower[:rows, extent_z:],
            upper[:rows, extent_z:],
            jnp.stack([v[:rows] for v in others]),
            node,
            heat,
        ]
        pair_specs = [SCALARS] + [WHOLE] * 6
        if last:
            pair_args.append(tile_places)
            pair_specs.append(WHOLE)
        contact, heat = call(
            functools.partial(pair_body, blocks, bin_count, last),
            [struct(3 * extent_x * extent_y, extent_z), struct(8, TILE_DEV) if last else struct(blocks, SEG)],
            [
                pltpu.VMEM((blocks * bin_count, 3, SEG, SEG), F32),
                pltpu.SMEM((bin_count * blocks * bin_count,), jnp.int32),
                pltpu.VMEM((8, segments), F32),
            ],
            100_000_000,
            pair_specs,
        )(*pair_args)
        update_args = [flags, displacement, velocity, nodal_mass, moduli if first else scaled, contact, lower, upper, back, front]
        update_outs = [struct(*shape), struct(*shape)]
        if not last:
            update_args += [segment_base, node]
            update_outs += [struct(rows, wide), struct(rows, wide), struct(rows, SEG)]
        if first:
            update_outs.append(struct(2, extent_x + 1, padded_y, extent_z))
        made = call(
            functools.partial(update_body, first, last),
            update_outs,
            [
                pltpu.VMEM((3, extent_x + 2, padded_y, extent_z), F32),
                pltpu.VMEM((extent_x + 2, 9, padded_y, extent_z), F32),
                pltpu.VMEM((extent_x + 1, 6, padded_y, extent_z), F32),
            ],
            20_000_000,
            [SCALARS] + [WHOLE] * (len(update_args) - 1),
        )(*update_args)
        displacement, velocity = made[:2]
        if not last:
            up, down, far = made[2:5]
        if first:
            scaled = made[-1]
    tile_heat = heat[1] + shifted(heat[0], "dom", -1) + shifted(heat[2], "dom", 1)
    return displacement, velocity, tile_heat


def solution(mesh):
    placed = (
        P(None, "dom", "bin", None),
        P(None, "dom", "bin", None),
        P(None, "dom", "bin", None),
        P("dom", "bin", None),
        P(("dom", "bin")),
        P(None, ("dom", "bin")),
        P(None, ("dom", "bin"), None),
        P("dom", "bin", None),
    )
    return jax.shard_map(
        per_device,
        mesh=mesh,
        in_specs=placed,
        out_specs=(P(None, "dom", "bin", None), P(None, "dom", "bin", None), P(("dom", "bin"))),
        check_vma=False,
    )
```

```python
import functools
import jax
import jax.numpy as jnp
from jax import lax
from jax.experimental import pallas as pl
from jax.experimental.pallas import tpu as pltpu
from jax.sharding import PartitionSpec as P

SEG = 128
TILE_DEV = 256
RADIUS = 0.09
PENALTY = 4.0
SHORT_GAIN = 100.0
TIME_STEP = 0.2
VMEM_BYTES = 40 * 1024 * 1024
F32 = jnp.float32
BF16 = jnp.bfloat16
WHOLE = pl.BlockSpec(memory_space=pltpu.VMEM)
SCALARS = pl.BlockSpec(memory_space=pltpu.SMEM)
NT = (((1,), (1,)), ((), ()))


def cycled(value, axis, steps):
    count = lax.axis_size(axis)
    return lax.ppermute(value, axis, [(source, (source + steps) % count) for source in range(count)])


def call(body, outs, scratch=(), flops=1_000_000, specs=None):
    return functools.partial(
        pl.pallas_call,
        body,
        out_shape=outs,
        out_specs=[WHOLE] * len(outs),
        scratch_shapes=list(scratch),
        compiler_params=pltpu.CompilerParams(vmem_limit_bytes=VMEM_BYTES),
        cost_estimate=pl.CostEstimate(flops=flops, bytes_accessed=4_000_000, transcendentals=0),
    )(in_specs=specs)


def split_two(value):
    high = value.astype(BF16)
    return high, (value - high.astype(F32)).astype(BF16)


def node_split(node_ref, extent_z):
    node = jnp.concatenate([node_ref[j : j + 1, :] for j in range(node_ref.shape[0])], axis=1)
    return lax.div(node, jnp.int32(extent_z)), lax.rem(node, jnp.int32(extent_z))


def one_hot_z(column, extent_z):
    depth = lax.broadcasted_iota(jnp.int32, (extent_z, column.shape[1]), 0)
    return jnp.where(depth == column, 1.0, 0.0).astype(BF16)


def gather_nodes(pieces, row, hot):
    rows = pieces[0].shape[0]
    picked = sum(jnp.dot(piece, hot, preferred_element_type=F32) for piece in pieces)
    at_row = lax.broadcasted_iota(jnp.int32, (rows, row.shape[1]), 0) == row
    return jnp.sum(jnp.where(at_row, picked, 0.0), axis=0, keepdims=True)


def store_positions(disp_ref, base_ref, node_ref, hot, targets):
    extent_x, extent_y, extent_z = disp_ref.shape[1:]
    rows = extent_x * extent_y
    blocks = node_ref.shape[0]
    row, _ = node_split(node_ref, extent_z)
    for p in range(3):
        plane = disp_ref[p].reshape(rows, extent_z)
        points = base_ref[p : p + 1, :] + gather_nodes(split_two(plane), row, hot)
        tile = jnp.concatenate([points[:, j * SEG : (j + 1) * SEG] for j in range(blocks)], axis=0)
        for ref, lane in targets:
            ref[p * blocks : (p + 1) * blocks, lane : lane + SEG] = tile


def store_column(source_ref, at, target_ref, first):
    count, extent_x, _, extent_z = source_ref.shape
    for p in range(count):
        tile = jnp.concatenate([source_ref[p, x, at : at + 1, :] for x in range(extent_x)], axis=0)
        target_ref[first + p * extent_x : first + (p + 1) * extent_x, 0:extent_z] = tile


def store_messages(disp_ref, base_ref, node_ref, hot, up_ref, down_ref, far_ref):
    extent_y, extent_z = disp_ref.shape[2:]
    store_column(disp_ref, extent_y - 1, up_ref, 0)
    store_column(disp_ref, 0, down_ref, 0)
    store_positions(disp_ref, base_ref, node_ref, hot, [(up_ref, extent_z), (down_ref, extent_z), (far_ref, 0)])


def first_body(disp_ref, base_ref, node_ref, moduli_ref, bins_ref, up_ref, down_ref, far_ref, hot_ref):
    _, extent_x, extent_y, extent_z = disp_ref.shape
    _, column = node_split(node_ref, extent_z)
    hot_ref[...] = one_hot_z(column, extent_z)
    store_messages(disp_ref, base_ref, node_ref, hot_ref[...], up_ref, down_ref, far_ref)
    rows = 3 * extent_x
    store_column(moduli_ref, extent_y - 1, up_ref, rows)
    bins = bins_ref[...]
    zeros = jnp.zeros((8, SEG), F32)
    up_ref[rows : rows + 8, extent_z:] = bins
    up_ref[rows + 8 : rows + 16, extent_z:] = zeros
    down_ref[rows : rows + 8, 0:extent_z] = jnp.zeros((8, extent_z), F32)
    down_ref[rows : rows + 8, extent_z:] = bins
    far_ref[rows : rows + 8, :] = bins


def layer_body(with_moduli, *refs):
    flag_ref, first_ref, last_ref, lower_ref, upper_ref, own_ref, far_ref = refs[:7]
    if with_moduli:
        moduli_ref, even_ref, odd_ref, points_ref = refs[7:]
    else:
        even_ref, odd_ref, points_ref = refs[7:]
    extent_y, extent_z = first_ref.shape[2:]
    rows = points_ref.shape[1]
    extent_x = rows // 3
    has_lower, has_upper, is_odd = flag_ref[0], flag_ref[1], flag_ref[4] > 0.5
    main = 3 * extent_y
    for p in range(3):
        low, high = first_ref[p, 0], last_ref[p, 0]
        even_ref[p * extent_y : (p + 1) * extent_y, :] = jnp.where(is_odd, low, high)
        odd_ref[p * extent_y : (p + 1) * extent_y, :] = jnp.where(is_odd, high, low)
    edges = []
    for x in (0, extent_x - 1):
        at = [p * extent_x + x for p in range(3)]
        above = [upper_ref[i : i + 1, 0:extent_z] * has_upper for i in at]
        below = [lower_ref[i : i + 1, 0:extent_z] * has_lower for i in at]
        if with_moduli:
            at = [(3 + m) * extent_x + extent_x - 1 for m in range(2)]
            rest = [lower_ref[i : i + 1, 0:extent_z] * has_lower for i in at]
        else:
            rest = [jnp.zeros((2, extent_z), F32)]
        edges.append(jnp.concatenate(above + below + rest, axis=0))
    even_ref[main : main + 8, :] = jnp.where(is_odd, edges[0], edges[1])
    odd_ref[main : main + 8, :] = jnp.where(is_odd, edges[1], edges[0])
    if with_moduli:
        for m in range(2):
            for target_ref in (even_ref, odd_ref):
                target_ref[main + 8 + m * extent_y : main + 8 + (m + 1) * extent_y, :] = moduli_ref[m, 0]
    points_ref[0] = own_ref[0:rows, :]
    points_ref[1] = lower_ref[0:rows, extent_z:]
    points_ref[2] = upper_ref[0:rows, extent_z:]
    for i in range(far_ref.shape[0]):
        points_ref[3 + i] = far_ref[i, 0:rows, :]


def pair_body(blocks, bin_count, last, *refs):
    if last:
        (bins_ref, points_ref, node_ref, hot_ref, heat_ref, tile_ref,
         contact_ref, partial_ref, spread, listed, push) = refs
    else:
        (bins_ref, points_ref, node_ref, hot_ref, heat_ref,
         contact_ref, total_ref, spread, listed, push) = refs
    total_blocks = blocks * bin_count
    stride = total_blocks + 2
    extent_z = contact_ref.shape[1]
    rows = contact_ref.shape[0] // 3
    counts = [jnp.int32(0)] * bin_count
    for i in range(total_blocks):
        named = bins_ref[i]
        taken = counts[0]
        for b in range(1, bin_count):
            taken = jnp.where(named == b, counts[b], taken)
        listed[named * stride + taken] = i
        counts = [count + (named == b).astype(jnp.int32) for b, count in enumerate(counts)]
    for b in range(bin_count):
        listed[b * stride + counts[b]] = total_blocks
    spread[total_blocks] = jnp.full((3, SEG, SEG), 1000.0, F32)
    for d in range(bin_count):
        turned = points_ref[d].T
        for p in range(3):
            for j in range(blocks):
                at = p * blocks + j
                spread[d * blocks + j, p] = jnp.broadcast_to(turned[:, at : at + 1], (SEG, SEG))
    heats = []
    for j in range(blocks):
        named = bins_ref[j]
        count = counts[0]
        for b in range(1, bin_count):
            count = jnp.where(named == b, counts[b], count)
        point = [jnp.broadcast_to(points_ref[0, p * blocks + j : p * blocks + j + 1, :], (8, SEG)) for p in range(3)]

        def against(i, sums):
            sums = list(sums)
            others = [listed[named * stride + 2 * i + half] for half in range(2)]
            for other, g in [(other, g) for other in others for g in range(SEG // 8)]:
                delta = [point[p] - spread[other, p, g * 8 : (g + 1) * 8, :] for p in range(3)]
                square = delta[0] * delta[0] + delta[1] * delta[1] + delta[2] * delta[2]
                inverse = lax.rsqrt(jnp.maximum(square, 1e-30))
                pressure = jnp.maximum(RADIUS - square * inverse, 0.0)
                factor = pressure * jnp.minimum(inverse, 1.0 / (0.25 * RADIUS))
                for p in range(3):
                    sums[p] = sums[p] + factor * delta[p]
                sums[3] = sums[3] + pressure * pressure
            return tuple(sums)

        sums = lax.fori_loop(0, (count + 1) // 2, against, (jnp.zeros((8, SEG), F32),) * 4)
        for p in range(3):
            push[p : p + 1, j * SEG : (j + 1) * SEG] = PENALTY * jnp.sum(sums[p], axis=0, keepdims=True)
        heats.append(SHORT_GAIN * jnp.sum(sums[3], axis=0, keepdims=True))
    row, _ = node_split(node_ref, extent_z)
    at_row = lax.broadcasted_iota(jnp.int32, (rows, row.shape[1]), 0) == row
    for p in range(3):
        placed = jnp.where(at_row, push[p : p + 1, :], 0.0)
        contact_ref[p * rows : (p + 1) * rows, :] = sum(
            jnp.dot(piece, hot_ref[...], preferred_element_type=F32) for piece in split_two(placed)
        )
    total = heat_ref[...] + jnp.concatenate(heats, axis=0)
    if not last:
        total_ref[...] = total
        return
    flat = jnp.concatenate([total[j : j + 1, :] for j in range(blocks)], axis=1)
    side, slot = tile_ref[0:1, :], tile_ref[1:2, :]
    hot_slot = one_hot_z(slot, TILE_DEV)
    at_side = lax.broadcasted_iota(jnp.int32, (8, flat.shape[1]), 0) == side
    placed = jnp.where(at_side, flat, 0.0)
    high, low = split_two(placed)
    lowest = (placed - high.astype(F32) - low.astype(F32)).astype(BF16)
    partial_ref[...] = sum(
        lax.dot_general(piece, hot_slot, NT, preferred_element_type=F32) for piece in (high, low, lowest)
    )


def turn_body(extent_z, node_ref, out_ref):
    node = node_ref[...]
    column = lax.rem(node, jnp.int32(extent_z)).astype(F32).T
    lane = lax.broadcasted_iota(jnp.int32, (SEG, extent_z), 1).astype(F32)
    for j in range(node.shape[0]):
        out_ref[j * SEG : (j + 1) * SEG, :] = jnp.where(lane == column[:, j : j + 1], 1.0, 0.0).astype(BF16)


def tile_body(own_ref, tiles_ref, node_ref, hot_ref, out_ref):
    extent_x, extent_y, extent_z = tiles_ref.shape
    row, _ = node_split(node_ref, extent_z)
    hot = hot_ref[...]
    tiles = tiles_ref[...].reshape(extent_x * extent_y, extent_z)
    device = lax.div(tiles, jnp.int32(TILE_DEV))
    slot = tiles - device * TILE_DEV
    offset = (device - own_ref[0]).astype(F32).astype(BF16)
    found = gather_nodes([offset], row, hot)
    side = jnp.where(found < -0.5, 0, jnp.where(found > 0.5, 2, 1))
    found_slot = gather_nodes([slot.astype(F32).astype(BF16)], row, hot).astype(jnp.int32)
    rest = jnp.zeros((6, row.shape[1]), jnp.int32)
    out_ref[...] = jnp.concatenate([side, found_slot, rest], axis=0)


def update_body(first, last, *refs):
    refs = list(refs)
    take = lambda count: [refs.pop(0) for _ in range(count)]
    flag_ref, disp_ref, vel_ref, mass_ref, moduli_ref, contact_ref, lower_ref, upper_ref, even_ref, odd_ref = take(10)
    if not last:
        base_ref, node_ref, hot_ref = take(3)
    new_disp_ref, new_vel_ref = take(2)
    if not last:
        up_ref, down_ref, far_ref = take(3)
    if first:
        (scaled,) = take(1)
    else:
        scaled = moduli_ref
    field, feature, stress = take(3)
    _, extent_x, extent_y, extent_z = disp_ref.shape
    padded_y = extent_y + 8
    has_lower, has_upper, has_back, has_front = [flag_ref[i] for i in range(4)]
    is_odd = flag_ref[4] > 0.5
    place = lax.broadcasted_iota(jnp.int32, (8, extent_z), 0)

    def back(rows):
        return jnp.where(is_odd, even_ref[0, rows, :], odd_ref[0, rows, :]) * has_back

    def front(rows):
        return jnp.where(is_odd, odd_ref[1, rows, :], even_ref[1, rows, :]) * has_front

    def halo_tile(above, below):
        return jnp.where(place == 0, above, jnp.where(place == 7, below, 0.0))

    for p in range(3):
        for x in range(extent_x):
            at = p * extent_x + x
            field[p, x + 1, 0:extent_y, :] = disp_ref[p, x]
            field[p, x + 1, extent_y:padded_y, :] = halo_tile(
                upper_ref[at : at + 1, 0:extent_z] * has_upper, lower_ref[at : at + 1, 0:extent_z] * has_lower
            )
        for x, layer in ((0, back), (extent_x + 1, front)):
            main = 3 * extent_y
            field[p, x, 0:extent_y, :] = layer(slice(p * extent_y, (p + 1) * extent_y))
            field[p, x, extent_y:padded_y, :] = halo_tile(
                layer(slice(main + p, main + p + 1)), layer(slice(main + 3 + p, main + 4 + p))
            )
    if first:
        scale = -1.0 / 16.0
        main = 3 * extent_y
        for m in range(2):
            for x in range(extent_x):
                at = (3 + m) * extent_x + x
                scaled[m, x + 1, 0:extent_y, :] = moduli_ref[m, x] * scale
                below = lower_ref[at : at + 1, 0:extent_z] * (has_lower * scale)
                scaled[m, x + 1, extent_y:padded_y, :] = jnp.where(place == 7, below, 0.0)
            begin = main + 8 + m * extent_y
            scaled[m, 0, 0:extent_y, :] = back(slice(begin, begin + extent_y)) * scale
            below = back(slice(main + 6 + m, main + 7 + m)) * scale
            scaled[m, 0, extent_y:padded_y, :] = jnp.where(place == 7, below, 0.0)

    def features(x, carry):
        for p in range(3):
            value = field[p, x]
            ahead = pltpu.roll(value, padded_y - 1, 0)
            total, change = value + ahead, ahead - value
            total_z, change_z = pltpu.roll(total, extent_z - 1, 1), pltpu.roll(change, extent_z - 1, 1)
            feature[x, p] = total + total_z
            feature[x, 3 + p] = change + change_z
            feature[x, 6 + p] = total_z - total
        return carry

    lax.fori_loop(0, extent_x + 2, features, 0)

    def stresses(x, carry):
        for t in range(padded_y // 8):
            rows = slice(t * 8, t * 8 + 8)
            along_x = [feature[x + 1, p, rows] - feature[x, p, rows] for p in range(3)]
            along_y = [feature[x + 1, 3 + p, rows] + feature[x, 3 + p, rows] for p in range(3)]
            along_z = [feature[x + 1, 6 + p, rows] + feature[x, 6 + p, rows] for p in range(3)]
            volume = scaled[0, x, rows] * (along_x[0] + along_y[1] + along_z[2])
            shear = scaled[1, x, rows]
            twice = shear + shear
            stress[x, 0, rows] = twice * along_x[0] + volume
            stress[x, 1, rows] = twice * along_y[1] + volume
            stress[x, 2, rows] = twice * along_z[2] + volume
            stress[x, 3, rows] = shear * (along_y[0] + along_x[1])
            stress[x, 4, rows] = shear * (along_z[0] + along_x[2])
            stress[x, 5, rows] = shear * (along_z[1] + along_y[2])
        return carry

    lax.fori_loop(0, extent_x + 1, stresses, 0)
    which = ((0, 3, 4), (3, 1, 5), (4, 5, 2))

    def forces(x, carry):
        step_mass = TIME_STEP / mass_ref[x]
        for p in range(3):
            of_x, of_y, of_z = which[p]
            part_x = stress[x, of_x] - stress[x + 1, of_x]
            part_y = stress[x, of_y] + stress[x + 1, of_y]
            part_z = stress[x, of_z] + stress[x + 1, of_z]
            plain = (part_x - part_y)[:extent_y] + pltpu.roll(part_x + part_y, 1, 0)[:extent_y]
            slope = part_z[:extent_y] + pltpu.roll(part_z, 1, 0)[:extent_y]
            internal = (plain - slope) + pltpu.roll(plain + slope, 1, 1)
            at = pl.ds(pl.multiple_of((p * extent_x + x) * extent_y, 8), extent_y)
            speed = vel_ref[p, x] + step_mass * (internal + contact_ref[at, :])
            new_vel_ref[p, x] = speed
            new_disp_ref[p, x] = disp_ref[p, x] + TIME_STEP * speed
        return carry

    lax.fori_loop(0, extent_x, forces, 0)
    if not last:
        store_messages(new_disp_ref, base_ref, node_ref, hot_ref[...], up_ref, down_ref, far_ref)


def swapped(value, axis):
    count = lax.axis_size(axis)
    even = [[i, i + 1] for i in range(0, count, 2)]
    odd = [[i, i + 1] for i in range(1, count - 1, 2)] + [[0, count - 1]]
    return [lax.all_gather(v, axis, axis_index_groups=groups) for v, groups in zip(value, (even, odd))]


def per_device(displacement, velocity, moduli, nodal_mass, segment_node, segment_base, contact_bin, element_tile):
    shape = displacement.shape
    _, extent_x, extent_y, extent_z = shape
    steps = contact_bin.shape[0]
    segments = segment_node.shape[0]
    blocks = segments // SEG
    bin_count, dom_count = lax.axis_size("bin"), lax.axis_size("dom")
    bin_at, dom_at = lax.axis_index("bin"), lax.axis_index("dom")
    own_device = dom_at * bin_count + bin_at
    is_odd = dom_at % 2 == 1
    flags = jnp.stack([bin_at > 0, bin_at < bin_count - 1, dom_at > 0, dom_at < dom_count - 1, is_odd]).astype(F32)
    node = segment_node.reshape(blocks, SEG)
    bins = contact_bin[:, :, 0].astype(F32)
    bins = jnp.pad(bins, ((0, 8 - steps), (0, SEG - blocks)))
    rows = 3 * extent_x
    wide = extent_z + SEG
    struct = lambda *dims: jax.ShapeDtypeStruct(dims, F32)
    padded_y = extent_y + 8
    layer_rows = 3 * extent_y + 8

    up, down, far, hot = call(
        first_body,
        [
            struct(rows + 16, wide),
            struct(rows + 8, wide),
            struct(rows + 8, SEG),
            jax.ShapeDtypeStruct((extent_z, segments), BF16),
        ],
        specs=[WHOLE] * 5,
    )(displacement, segment_base, node, moduli, bins)
    (turned,) = call(
        functools.partial(turn_body, extent_z),
        [jax.ShapeDtypeStruct((segments, extent_z), BF16)],
        specs=[WHOLE],
    )(node)
    (tile_places,) = call(
        tile_body, [jax.ShapeDtypeStruct((8, segments), jnp.int32)], specs=[SCALARS] + [WHOLE] * 3
    )(own_device[None].astype(jnp.int32), element_tile, node, hot)
    heat = jnp.zeros((blocks, SEG), F32)
    scaled = None
    for step in range(steps):
        lower = cycled(up, "bin", 1)
        upper = cycled(down, "bin", -1)
        others = jnp.stack([cycled(far, "bin", shift) for shift in range(2, bin_count - 1)])
        first, last = step == 0, step == steps - 1
        if first:
            of_bins = [bins[:steps, :blocks]]
            of_bins += [v[rows : rows + steps, extent_z : extent_z + blocks] for v in (lower, upper)]
            of_bins += [v[rows : rows + steps, :blocks] for v in others]
            all_bins = jnp.concatenate(of_bins, axis=1).astype(jnp.int32)
        layer = lambda at, count=3: pl.BlockSpec((count, 1, extent_y, extent_z), lambda i: (0, at, 0, 0))
        full = lambda *dims: pl.BlockSpec(dims, lambda i: (0,) * len(dims))
        send_rows = layer_rows + (2 * extent_y if first else 0)
        layer_args = [flags, displacement, displacement, lower, upper, far, others]
        layer_specs = [SCALARS, layer(0), layer(extent_x - 1)] + [full(*v.shape) for v in layer_args[3:]]
        if first:
            layer_args.append(moduli)
            layer_specs.append(layer(extent_x - 1, 2))
        to_even, to_odd, points = pl.pallas_call(
            functools.partial(layer_body, first),
            grid=(1,),
            out_shape=[struct(send_rows, extent_z)] * 2 + [struct(bin_count, rows, SEG)],
            in_specs=layer_specs,
            out_specs=[full(send_rows, extent_z)] * 2 + [full(bin_count, rows, SEG)],
            compiler_params=pltpu.CompilerParams(vmem_limit_bytes=VMEM_BYTES),
            cost_estimate=pl.CostEstimate(flops=100_000, bytes_accessed=500_000, transcendentals=0),
        )(*layer_args)
        of_even, of_odd = swapped((to_even, to_odd), "dom")
        pair_args = [all_bins[step], points, node, turned, heat]
        pair_specs = [SCALARS] + [WHOLE] * 4
        if last:
            pair_args.append(tile_places)
            pair_specs.append(WHOLE)
        contact, heat = call(
            functools.partial(pair_body, blocks, bin_count, last),
            [struct(3 * extent_x * extent_y, extent_z), struct(8, TILE_DEV) if last else struct(blocks, SEG)],
            [
                pltpu.VMEM((blocks * bin_count + 1, 3, SEG, SEG), F32),
                pltpu.SMEM((bin_count * (blocks * bin_count + 2),), jnp.int32),
                pltpu.VMEM((8, segments), F32),
            ],
            100_000_000,
            pair_specs,
        )(*pair_args)
        if last:
            heat, of_even, of_odd = lax.optimization_barrier((heat, of_even, of_odd))
        update_args = [flags, displacement, velocity, nodal_mass, moduli if first else scaled, contact, lower, upper]
        update_args += [of_even, of_odd]
        update_outs = [struct(*shape), struct(*shape)]
        if not last:
            update_args += [segment_base, node, hot]
            update_outs += [struct(rows, wide), struct(rows, wide), struct(rows, SEG)]
        if first:
            update_outs.append(struct(2, extent_x + 1, padded_y, extent_z))
        made = call(
            functools.partial(update_body, first, last),
            update_outs,
            [
                pltpu.VMEM((3, extent_x + 2, padded_y, extent_z), F32),
                pltpu.VMEM((extent_x + 2, 9, padded_y, extent_z), F32),
                pltpu.VMEM((extent_x + 1, 6, padded_y, extent_z), F32),
            ],
            20_000_000,
            [SCALARS] + [WHOLE] * (len(update_args) - 1),
        )(*update_args)
        displacement, velocity = made[:2]
        if not last:
            up, down, far = made[2:5]
        if first:
            scaled = made[-1]
    even, odd = swapped((heat, heat), "dom")
    from_lower = jnp.where(is_odd, even[0, 2], odd[0, 2]) * flags[2]
    from_upper = jnp.where(is_odd, odd[1, 0], even[1, 0]) * flags[3]
    return displacement, velocity, heat[1] + from_upper + from_lower


def solution(mesh):
    placed = (
        P(None, "dom", "bin", None),
        P(None, "dom", "bin", None),
        P(None, "dom", "bin", None),
        P("dom", "bin", None),
        P(("dom", "bin")),
        P(None, ("dom", "bin")),
        P(None, ("dom", "bin"), None),
        P("dom", "bin", None),
    )
    return jax.shard_map(
        per_device,
        mesh=mesh,
        in_specs=placed,
        out_specs=(P(None, "dom", "bin", None), P(None, "dom", "bin", None), P(("dom", "bin"))),
        check_vma=False,
    )
```

```python
import functools
import jax
import jax.numpy as jnp
from jax import lax
from jax.experimental import pallas as pl
from jax.experimental.pallas import tpu as pltpu
from jax.sharding import PartitionSpec as P

SEG = 128
TILE_DEV = 256
RADIUS = 0.09
PENALTY = 4.0
SHORT_GAIN = 100.0
TIME_STEP = 0.2
VMEM_BYTES = 40 * 1024 * 1024
F32 = jnp.float32
BF16 = jnp.bfloat16
WHOLE = pl.BlockSpec(memory_space=pltpu.VMEM)
SCALARS = pl.BlockSpec(memory_space=pltpu.SMEM)
NT = (((1,), (1,)), ((), ()))


def shifted(value, axis, steps):
    count = lax.axis_size(axis)
    first, last = (max(0, -steps), min(count, count - steps))
    return lax.ppermute(value, axis, [(source, source + steps) for source in range(first, last)])


def cycled(value, axis, steps):
    count = lax.axis_size(axis)
    return lax.ppermute(value, axis, [(source, (source + steps) % count) for source in range(count)])


def call(body, outs, scratch=(), specs=None):
    return functools.partial(
        pl.pallas_call,
        body,
        out_shape=outs,
        out_specs=[WHOLE] * len(outs),
        scratch_shapes=list(scratch),
        compiler_params=pltpu.CompilerParams(vmem_limit_bytes=VMEM_BYTES),
        cost_estimate=pl.CostEstimate(flops=1_000, bytes_accessed=1_000, transcendentals=0),
    )(in_specs=specs)


def split_two(value):
    high = value.astype(BF16)
    return high, (value - high.astype(F32)).astype(BF16)


def node_split(node_ref, extent_z):
    node = jnp.concatenate([node_ref[j : j + 1, :] for j in range(node_ref.shape[0])], axis=1)
    return lax.div(node, jnp.int32(extent_z)), lax.rem(node, jnp.int32(extent_z))


def one_hot_z(column, extent_z):
    depth = lax.broadcasted_iota(jnp.int32, (extent_z, column.shape[1]), 0)
    return jnp.where(depth == column, 1.0, 0.0).astype(BF16)


def gather_nodes(pieces, row, hot):
    rows = pieces[0].shape[0]
    picked = sum(jnp.dot(piece, hot, preferred_element_type=F32) for piece in pieces)
    at_row = lax.broadcasted_iota(jnp.int32, (rows, row.shape[1]), 0) == row
    return jnp.sum(jnp.where(at_row, picked, 0.0), axis=0, keepdims=True)


def store_positions(disp_ref, base_ref, node_ref, hot, targets):
    extent_x, extent_y, extent_z = disp_ref.shape[1:]
    rows = extent_x * extent_y
    blocks = node_ref.shape[0]
    row, _ = node_split(node_ref, extent_z)
    for p in range(3):
        plane = disp_ref[p].reshape(rows, extent_z)
        points = base_ref[p : p + 1, :] + gather_nodes(split_two(plane), row, hot)
        tile = jnp.concatenate([points[:, j * SEG : (j + 1) * SEG] for j in range(blocks)], axis=0)
        for ref, lane in targets:
            ref[p * blocks : (p + 1) * blocks, lane : lane + SEG] = tile


def store_column(source_ref, at, target_ref, first):
    count, extent_x, _, extent_z = source_ref.shape
    for p in range(count):
        tile = jnp.concatenate([source_ref[p, x, at : at + 1, :] for x in range(extent_x)], axis=0)
        target_ref[first + p * extent_x : first + (p + 1) * extent_x, 0:extent_z] = tile


def store_messages(disp_ref, base_ref, node_ref, hot, up_ref, down_ref, far_ref):
    extent_y, extent_z = disp_ref.shape[2:]
    store_column(disp_ref, extent_y - 1, up_ref, 0)
    store_column(disp_ref, 0, down_ref, 0)
    store_positions(disp_ref, base_ref, node_ref, hot, [(up_ref, extent_z), (down_ref, extent_z), (far_ref, 0)])


def first_body(disp_ref, base_ref, node_ref, moduli_ref, bins_ref, up_ref, down_ref, far_ref, hot_ref):
    _, extent_x, extent_y, extent_z = disp_ref.shape
    _, column = node_split(node_ref, extent_z)
    hot_ref[...] = one_hot_z(column, extent_z)
    store_messages(disp_ref, base_ref, node_ref, hot_ref[...], up_ref, down_ref, far_ref)
    rows = 3 * extent_x
    store_column(moduli_ref, moduli_ref.shape[2] - 1, up_ref, rows)
    bins = bins_ref[...]
    zeros = jnp.zeros((8, SEG), F32)
    up_ref[rows : rows + 8, extent_z:] = bins
    up_ref[rows + 8 : rows + 16, extent_z:] = zeros
    down_ref[rows : rows + 8, 0:extent_z] = jnp.zeros((8, extent_z), F32)
    down_ref[rows : rows + 8, extent_z:] = bins
    far_ref[rows : rows + 8, :] = bins


def layer_body(with_moduli, *refs):
    flag_ref, first_ref, last_ref, lower_ref, upper_ref = refs[:5]
    if with_moduli:
        moduli_ref, up_ref, down_ref = refs[7:]
    else:
        up_ref, down_ref = refs[7:]
    extent_y, extent_z = first_ref.shape[2:]
    main = 3 * extent_y
    extent_x = lower_ref.shape[0] // (5 if with_moduli else 3)
    has_lower, has_upper = flag_ref[0], flag_ref[1]
    for x, source_ref, target_ref in ((0, first_ref, down_ref), (extent_x - 1, last_ref, up_ref)):
        for p in range(3):
            target_ref[p * extent_y : (p + 1) * extent_y, :] = source_ref[p, 0]
        at = [p * extent_x + x for p in range(3)]
        above = [upper_ref[i : i + 1, 0:extent_z] * has_upper for i in at]
        below = [lower_ref[i : i + 1, 0:extent_z] * has_lower for i in at]
        if with_moduli and x > 0:
            at = [(3 + m) * extent_x + x for m in range(2)]
            rest = [lower_ref[i : i + 1, 0:extent_z] * has_lower for i in at]
        else:
            rest = [jnp.zeros((2, extent_z), F32)]
        target_ref[main : main + 8, :] = jnp.concatenate(above + below + rest, axis=0)
    if with_moduli:
        for m in range(2):
            up_ref[main + 8 + m * extent_y : main + 8 + (m + 1) * extent_y, :] = moduli_ref[m, 0]


def pair_sums(bins_ref, own_ref, sources, begin, bin_count, sums_of, store, spread, listed):
    rows = own_ref.shape[0] // 24 * 24
    blocks = rows // 3
    total_blocks = blocks * len(sources)
    stride = total_blocks + 2
    counts = [jnp.int32(0)] * bin_count
    for i in range(total_blocks):
        named = bins_ref[begin + i]
        taken = counts[0]
        for b in range(1, bin_count):
            taken = jnp.where(named == b, counts[b], taken)
        listed[named * stride + taken] = i
        counts = [count + (named == b).astype(jnp.int32) for b, count in enumerate(counts)]
    for b in range(bin_count):
        listed[b * stride + counts[b]] = total_blocks
    spread[total_blocks] = jnp.full((3, SEG, SEG), 1000.0, F32)
    for d, source in enumerate(sources):
        turned = source.T
        for p in range(3):
            for j in range(blocks):
                at = p * blocks + j
                spread[d * blocks + j, p] = jnp.broadcast_to(turned[:, at : at + 1], (SEG, SEG))
    for j in range(blocks):
        named = bins_ref[j]
        count = counts[0]
        for b in range(1, bin_count):
            count = jnp.where(named == b, counts[b], count)
        point = [jnp.broadcast_to(own_ref[p * blocks + j : p * blocks + j + 1, :], (8, SEG)) for p in range(3)]

        def against(i, sums):
            sums = list(sums)
            others = [listed[named * stride + 2 * i + half] for half in range(2)]
            for other, g in [(other, g) for other in others for g in range(SEG // 8)]:
                delta = [point[p] - spread[other, p, g * 8 : (g + 1) * 8, :] for p in range(3)]
                square = delta[0] * delta[0] + delta[1] * delta[1] + delta[2] * delta[2]
                inverse = lax.rsqrt(jnp.maximum(square, 1e-30))
                pressure = jnp.maximum(RADIUS - square * inverse, 0.0)
                factor = pressure * jnp.minimum(inverse, 1.0 / (0.25 * RADIUS))
                for p in range(3):
                    sums[p] = sums[p] + factor * delta[p]
                sums[3] = sums[3] + pressure * pressure
            return tuple(sums)

        store(j, lax.fori_loop(0, (count + 1) // 2, against, sums_of(j)))


def near_body(bin_count, bins_ref, own_ref, lower_ref, _, sums_ref, spread, listed):
    rows = own_ref.shape[0] // 24 * 24
    extent_z = lower_ref.shape[1] - SEG

    def store(j, sums):
        for q in range(4):
            sums_ref[j, q] = sums[q]

    sources = [own_ref[0:rows, :], lower_ref[0:rows, extent_z:]]
    zero = (jnp.zeros((8, SEG), F32),) * 4
    pair_sums(bins_ref, own_ref, sources, 0, bin_count, lambda j: zero, store, spread, listed)


def rest_body(bin_count, last, *refs):
    bins_ref, own_ref, upper_ref, far_ref, sums_ref, node_ref, hot_ref, heat_ref = refs[:8]
    if last:
        tile_ref, contact_ref, partial_ref, spread, listed, push = refs[8:]
    else:
        contact_ref, total_ref, spread, listed, push = refs[8:]
    extent_z = contact_ref.shape[1]
    rows = contact_ref.shape[0] // 3
    point_rows = own_ref.shape[0] // 24 * 24
    blocks = node_ref.shape[0]
    heats = []

    def store(j, sums):
        for p in range(3):
            push[p : p + 1, j * SEG : (j + 1) * SEG] = PENALTY * jnp.sum(sums[p], axis=0, keepdims=True)
        heats.append(SHORT_GAIN * jnp.sum(sums[3], axis=0, keepdims=True))

    sources = [upper_ref[0:point_rows, extent_z:]] + [far_ref[i, 0:point_rows, :] for i in range(far_ref.shape[0])]
    sums_of = lambda j: tuple(sums_ref[j, q] for q in range(4))
    pair_sums(bins_ref, own_ref, sources, 2 * blocks, bin_count, sums_of, store, spread, listed)
    row, _ = node_split(node_ref, extent_z)
    at_row = lax.broadcasted_iota(jnp.int32, (rows, row.shape[1]), 0) == row
    for p in range(3):
        placed = jnp.where(at_row, push[p : p + 1, :], 0.0)
        contact_ref[p * rows : (p + 1) * rows, :] = sum(
            jnp.dot(piece, hot_ref[...], preferred_element_type=F32) for piece in split_two(placed)
        )
    total = heat_ref[...] + jnp.concatenate(heats, axis=0)
    if not last:
        total_ref[...] = total
        return
    flat = jnp.concatenate([total[j : j + 1, :] for j in range(blocks)], axis=1)
    side, slot = tile_ref[0:1, :], tile_ref[1:2, :]
    hot_slot = one_hot_z(slot, TILE_DEV)
    at_side = lax.broadcasted_iota(jnp.int32, (8, flat.shape[1]), 0) == side
    placed = jnp.where(at_side, flat, 0.0)
    high, low = split_two(placed)
    lowest = (placed - high.astype(F32) - low.astype(F32)).astype(BF16)
    partial_ref[...] = sum(
        lax.dot_general(piece, hot_slot, NT, preferred_element_type=F32) for piece in (high, low, lowest)
    )


def turn_body(extent_z, node_ref, out_ref):
    node = node_ref[...]
    column = lax.rem(node, jnp.int32(extent_z)).astype(F32).T
    lane = lax.broadcasted_iota(jnp.int32, (SEG, extent_z), 1).astype(F32)
    for j in range(node.shape[0]):
        out_ref[j * SEG : (j + 1) * SEG, :] = jnp.where(lane == column[:, j : j + 1], 1.0, 0.0).astype(BF16)


def tile_body(own_ref, tiles_ref, node_ref, hot_ref, out_ref):
    extent_x, extent_y, extent_z = tiles_ref.shape
    row, _ = node_split(node_ref, extent_z)
    hot = hot_ref[...]
    tiles = tiles_ref[...].reshape(extent_x * extent_y, extent_z)
    device = lax.div(tiles, jnp.int32(TILE_DEV))
    slot = tiles - device * TILE_DEV
    offset = (device - own_ref[0]).astype(F32).astype(BF16)
    found = gather_nodes([offset], row, hot)
    side = jnp.where(found < -0.5, 0, jnp.where(found > 0.5, 2, 1))
    found_slot = gather_nodes([slot.astype(F32).astype(BF16)], row, hot).astype(jnp.int32)
    rest = jnp.zeros((6, row.shape[1]), jnp.int32)
    out_ref[...] = jnp.concatenate([side, found_slot, rest], axis=0)


WHICH = ((0, 3, 4), (3, 1, 5), (4, 5, 2))
SCALE = -1.0 / 16.0


def ahead_z(value):
    return pltpu.roll(value, value.shape[1] - 1, 1)


def behind_z(value):
    return pltpu.roll(value, 1, 1)


def ahead_row(value):
    return pltpu.roll(value, value.shape[0] - 1, 0)


def behind_row(value):
    return pltpu.roll(value, 1, 0)


def features(near, far):
    total, change = near + far, far - near
    total_z = ahead_z(total)
    return total + total_z, change + ahead_z(change), total_z - total


def stress_of(along_x, along_y, along_z, volume_modulus, shear):
    volume = volume_modulus * (along_x[0] + along_y[1] + along_z[2])
    twice = shear + shear
    return (
        twice * along_x[0] + volume,
        twice * along_y[1] + volume,
        twice * along_z[2] + volume,
        shear * (along_y[0] + along_x[1]),
        shear * (along_z[0] + along_x[2]),
        shear * (along_z[1] + along_y[2]),
    )


def spread_z(plain, slope):
    return (plain - slope) + behind_z(plain + slope)


def inner_body(disp_ref, moduli_ref, out_ref, feature, stress):
    _, extent_x, extent_y, extent_z = disp_ref.shape

    def fill(x, carry):
        for p in range(3):
            value = disp_ref[p, x]
            for q, part in enumerate(features(value, ahead_row(value))):
                feature[x, 3 * q + p] = part
        return carry

    lax.fori_loop(0, extent_x, fill, 0)
    for c in range(6):
        stress[0, c] = jnp.zeros((extent_y, extent_z), F32)
        stress[extent_x, c] = jnp.zeros((extent_y, extent_z), F32)
    place = lax.broadcasted_iota(jnp.int32, (8, extent_z), 0)

    def load(x, carry):
        for t in range(extent_y // 8):
            rows = slice(t * 8, t * 8 + 8)
            scale = jnp.where(place == 7, 0.0, SCALE) if t == extent_y // 8 - 1 else SCALE
            along_x = [feature[x + 1, p, rows] - feature[x, p, rows] for p in range(3)]
            along_y = [feature[x + 1, 3 + p, rows] + feature[x, 3 + p, rows] for p in range(3)]
            along_z = [feature[x + 1, 6 + p, rows] + feature[x, 6 + p, rows] for p in range(3)]
            found = stress_of(along_x, along_y, along_z, moduli_ref[0, x, rows] * scale, moduli_ref[1, x, rows] * scale)
            for c in range(6):
                stress[x + 1, c, rows] = found[c]
        return carry

    lax.fori_loop(0, extent_x - 1, load, 0)

    def force(x, carry):
        for p in range(3):
            of_x, of_y, of_z = WHICH[p]
            part_x = stress[x, of_x] - stress[x + 1, of_x]
            part_y = stress[x, of_y] + stress[x + 1, of_y]
            part_z = stress[x, of_z] + stress[x + 1, of_z]
            plain = (part_x - part_y) + behind_row(part_x + part_y)
            out_ref[p, x] = spread_z(plain, part_z + behind_row(part_z))
        return carry

    lax.fori_loop(0, extent_x, force, 0)


def update_body(first, last, *refs):
    refs = list(refs)
    take = lambda count: [refs.pop(0) for _ in range(count)]
    flag_ref, disp_ref, vel_ref, mass_ref, inner_ref, contact_ref = take(6)
    own_up_ref, own_down_ref, lower_ref, upper_ref, back_ref, front_ref, rim_ref = take(7)
    if not last:
        base_ref, node_ref, hot_ref = take(3)
    new_disp_ref, new_vel_ref = take(2)
    if not last:
        up_ref, down_ref, far_ref = take(3)
    if first:
        moduli_ref, rim_ref = rim_ref, take(1)[0]
    (side_low, side_high, face_low, face_high) = take(4)
    _, extent_x, extent_y, extent_z = disp_ref.shape
    has_lower, has_upper = flag_ref[0], flag_ref[1]
    place = lax.broadcasted_iota(jnp.int32, (8, extent_z), 0)
    all_but_last = lax.broadcasted_iota(jnp.int32, (extent_y, extent_z), 0) < extent_y - 1
    main = 3 * extent_y

    def ring(tile, above, below):
        return jnp.concatenate([tile, jnp.where(place == 0, above, jnp.where(place == 7, below, 0.0))], axis=0)

    if first:
        for m in range(2):
            at = slice((3 + m) * extent_x, (4 + m) * extent_x)
            begin = main + 8 + m * extent_y
            of_back = back_ref[begin : begin + extent_y, :]
            high = ring(own_up_ref[at, 0:extent_z], 0.0, of_back[extent_y - 1 :])
            low = ring(lower_ref[at, 0:extent_z] * has_lower, 0.0, back_ref[main + 6 + m : main + 7 + m, :])
            rim_ref[m] = high * SCALE
            rim_ref[2 + m] = low * SCALE
            rim_ref[4 + m] = jnp.where(all_but_last, of_back * SCALE, 0.0)
            rim_ref[6 + m] = jnp.where(all_but_last, moduli_ref[m, extent_x - 1] * SCALE, 0.0)

    def rows_of(tile_ref, weight, row, extra):
        made = []
        for p in range(3):
            at = main + extra + p if row is None else p * extent_y + row
            tile = tile_ref[p * extent_x : (p + 1) * extent_x, 0:extent_z]
            tile = tile if weight is None else tile * weight
            made.append(ring(tile, front_ref[at : at + 1, :], back_ref[at : at + 1, :]))
        return made

    def side(near, far, at, sign, target):
        parts = [features(near[p], far[p]) for p in range(3)]
        along_x = [ahead_row(parts[p][0]) - parts[p][0] for p in range(3)]
        along_y = [ahead_row(parts[p][1]) + parts[p][1] for p in range(3)]
        along_z = [ahead_row(parts[p][2]) + parts[p][2] for p in range(3)]
        found = stress_of(along_x, along_y, along_z, rim_ref[at], rim_ref[at + 1])
        for p in range(3):
            of_x, of_y, of_z = [found[c] for c in WHICH[p]]
            part_x = (behind_row(of_x) - of_x)[:extent_x]
            part_y = (behind_row(of_y) + of_y)[:extent_x]
            part_z = (behind_row(of_z) + of_z)[:extent_x]
            target[p] = spread_z(part_x + sign * part_y, part_z)

    side(rows_of(own_up_ref, None, extent_y - 1, 0), rows_of(upper_ref, has_upper, None, 0), 0, -1.0, side_high)
    side(rows_of(lower_ref, has_lower, None, 3), rows_of(own_down_ref, None, 0, 0), 2, 1.0, side_low)

    def face(near, far, at, sign, target):
        parts_near = [features(value, ahead_row(value)) for value in near]
        parts_far = [features(value, ahead_row(value)) for value in far]
        along_x = [parts_far[p][0] - parts_near[p][0] for p in range(3)]
        along_y = [parts_far[p][1] + parts_near[p][1] for p in range(3)]
        along_z = [parts_far[p][2] + parts_near[p][2] for p in range(3)]
        found = stress_of(along_x, along_y, along_z, rim_ref[at], rim_ref[at + 1])
        for p in range(3):
            of_x, of_y, of_z = [found[c] for c in WHICH[p]]
            of_x = of_x * sign
            plain = (of_x - of_y) + behind_row(of_x + of_y)
            target[p] = spread_z(plain, of_z + behind_row(of_z))

    layer_of = lambda ref: [ref[p * extent_y : (p + 1) * extent_y, :] for p in range(3)]
    own_layer = lambda x: [disp_ref[p, x] for p in range(3)]
    face(layer_of(back_ref), own_layer(0), 4, 1.0, face_low)
    face(own_layer(extent_x - 1), layer_of(front_ref), 6, -1.0, face_high)

    for x in range(extent_x):
        step_mass = TIME_STEP / mass_ref[x]
        for p in range(3):
            at = (p * extent_x + x) * extent_y
            load = inner_ref[p, x] + contact_ref[at : at + extent_y, :]
            if x == 0:
                load = load + face_low[p]
            if x == extent_x - 1:
                load = load + face_high[p]
            begin = load[:8] + jnp.where(place == 0, side_low[p, x : x + 1, :], 0.0)
            end = load[extent_y - 8 :] + jnp.where(place == 7, side_high[p, x : x + 1, :], 0.0)
            load = jnp.concatenate([begin, load[8 : extent_y - 8], end] if extent_y > 16 else [begin, end], axis=0)
            speed = vel_ref[p, x] + step_mass * load
            new_vel_ref[p, x] = speed
            new_disp_ref[p, x] = disp_ref[p, x] + TIME_STEP * speed
    if not last:
        store_messages(new_disp_ref, base_ref, node_ref, hot_ref[...], up_ref, down_ref, far_ref)


def per_device(displacement, velocity, moduli, nodal_mass, segment_node, segment_base, contact_bin, element_tile):
    shape = displacement.shape
    _, extent_x, extent_y, extent_z = shape
    steps = contact_bin.shape[0]
    segments = segment_node.shape[0]
    blocks = segments // SEG
    bin_count = lax.axis_size("bin")
    bin_at = lax.axis_index("bin")
    own_device = lax.axis_index("dom") * bin_count + bin_at
    flags = jnp.stack([bin_at > 0, bin_at < bin_count - 1]).astype(F32)
    node = segment_node.reshape(blocks, SEG)
    bins = contact_bin[:, :, 0].astype(F32)
    bins = jnp.pad(bins, ((0, 8 - steps), (0, SEG - blocks)))
    rows = 3 * extent_x
    wide = extent_z + SEG
    struct = lambda *dims: jax.ShapeDtypeStruct(dims, F32)
    layer_rows = 3 * extent_y + 8
    full = lambda *dims: pl.BlockSpec(dims, lambda i: (0,) * len(dims))

    first_outs = [
        struct(rows + 16, wide),
        struct(rows + 8, wide),
        struct(rows + 8, SEG),
        jax.ShapeDtypeStruct((extent_z, segments), BF16),
    ]
    first_args = (displacement, segment_base, node, moduli, bins)
    first_specs = [full(*v.shape) for v in first_args]
    first_specs[3] = pl.BlockSpec((2, extent_x, 8, extent_z), lambda i: (0, 0, extent_y // 8 - 1, 0))
    up, down, far, hot = pl.pallas_call(
        first_body,
        grid=(1,),
        out_shape=first_outs,
        in_specs=first_specs,
        out_specs=[full(*v.shape) for v in first_outs],
        compiler_params=pltpu.CompilerParams(vmem_limit_bytes=60 * 1024 * 1024),
        cost_estimate=pl.CostEstimate(flops=1_000, bytes_accessed=1_000, transcendentals=0),
    )(*first_args)
    (turned,) = call(
        functools.partial(turn_body, extent_z),
        [jax.ShapeDtypeStruct((segments, extent_z), BF16)],
        specs=[WHOLE],
    )(node)
    (tile_places,) = call(
        tile_body, [jax.ShapeDtypeStruct((8, segments), jnp.int32)], specs=[SCALARS] + [WHOLE] * 3
    )(own_device[None].astype(jnp.int32), element_tile, node, hot)
    heat = jnp.zeros((blocks, SEG), F32)
    rim = moduli
    for step in range(steps):
        lower = cycled(up, "bin", 1)
        upper = cycled(down, "bin", -1)
        others = jnp.stack([cycled(far, "bin", shift) for shift in range(2, bin_count - 1)])
        first, last = step == 0, step == steps - 1
        (inner,) = call(
            inner_body,
            [struct(*shape)],
            [pltpu.VMEM((extent_x, 9, extent_y, extent_z), F32), pltpu.VMEM((extent_x + 1, 6, extent_y, extent_z), F32)],
            [WHOLE] * 2,
        )(displacement, moduli)
        if first:
            of_bins = [bins[:steps, :blocks]]
            of_bins += [v[rows : rows + steps, extent_z : extent_z + blocks] for v in (lower, upper)]
            of_bins += [v[rows : rows + steps, :blocks] for v in others]
            all_bins = jnp.concatenate(of_bins, axis=1).astype(jnp.int32)
        layer = lambda at, count=3: pl.BlockSpec((count, 1, extent_y, extent_z), lambda i: (0, at, 0, 0))
        up_rows = layer_rows + (2 * extent_y if first else 0)
        layer_args = [flags, displacement, displacement, lower, upper, inner, others]
        layer_specs = [SCALARS, layer(0), layer(extent_x - 1), full(*lower.shape), full(*upper.shape)]
        layer_specs += [pl.BlockSpec(memory_space=pl.ANY)] * 2
        if first:
            layer_args.append(moduli)
            layer_specs.append(layer(extent_x - 1, 2))
        to_front, to_back = pl.pallas_call(
            functools.partial(layer_body, first),
            grid=(1,),
            out_shape=[struct(up_rows, extent_z), struct(layer_rows, extent_z)],
            in_specs=layer_specs,
            out_specs=[full(up_rows, extent_z), full(layer_rows, extent_z)],
            compiler_params=pltpu.CompilerParams(vmem_limit_bytes=VMEM_BYTES),
            cost_estimate=pl.CostEstimate(flops=1_000, bytes_accessed=1_000, transcendentals=0),
        )(*layer_args)
        back = shifted(to_front, "dom", 1)
        near_blocks = 2 * blocks
        far_blocks = blocks * (bin_count - 2)
        pair_scratch = lambda count: [
            pltpu.VMEM((count + 1, 3, SEG, SEG), F32),
            pltpu.SMEM((bin_count * (count + 2),), jnp.int32),
        ]
        (sums,) = call(
            functools.partial(near_body, bin_count),
            [struct(blocks, 4, 8, SEG)],
            pair_scratch(near_blocks),
            [SCALARS, WHOLE, WHOLE, pl.BlockSpec(memory_space=pl.ANY)],
        )(all_bins[step], far, lower, to_front)
        to_back, sums, back = lax.optimization_barrier((to_back, sums, back))
        front = shifted(to_back, "dom", -1)
        pair_args = [all_bins[step], far, upper, others, sums, node, turned, heat]
        if last:
            pair_args.append(tile_places)
        contact, heat = call(
            functools.partial(rest_body, bin_count, last),
            [struct(3 * extent_x * extent_y, extent_z), struct(8, TILE_DEV) if last else struct(blocks, SEG)],
            pair_scratch(far_blocks) + [pltpu.VMEM((8, segments), F32)],
            [SCALARS] + [WHOLE] * (len(pair_args) - 1),
        )(*pair_args)
        if last:
            heat, back, front = lax.optimization_barrier((heat, back, front))
        update_args = [flags, displacement, velocity, nodal_mass, inner, contact, up, down, lower, upper, back, front, rim]
        update_outs = [struct(*shape), struct(*shape)]
        if not last:
            update_args += [segment_base, node, hot]
            update_outs += [struct(rows, wide), struct(rows, wide), struct(rows, SEG)]
        if first:
            update_outs.append(struct(8, extent_y, extent_z))
        made = call(
            functools.partial(update_body, first, last),
            update_outs,
            [pltpu.VMEM((3, extent_x, extent_z), F32)] * 2 + [pltpu.VMEM((3, extent_y, extent_z), F32)] * 2,
            [SCALARS] + [WHOLE] * (len(update_args) - 1),
        )(*update_args)
        displacement, velocity = made[:2]
        if not last:
            up, down, far = made[2:5]
        if first:
            rim = made[-1]
    tile_heat = heat[1] + shifted(heat[0], "dom", -1) + shifted(heat[2], "dom", 1)
    return displacement, velocity, tile_heat


def solution(mesh):
    placed = (
        P(None, "dom", "bin", None),
        P(None, "dom", "bin", None),
        P(None, "dom", "bin", None),
        P("dom", "bin", None),
        P(("dom", "bin")),
        P(None, ("dom", "bin")),
        P(None, ("dom", "bin"), None),
        P("dom", "bin", None),
    )
    return jax.shard_map(
        per_device,
        mesh=mesh,
        in_specs=placed,
        out_specs=(P(None, "dom", "bin", None), P(None, "dom", "bin", None), P(("dom", "bin"))),
        check_vma=False,
    )
```

```python
import functools
import jax
import jax.numpy as jnp
from jax import lax
from jax.experimental import pallas as pl
from jax.experimental.pallas import tpu as pltpu
from jax.sharding import PartitionSpec as P

SEG = 128
TILE_DEV = 256
RADIUS = 0.09
PENALTY = 4.0
SHORT_GAIN = 100.0
TIME_STEP = 0.2
VMEM_BYTES = 40 * 1024 * 1024
F32 = jnp.float32
BF16 = jnp.bfloat16
WHOLE = pl.BlockSpec(memory_space=pltpu.VMEM)
SCALARS = pl.BlockSpec(memory_space=pltpu.SMEM)
NT = (((1,), (1,)), ((), ()))


def swapped(value, axis, odd):
    count = lax.axis_size(axis)
    first = 1 if odd else 0
    partner = list(range(count))
    for i in range(first, count - 1, 2):
        partner[i], partner[i + 1] = i + 1, i
    return lax.ppermute(value, axis, list(enumerate(partner)))


def cycled(value, axis, steps):
    count = lax.axis_size(axis)
    return lax.ppermute(value, axis, [(source, (source + steps) % count) for source in range(count)])


def call(body, outs, scratch=(), specs=None):
    return functools.partial(
        pl.pallas_call,
        body,
        out_shape=outs,
        out_specs=[WHOLE] * len(outs),
        scratch_shapes=list(scratch),
        compiler_params=pltpu.CompilerParams(vmem_limit_bytes=VMEM_BYTES),
        cost_estimate=pl.CostEstimate(flops=1_000, bytes_accessed=1_000, transcendentals=0),
    )(in_specs=specs)


def split_two(value):
    high = value.astype(BF16)
    return high, (value - high.astype(F32)).astype(BF16)


def node_split(node_ref, extent_z):
    node = jnp.concatenate([node_ref[j : j + 1, :] for j in range(node_ref.shape[0])], axis=1)
    return lax.div(node, jnp.int32(extent_z)), lax.rem(node, jnp.int32(extent_z))


def one_hot_z(column, extent_z):
    depth = lax.broadcasted_iota(jnp.int32, (extent_z, column.shape[1]), 0)
    return jnp.where(depth == column, 1.0, 0.0).astype(BF16)


def gather_nodes(pieces, row, hot):
    rows = pieces[0].shape[0]
    picked = sum(jnp.dot(piece, hot, preferred_element_type=F32) for piece in pieces)
    at_row = lax.broadcasted_iota(jnp.int32, (rows, row.shape[1]), 0) == row
    return jnp.sum(jnp.where(at_row, picked, 0.0), axis=0, keepdims=True)


def store_positions(disp_ref, base_ref, node_ref, hot, targets):
    extent_x, extent_y, extent_z = disp_ref.shape[1:]
    rows = extent_x * extent_y
    blocks = node_ref.shape[0]
    row, _ = node_split(node_ref, extent_z)
    for p in range(3):
        plane = disp_ref[p].reshape(rows, extent_z)
        points = base_ref[p : p + 1, :] + gather_nodes(split_two(plane), row, hot)
        tile = jnp.concatenate([points[:, j * SEG : (j + 1) * SEG] for j in range(blocks)], axis=0)
        for ref, lane in targets:
            ref[p * blocks : (p + 1) * blocks, lane : lane + SEG] = tile


def store_column(source_ref, at, target_ref, first):
    count, extent_x, _, extent_z = source_ref.shape
    for p in range(count):
        tile = jnp.concatenate([source_ref[p, x, at : at + 1, :] for x in range(extent_x)], axis=0)
        target_ref[first + p * extent_x : first + (p + 1) * extent_x, 0:extent_z] = tile


def store_messages(disp_ref, base_ref, node_ref, hot, up_ref, down_ref, far_ref):
    extent_y, extent_z = disp_ref.shape[2:]
    store_column(disp_ref, extent_y - 1, up_ref, 0)
    store_column(disp_ref, 0, down_ref, 0)
    store_positions(disp_ref, base_ref, node_ref, hot, [(up_ref, extent_z), (down_ref, extent_z), (far_ref, 0)])


def first_body(disp_ref, base_ref, node_ref, moduli_ref, bins_ref, up_ref, down_ref, far_ref, hot_ref):
    _, extent_x, extent_y, extent_z = disp_ref.shape
    _, column = node_split(node_ref, extent_z)
    hot_ref[...] = one_hot_z(column, extent_z)
    store_messages(disp_ref, base_ref, node_ref, hot_ref[...], up_ref, down_ref, far_ref)
    rows = 3 * extent_x
    store_column(moduli_ref, moduli_ref.shape[2] - 1, up_ref, rows)
    steps, blocks = bins_ref.shape
    bins = bins_ref[...].astype(F32)
    zeros = jnp.zeros((8, SEG), F32)
    up_ref[rows + 8 : rows + 16, extent_z:] = zeros
    down_ref[rows : rows + 8, 0:extent_z] = jnp.zeros((8, extent_z), F32)
    for ref, lane in ((up_ref, extent_z), (down_ref, extent_z), (far_ref, 0)):
        ref[rows : rows + 8, lane : lane + SEG] = zeros
        ref[rows : rows + steps, lane : lane + blocks] = bins


def layer_body(with_moduli, *refs):
    flag_ref, first_ref, last_ref, lower_ref, upper_ref = refs[:5]
    if with_moduli:
        moduli_ref, even_ref, odd_ref = refs[7:]
    else:
        even_ref, odd_ref = refs[7:]
    extent_y, extent_z = first_ref.shape[2:]
    main = 3 * extent_y
    extent_x = lower_ref.shape[0] // (5 if with_moduli else 3)
    has_lower, has_upper, is_odd = flag_ref[0], flag_ref[1], flag_ref[4] > 0.5
    for p in range(3):
        low, high = first_ref[p, 0], last_ref[p, 0]
        even_ref[p * extent_y : (p + 1) * extent_y, :] = jnp.where(is_odd, low, high)
        odd_ref[p * extent_y : (p + 1) * extent_y, :] = jnp.where(is_odd, high, low)
    edges = []
    for x in (0, extent_x - 1):
        at = [p * extent_x + x for p in range(3)]
        above = [upper_ref[i : i + 1, 0:extent_z] * has_upper for i in at]
        below = [lower_ref[i : i + 1, 0:extent_z] * has_lower for i in at]
        if with_moduli:
            at = [(3 + m) * extent_x + x for m in range(2)]
            rest = [lower_ref[i : i + 1, 0:extent_z] * has_lower for i in at]
        else:
            rest = [jnp.zeros((2, extent_z), F32)]
        edges.append(jnp.concatenate(above + below + rest, axis=0))
    even_ref[main : main + 8, :] = jnp.where(is_odd, edges[0], edges[1])
    odd_ref[main : main + 8, :] = jnp.where(is_odd, edges[1], edges[0])
    if with_moduli:
        for m in range(2):
            for target_ref in (even_ref, odd_ref):
                target_ref[main + 8 + m * extent_y : main + 8 + (m + 1) * extent_y, :] = moduli_ref[m, 0]


def pair_sums(bins_ref, own_ref, sources, begin, bin_count, sums_of, store, spread, listed):
    rows = own_ref.shape[0] // 24 * 24
    blocks = rows // 3
    total_blocks = blocks * len(sources)
    stride = total_blocks + 2
    counts = [jnp.int32(0)] * bin_count
    for i in range(total_blocks):
        named = bins_ref[begin + i]
        taken = counts[0]
        for b in range(1, bin_count):
            taken = jnp.where(named == b, counts[b], taken)
        listed[named * stride + taken] = i
        counts = [count + (named == b).astype(jnp.int32) for b, count in enumerate(counts)]
    for b in range(bin_count):
        listed[b * stride + counts[b]] = total_blocks
    spread[total_blocks] = jnp.full((3, SEG, SEG), 1000.0, F32)
    for d, source in enumerate(sources):
        turned = source.T
        for p in range(3):
            for j in range(blocks):
                at = p * blocks + j
                spread[d * blocks + j, p] = jnp.broadcast_to(turned[:, at : at + 1], (SEG, SEG))
    for j in range(blocks):
        named = bins_ref[j]
        count = counts[0]
        for b in range(1, bin_count):
            count = jnp.where(named == b, counts[b], count)
        point = [jnp.broadcast_to(own_ref[p * blocks + j : p * blocks + j + 1, :], (8, SEG)) for p in range(3)]

        def against(i, sums):
            sums = list(sums)
            others = [listed[named * stride + 2 * i + half] for half in range(2)]
            for other, g in [(other, g) for other in others for g in range(SEG // 8)]:
                delta = [point[p] - spread[other, p, g * 8 : (g + 1) * 8, :] for p in range(3)]
                square = delta[0] * delta[0] + delta[1] * delta[1] + delta[2] * delta[2]
                inverse = lax.rsqrt(jnp.maximum(square, 1e-30))
                pressure = jnp.maximum(RADIUS - square * inverse, 0.0)
                factor = pressure * jnp.minimum(inverse, 1.0 / (0.25 * RADIUS))
                for p in range(3):
                    sums[p] = sums[p] + factor * delta[p]
                sums[3] = sums[3] + pressure * pressure
            return tuple(sums)

        store(j, lax.fori_loop(0, (count + 1) // 2, against, sums_of(j)))


def near_body(bin_count, bins_ref, own_ref, lower_ref, _, sums_ref, spread, listed):
    rows = own_ref.shape[0] // 24 * 24
    extent_z = lower_ref.shape[1] - SEG

    def store(j, sums):
        for q in range(4):
            sums_ref[j, q] = sums[q]

    sources = [own_ref[0:rows, :], lower_ref[0:rows, extent_z:]]
    zero = (jnp.zeros((8, SEG), F32),) * 4
    pair_sums(bins_ref, own_ref, sources, 0, bin_count, lambda j: zero, store, spread, listed)


def rest_body(bin_count, last, *refs):
    bins_ref, own_ref, upper_ref, far_ref, sums_ref, node_ref, hot_ref, heat_ref = refs[:8]
    if last:
        tile_ref, flag_ref, contact_ref, partial_ref, spread, listed, push = refs[8:]
    else:
        contact_ref, total_ref, spread, listed, push = refs[8:]
    extent_z = contact_ref.shape[1]
    rows = contact_ref.shape[0] // 3
    point_rows = own_ref.shape[0] // 24 * 24
    blocks = node_ref.shape[0]
    heats = []

    def store(j, sums):
        for p in range(3):
            push[p : p + 1, j * SEG : (j + 1) * SEG] = PENALTY * jnp.sum(sums[p], axis=0, keepdims=True)
        heats.append(SHORT_GAIN * jnp.sum(sums[3], axis=0, keepdims=True))

    sources = [upper_ref[0:point_rows, extent_z:]] + [far_ref[i, 0:point_rows, :] for i in range(far_ref.shape[0])]
    sums_of = lambda j: tuple(sums_ref[j, q] for q in range(4))
    pair_sums(bins_ref, own_ref, sources, 2 * blocks, bin_count, sums_of, store, spread, listed)
    row, _ = node_split(node_ref, extent_z)
    at_row = lax.broadcasted_iota(jnp.int32, (rows, row.shape[1]), 0) == row
    for p in range(3):
        placed = jnp.where(at_row, push[p : p + 1, :], 0.0)
        contact_ref[p * rows : (p + 1) * rows, :] = sum(
            jnp.dot(piece, hot_ref[...], preferred_element_type=F32) for piece in split_two(placed)
        )
    total = heat_ref[...] + jnp.concatenate(heats, axis=0)
    if not last:
        total_ref[...] = total
        return
    flat = jnp.concatenate([total[j : j + 1, :] for j in range(blocks)], axis=1)
    side, slot = tile_ref[0:1, :], tile_ref[1:2, :]
    hot_slot = one_hot_z(slot, TILE_DEV)
    at_side = lax.broadcasted_iota(jnp.int32, (8, flat.shape[1]), 0) == side
    placed = jnp.where(at_side, flat, 0.0)
    high, low = split_two(placed)
    lowest = (placed - high.astype(F32) - low.astype(F32)).astype(BF16)
    made = sum(lax.dot_general(piece, hot_slot, NT, preferred_element_type=F32) for piece in (high, low, lowest))
    is_odd = flag_ref[4] > 0.5
    to_even = jnp.where(is_odd, made[0:1], made[2:3])
    to_odd = jnp.where(is_odd, made[2:3], made[0:1])
    partial_ref[...] = jnp.concatenate([to_even, made[1:2], to_odd, made[3:]], axis=0)


def turn_body(extent_z, node_ref, out_ref):
    node = node_ref[...]
    column = lax.rem(node, jnp.int32(extent_z)).astype(F32).T
    lane = lax.broadcasted_iota(jnp.int32, (SEG, extent_z), 1).astype(F32)
    for j in range(node.shape[0]):
        out_ref[j * SEG : (j + 1) * SEG, :] = jnp.where(lane == column[:, j : j + 1], 1.0, 0.0).astype(BF16)


def tile_body(own_ref, tiles_ref, node_ref, hot_ref, out_ref):
    extent_x, extent_y, extent_z = tiles_ref.shape
    row, _ = node_split(node_ref, extent_z)
    hot = hot_ref[...]
    tiles = tiles_ref[...].reshape(extent_x * extent_y, extent_z)
    device = lax.div(tiles, jnp.int32(TILE_DEV))
    slot = tiles - device * TILE_DEV
    offset = (device - own_ref[0]).astype(F32).astype(BF16)
    found = gather_nodes([offset], row, hot)
    side = jnp.where(found < -0.5, 0, jnp.where(found > 0.5, 2, 1))
    found_slot = gather_nodes([slot.astype(F32).astype(BF16)], row, hot).astype(jnp.int32)
    rest = jnp.zeros((6, row.shape[1]), jnp.int32)
    out_ref[...] = jnp.concatenate([side, found_slot, rest], axis=0)


WHICH = ((0, 3, 4), (3, 1, 5), (4, 5, 2))
SCALE = -1.0 / 16.0


def ahead_z(value):
    return pltpu.roll(value, value.shape[1] - 1, 1)


def behind_z(value):
    return pltpu.roll(value, 1, 1)


def ahead_row(value):
    return pltpu.roll(value, value.shape[0] - 1, 0)


def behind_row(value):
    return pltpu.roll(value, 1, 0)


def features(near, far):
    total, change = near + far, far - near
    total_z = ahead_z(total)
    return total + total_z, change + ahead_z(change), total_z - total


def stress_of(along_x, along_y, along_z, volume_modulus, shear):
    volume = volume_modulus * (along_x[0] + along_y[1] + along_z[2])
    twice = shear + shear
    return (
        twice * along_x[0] + volume,
        twice * along_y[1] + volume,
        twice * along_z[2] + volume,
        shear * (along_y[0] + along_x[1]),
        shear * (along_z[0] + along_x[2]),
        shear * (along_z[1] + along_y[2]),
    )


def spread_z(plain, slope):
    return (plain - slope) + behind_z(plain + slope)


def inner_body(disp_ref, moduli_ref, out_ref, feature, stress):
    _, extent_x, extent_y, extent_z = disp_ref.shape

    def fill(x, carry):
        for p in range(3):
            value = disp_ref[p, x]
            for q, part in enumerate(features(value, ahead_row(value))):
                feature[x, 3 * q + p] = part
        return carry

    lax.fori_loop(0, extent_x, fill, 0)
    for c in range(6):
        stress[0, c] = jnp.zeros((extent_y, extent_z), F32)
        stress[extent_x, c] = jnp.zeros((extent_y, extent_z), F32)
    place = lax.broadcasted_iota(jnp.int32, (8, extent_z), 0)

    def load(x, carry):
        for t in range(extent_y // 8):
            rows = slice(t * 8, t * 8 + 8)
            scale = jnp.where(place == 7, 0.0, SCALE) if t == extent_y // 8 - 1 else SCALE
            along_x = [feature[x + 1, p, rows] - feature[x, p, rows] for p in range(3)]
            along_y = [feature[x + 1, 3 + p, rows] + feature[x, 3 + p, rows] for p in range(3)]
            along_z = [feature[x + 1, 6 + p, rows] + feature[x, 6 + p, rows] for p in range(3)]
            found = stress_of(along_x, along_y, along_z, moduli_ref[0, x, rows] * scale, moduli_ref[1, x, rows] * scale)
            for c in range(6):
                stress[x + 1, c, rows] = found[c]
        return carry

    lax.fori_loop(0, extent_x - 1, load, 0)

    def force(x, carry):
        for p in range(3):
            of_x, of_y, of_z = WHICH[p]
            part_x = stress[x, of_x] - stress[x + 1, of_x]
            part_y = stress[x, of_y] + stress[x + 1, of_y]
            part_z = stress[x, of_z] + stress[x + 1, of_z]
            plain = (part_x - part_y) + behind_row(part_x + part_y)
            out_ref[p, x] = spread_z(plain, part_z + behind_row(part_z))
        return carry

    lax.fori_loop(0, extent_x, force, 0)


def update_body(first, last, *refs):
    refs = list(refs)
    take = lambda count: [refs.pop(0) for _ in range(count)]
    flag_ref, disp_ref, vel_ref, mass_ref, inner_ref, contact_ref = take(6)
    own_up_ref, own_down_ref, lower_ref, upper_ref, even_ref, odd_ref, rim_ref = take(7)
    if not last:
        base_ref, node_ref, hot_ref = take(3)
    new_disp_ref, new_vel_ref = take(2)
    if not last:
        up_ref, down_ref, far_ref = take(3)
    if first:
        moduli_ref, rim_ref = rim_ref, take(1)[0]
    (side_low, side_high, face_low, face_high) = take(4)
    _, extent_x, extent_y, extent_z = disp_ref.shape
    has_lower, has_upper, has_back, has_front = [flag_ref[i] for i in range(4)]
    is_odd = flag_ref[4] > 0.5
    place = lax.broadcasted_iota(jnp.int32, (8, extent_z), 0)
    all_but_last = lax.broadcasted_iota(jnp.int32, (extent_y, extent_z), 0) < extent_y - 1
    main = 3 * extent_y

    def back(begin, count):
        rows = slice(begin, begin + count)
        return jnp.where(is_odd, even_ref[rows, :], odd_ref[rows, :]) * has_back

    def front(begin, count):
        rows = slice(begin, begin + count)
        return jnp.where(is_odd, odd_ref[rows, :], even_ref[rows, :]) * has_front

    def ring(tile, above, below):
        return jnp.concatenate([tile, jnp.where(place == 0, above, jnp.where(place == 7, below, 0.0))], axis=0)

    if first:
        for m in range(2):
            at = slice((3 + m) * extent_x, (4 + m) * extent_x)
            begin = main + 8 + m * extent_y
            of_back = back(begin, extent_y)
            high = ring(own_up_ref[at, 0:extent_z], 0.0, of_back[extent_y - 1 :])
            low = ring(lower_ref[at, 0:extent_z] * has_lower, 0.0, back(main + 6 + m, 1))
            rim_ref[m] = high * SCALE
            rim_ref[2 + m] = low * SCALE
            rim_ref[4 + m] = jnp.where(all_but_last, of_back * SCALE, 0.0)
            rim_ref[6 + m] = jnp.where(all_but_last, moduli_ref[m, extent_x - 1] * SCALE, 0.0)

    def rows_of(tile_ref, weight, row, extra):
        made = []
        for p in range(3):
            at = main + extra + p if row is None else p * extent_y + row
            tile = tile_ref[p * extent_x : (p + 1) * extent_x, 0:extent_z]
            tile = tile if weight is None else tile * weight
            made.append(ring(tile, front(at, 1), back(at, 1)))
        return made

    def side(near, far, at, sign, target):
        parts = [features(near[p], far[p]) for p in range(3)]
        along_x = [ahead_row(parts[p][0]) - parts[p][0] for p in range(3)]
        along_y = [ahead_row(parts[p][1]) + parts[p][1] for p in range(3)]
        along_z = [ahead_row(parts[p][2]) + parts[p][2] for p in range(3)]
        found = stress_of(along_x, along_y, along_z, rim_ref[at], rim_ref[at + 1])
        for p in range(3):
            of_x, of_y, of_z = [found[c] for c in WHICH[p]]
            part_x = (behind_row(of_x) - of_x)[:extent_x]
            part_y = (behind_row(of_y) + of_y)[:extent_x]
            part_z = (behind_row(of_z) + of_z)[:extent_x]
            target[p] = spread_z(part_x + sign * part_y, part_z)

    side(rows_of(own_up_ref, None, extent_y - 1, 0), rows_of(upper_ref, has_upper, None, 0), 0, -1.0, side_high)
    side(rows_of(lower_ref, has_lower, None, 3), rows_of(own_down_ref, None, 0, 0), 2, 1.0, side_low)

    def face(near, far, at, sign, target):
        parts_near = [features(value, ahead_row(value)) for value in near]
        parts_far = [features(value, ahead_row(value)) for value in far]
        along_x = [parts_far[p][0] - parts_near[p][0] for p in range(3)]
        along_y = [parts_far[p][1] + parts_near[p][1] for p in range(3)]
        along_z = [parts_far[p][2] + parts_near[p][2] for p in range(3)]
        found = stress_of(along_x, along_y, along_z, rim_ref[at], rim_ref[at + 1])
        for p in range(3):
            of_x, of_y, of_z = [found[c] for c in WHICH[p]]
            of_x = of_x * sign
            plain = (of_x - of_y) + behind_row(of_x + of_y)
            target[p] = spread_z(plain, of_z + behind_row(of_z))

    layer_of = lambda side_of: [side_of(p * extent_y, extent_y) for p in range(3)]
    own_layer = lambda x: [disp_ref[p, x] for p in range(3)]
    face(layer_of(back), own_layer(0), 4, 1.0, face_low)
    face(own_layer(extent_x - 1), layer_of(front), 6, -1.0, face_high)

    for x in range(extent_x):
        step_mass = TIME_STEP / mass_ref[x]
        for p in range(3):
            at = (p * extent_x + x) * extent_y
            load = inner_ref[p, x] + contact_ref[at : at + extent_y, :]
            if x == 0:
                load = load + face_low[p]
            if x == extent_x - 1:
                load = load + face_high[p]
            begin = load[:8] + jnp.where(place == 0, side_low[p, x : x + 1, :], 0.0)
            end = load[extent_y - 8 :] + jnp.where(place == 7, side_high[p, x : x + 1, :], 0.0)
            load = jnp.concatenate([begin, load[8 : extent_y - 8], end] if extent_y > 16 else [begin, end], axis=0)
            speed = vel_ref[p, x] + step_mass * load
            new_vel_ref[p, x] = speed
            new_disp_ref[p, x] = disp_ref[p, x] + TIME_STEP * speed
    if not last:
        store_messages(new_disp_ref, base_ref, node_ref, hot_ref[...], up_ref, down_ref, far_ref)


def per_device(displacement, velocity, moduli, nodal_mass, segment_node, segment_base, contact_bin, element_tile):
    shape = displacement.shape
    _, extent_x, extent_y, extent_z = shape
    steps = contact_bin.shape[0]
    segments = segment_node.shape[0]
    blocks = segments // SEG
    bin_count = lax.axis_size("bin")
    bin_at = lax.axis_index("bin")
    dom_at, dom_count = lax.axis_index("dom"), lax.axis_size("dom")
    own_device = dom_at * bin_count + bin_at
    checks = (bin_at > 0, bin_at < bin_count - 1, dom_at > 0, dom_at < dom_count - 1, dom_at % 2 == 1)
    flags = jnp.stack(checks).astype(F32)
    node = segment_node.reshape(blocks, SEG)
    bins = contact_bin[:, :, 0]
    rows = 3 * extent_x
    wide = extent_z + SEG
    struct = lambda *dims: jax.ShapeDtypeStruct(dims, F32)
    layer_rows = 3 * extent_y + 8
    full = lambda *dims: pl.BlockSpec(dims, lambda i: (0,) * len(dims))

    first_outs = [
        struct(rows + 16, wide),
        struct(rows + 8, wide),
        struct(rows + 8, SEG),
        jax.ShapeDtypeStruct((extent_z, segments), BF16),
    ]
    first_args = (displacement, segment_base, node, moduli, bins)
    first_specs = [full(*v.shape) for v in first_args]
    first_specs[3] = pl.BlockSpec((2, extent_x, 8, extent_z), lambda i: (0, 0, extent_y // 8 - 1, 0))
    up, down, far, hot = pl.pallas_call(
        first_body,
        grid=(1,),
        out_shape=first_outs,
        in_specs=first_specs,
        out_specs=[full(*v.shape) for v in first_outs],
        compiler_params=pltpu.CompilerParams(vmem_limit_bytes=60 * 1024 * 1024),
        cost_estimate=pl.CostEstimate(flops=1_000, bytes_accessed=1_000, transcendentals=0),
    )(*first_args)
    (turned,) = call(
        functools.partial(turn_body, extent_z),
        [jax.ShapeDtypeStruct((segments, extent_z), BF16)],
        specs=[WHOLE],
    )(node)
    (tile_places,) = call(
        tile_body, [jax.ShapeDtypeStruct((8, segments), jnp.int32)], specs=[SCALARS] + [WHOLE] * 3
    )(own_device[None].astype(jnp.int32), element_tile, node, hot)
    heat = jnp.zeros((blocks, SEG), F32)
    rim = moduli
    for step in range(steps):
        lower = cycled(up, "bin", 1)
        upper = cycled(down, "bin", -1)
        others = jnp.stack([cycled(far, "bin", shift) for shift in range(2, bin_count - 1)])
        first, last = step == 0, step == steps - 1
        (inner,) = call(
            inner_body,
            [struct(*shape)],
            [pltpu.VMEM((extent_x, 9, extent_y, extent_z), F32), pltpu.VMEM((extent_x + 1, 6, extent_y, extent_z), F32)],
            [WHOLE] * 2,
        )(displacement, moduli)
        if first:
            of_bins = [bins.astype(F32)]
            of_bins += [v[rows : rows + steps, extent_z : extent_z + blocks] for v in (lower, upper)]
            of_bins += [v[rows : rows + steps, :blocks] for v in others]
            all_bins = jnp.concatenate(of_bins, axis=1).astype(jnp.int32)
        layer = lambda at, count=3: pl.BlockSpec((count, 1, extent_y, extent_z), lambda i: (0, at, 0, 0))
        send_rows = layer_rows + (2 * extent_y if first else 0)
        layer_args = [flags, displacement, displacement, lower, upper, inner, others]
        layer_specs = [SCALARS, layer(0), layer(extent_x - 1), full(*lower.shape), full(*upper.shape)]
        layer_specs += [pl.BlockSpec(memory_space=pl.ANY)] * 2
        if first:
            layer_args.append(moduli)
            layer_specs.append(layer(extent_x - 1, 2))
        to_even, to_odd = pl.pallas_call(
            functools.partial(layer_body, first),
            grid=(1,),
            out_shape=[struct(send_rows, extent_z)] * 2,
            in_specs=layer_specs,
            out_specs=[full(send_rows, extent_z)] * 2,
            compiler_params=pltpu.CompilerParams(vmem_limit_bytes=VMEM_BYTES),
            cost_estimate=pl.CostEstimate(flops=1_000, bytes_accessed=1_000, transcendentals=0),
        )(*layer_args)
        of_even = swapped(to_even, "dom", False)
        near_blocks = 2 * blocks
        far_blocks = blocks * (bin_count - 2)
        pair_scratch = lambda count: [
            pltpu.VMEM((count + 1, 3, SEG, SEG), F32),
            pltpu.SMEM((bin_count * (count + 2),), jnp.int32),
        ]
        (sums,) = call(
            functools.partial(near_body, bin_count),
            [struct(blocks, 4, 8, SEG)],
            pair_scratch(near_blocks),
            [SCALARS, WHOLE, WHOLE, pl.BlockSpec(memory_space=pl.ANY)],
        )(all_bins[step], far, lower, to_even)
        to_odd, sums, of_even = lax.optimization_barrier((to_odd, sums, of_even))
        of_odd = swapped(to_odd, "dom", True)
        pair_args = [all_bins[step], far, upper, others, sums, node, turned, heat]
        if last:
            pair_args += [tile_places, flags]
        contact, heat = call(
            functools.partial(rest_body, bin_count, last),
            [struct(3 * extent_x * extent_y, extent_z), struct(8, TILE_DEV) if last else struct(blocks, SEG)],
            pair_scratch(far_blocks) + [pltpu.VMEM((8, segments), F32)],
            [SCALARS] + [WHOLE] * (len(pair_args) - 2) + [SCALARS if last else WHOLE],
        )(*pair_args)
        if last:
            heat, of_even, of_odd = lax.optimization_barrier((heat, of_even, of_odd))
        update_args = [flags, displacement, velocity, nodal_mass, inner, contact, up, down, lower, upper]
        update_args += [of_even, of_odd, rim]
        update_outs = [struct(*shape), struct(*shape)]
        if not last:
            update_args += [segment_base, node, hot]
            update_outs += [struct(rows, wide), struct(rows, wide), struct(rows, SEG)]
        if first:
            update_outs.append(struct(8, extent_y, extent_z))
        made = call(
            functools.partial(update_body, first, last),
            update_outs,
            [pltpu.VMEM((3, extent_x, extent_z), F32)] * 2 + [pltpu.VMEM((3, extent_y, extent_z), F32)] * 2,
            [SCALARS] + [WHOLE] * (len(update_args) - 1),
        )(*update_args)
        displacement, velocity = made[:2]
        if not last:
            up, down, far = made[2:5]
        if first:
            rim = made[-1]
    odd_weight = jnp.where(dom_at % 2 == 1, flags[3], flags[2])
    from_even, from_odd = swapped(heat[0], "dom", False), swapped(heat[2], "dom", True)
    if dom_count % 2:
        from_even = from_even * flags[3]
    tile_heat = heat[1] + from_even + from_odd * odd_weight
    return displacement, velocity, tile_heat


def solution(mesh):
    placed = (
        P(None, "dom", "bin", None),
        P(None, "dom", "bin", None),
        P(None, "dom", "bin", None),
        P("dom", "bin", None),
        P(("dom", "bin")),
        P(None, ("dom", "bin")),
        P(None, ("dom", "bin"), None),
        P("dom", "bin", None),
    )
    return jax.shard_map(
        per_device,
        mesh=mesh,
        in_specs=placed,
        out_specs=(P(None, "dom", "bin", None), P(None, "dom", "bin", None), P(("dom", "bin"))),
        check_vma=False,
    )
```

```python
import functools
import jax
import jax.numpy as jnp
from jax import lax
from jax.experimental import pallas as pl
from jax.experimental.pallas import tpu as pltpu
from jax.sharding import PartitionSpec as P

SEG = 128
TILE_DEV = 256
RADIUS = 0.09
PENALTY = 4.0
SHORT_GAIN = 100.0
TIME_STEP = 0.2
VMEM_BYTES = 40 * 1024 * 1024
F32 = jnp.float32
BF16 = jnp.bfloat16
WHOLE = pl.BlockSpec(memory_space=pltpu.VMEM)
SCALARS = pl.BlockSpec(memory_space=pltpu.SMEM)
NT = (((1,), (1,)), ((), ()))


def swapped(value, axis):
    count = lax.axis_size(axis)
    return lax.ppermute(value, axis, [(i, i ^ 1) for i in range(count)])


def relayed(value, axis):
    count = lax.axis_size(axis)
    target = [i + 2 if i % 2 == 0 else i - 2 for i in range(count)]
    target[count - 2], target[1] = count - 1, 0
    return lax.ppermute(value, axis, list(enumerate(target)))


def cycled(value, axis, steps):
    count = lax.axis_size(axis)
    return lax.ppermute(value, axis, [(source, (source + steps) % count) for source in range(count)])


def call(body, outs, scratch=(), specs=None):
    return functools.partial(
        pl.pallas_call,
        body,
        out_shape=outs,
        out_specs=[WHOLE] * len(outs),
        scratch_shapes=list(scratch),
        compiler_params=pltpu.CompilerParams(vmem_limit_bytes=VMEM_BYTES),
        cost_estimate=pl.CostEstimate(flops=1_000, bytes_accessed=1_000, transcendentals=0),
    )(in_specs=specs)


def split_two(value):
    high = value.astype(BF16)
    return high, (value - high.astype(F32)).astype(BF16)


def node_split(node_ref, extent_z):
    node = jnp.concatenate([node_ref[j : j + 1, :] for j in range(node_ref.shape[0])], axis=1)
    return lax.div(node, jnp.int32(extent_z)), lax.rem(node, jnp.int32(extent_z))


def one_hot_z(column, extent_z):
    depth = lax.broadcasted_iota(jnp.int32, (extent_z, column.shape[1]), 0)
    return jnp.where(depth == column, 1.0, 0.0).astype(BF16)


def gather_nodes(pieces, row, hot):
    rows = pieces[0].shape[0]
    picked = sum(jnp.dot(piece, hot, preferred_element_type=F32) for piece in pieces)
    at_row = lax.broadcasted_iota(jnp.int32, (rows, row.shape[1]), 0) == row
    return jnp.sum(jnp.where(at_row, picked, 0.0), axis=0, keepdims=True)


def store_positions(disp_ref, base_ref, node_ref, hot, targets):
    extent_x, extent_y, extent_z = disp_ref.shape[1:]
    rows = extent_x * extent_y
    blocks = node_ref.shape[0]
    row, _ = node_split(node_ref, extent_z)
    for p in range(3):
        plane = disp_ref[p].reshape(rows, extent_z)
        points = base_ref[p : p + 1, :] + gather_nodes(split_two(plane), row, hot)
        tile = jnp.concatenate([points[:, j * SEG : (j + 1) * SEG] for j in range(blocks)], axis=0)
        for ref, lane in targets:
            ref[p * blocks : (p + 1) * blocks, lane : lane + SEG] = tile


def store_column(source_ref, at, target_ref, first):
    count, extent_x, _, extent_z = source_ref.shape
    for p in range(count):
        tile = jnp.concatenate([source_ref[p, x, at : at + 1, :] for x in range(extent_x)], axis=0)
        target_ref[first + p * extent_x : first + (p + 1) * extent_x, 0:extent_z] = tile


def store_messages(disp_ref, base_ref, node_ref, hot, up_ref, down_ref, far_ref):
    extent_y, extent_z = disp_ref.shape[2:]
    store_column(disp_ref, extent_y - 1, up_ref, 0)
    store_column(disp_ref, 0, down_ref, 0)
    store_positions(disp_ref, base_ref, node_ref, hot, [(up_ref, extent_z), (down_ref, extent_z), (far_ref, 0)])


def first_body(_, disp_ref, base_ref, node_ref, moduli_ref, bins_ref, up_ref, down_ref, far_ref, hot_ref):
    _, extent_x, extent_y, extent_z = disp_ref.shape
    _, column = node_split(node_ref, extent_z)
    hot_ref[...] = one_hot_z(column, extent_z)
    store_messages(disp_ref, base_ref, node_ref, hot_ref[...], up_ref, down_ref, far_ref)
    rows = 3 * extent_x
    store_column(moduli_ref, moduli_ref.shape[2] - 1, up_ref, rows)
    steps, blocks = bins_ref.shape
    bins = bins_ref[...].astype(F32)
    zeros = jnp.zeros((8, SEG), F32)
    up_ref[rows + 8 : rows + 16, extent_z:] = zeros
    down_ref[rows : rows + 8, 0:extent_z] = jnp.zeros((8, extent_z), F32)
    for ref, lane in ((up_ref, extent_z), (down_ref, extent_z), (far_ref, 0)):
        ref[rows : rows + 8, lane : lane + SEG] = zeros
        ref[rows : rows + steps, lane : lane + blocks] = bins


def layer_body(with_moduli, *refs):
    flag_ref, first_ref, last_ref, lower_ref, upper_ref = refs[:5]
    if with_moduli:
        moduli_ref, even_ref, odd_ref = refs[7:]
    else:
        even_ref, odd_ref = refs[7:]
    extent_y, extent_z = first_ref.shape[2:]
    main = 3 * extent_y
    extent_x = lower_ref.shape[0] // (5 if with_moduli else 3)
    has_lower, has_upper, is_odd = flag_ref[0], flag_ref[1], flag_ref[4] > 0.5
    for p in range(3):
        low, high = first_ref[p, 0], last_ref[p, 0]
        even_ref[p * extent_y : (p + 1) * extent_y, :] = jnp.where(is_odd, low, high)
        odd_ref[p * extent_y : (p + 1) * extent_y, :] = jnp.where(is_odd, high, low)
    edges = []
    for x in (0, extent_x - 1):
        at = [p * extent_x + x for p in range(3)]
        above = [upper_ref[i : i + 1, 0:extent_z] * has_upper for i in at]
        below = [lower_ref[i : i + 1, 0:extent_z] * has_lower for i in at]
        if with_moduli:
            at = [(3 + m) * extent_x + x for m in range(2)]
            rest = [lower_ref[i : i + 1, 0:extent_z] * has_lower for i in at]
        else:
            rest = [jnp.zeros((2, extent_z), F32)]
        edges.append(jnp.concatenate(above + below + rest, axis=0))
    even_ref[main : main + 8, :] = jnp.where(is_odd, edges[0], edges[1])
    odd_ref[main : main + 8, :] = jnp.where(is_odd, edges[1], edges[0])
    if with_moduli:
        for m in range(2):
            for target_ref in (even_ref, odd_ref):
                target_ref[main + 8 + m * extent_y : main + 8 + (m + 1) * extent_y, :] = moduli_ref[m, 0]


def pair_sums(bins_ref, own_ref, sources, begin, bin_count, sums_of, store, spread, listed):
    rows = own_ref.shape[0] // 24 * 24
    blocks = rows // 3
    total_blocks = blocks * len(sources)
    stride = total_blocks + 2
    counts = [jnp.int32(0)] * bin_count
    for i in range(total_blocks):
        named = bins_ref[begin + i]
        taken = counts[0]
        for b in range(1, bin_count):
            taken = jnp.where(named == b, counts[b], taken)
        listed[named * stride + taken] = i
        counts = [count + (named == b).astype(jnp.int32) for b, count in enumerate(counts)]
    for b in range(bin_count):
        listed[b * stride + counts[b]] = total_blocks
    spread[total_blocks] = jnp.full((3, SEG, SEG), 1000.0, F32)
    for d, source in enumerate(sources):
        turned = source.T
        for p in range(3):
            for j in range(blocks):
                at = p * blocks + j
                spread[d * blocks + j, p] = jnp.broadcast_to(turned[:, at : at + 1], (SEG, SEG))
    for j in range(blocks):
        named = bins_ref[j]
        count = counts[0]
        for b in range(1, bin_count):
            count = jnp.where(named == b, counts[b], count)
        point = [jnp.broadcast_to(own_ref[p * blocks + j : p * blocks + j + 1, :], (8, SEG)) for p in range(3)]

        def against(i, sums):
            sums = list(sums)
            others = [listed[named * stride + 2 * i + half] for half in range(2)]
            for other, g in [(other, g) for other in others for g in range(SEG // 8)]:
                delta = [point[p] - spread[other, p, g * 8 : (g + 1) * 8, :] for p in range(3)]
                square = delta[0] * delta[0] + delta[1] * delta[1] + delta[2] * delta[2]
                inverse = lax.rsqrt(jnp.maximum(square, 1e-30))
                pressure = jnp.maximum(RADIUS - square * inverse, 0.0)
                factor = pressure * jnp.minimum(inverse, 1.0 / (0.25 * RADIUS))
                for p in range(3):
                    sums[p] = sums[p] + factor * delta[p]
                sums[3] = sums[3] + pressure * pressure
            return tuple(sums)

        store(j, lax.fori_loop(0, (count + 1) // 2, against, sums_of(j)))


def near_body(bin_count, bins_ref, own_ref, lower_ref, _, sums_ref, spread, listed):
    rows = own_ref.shape[0] // 24 * 24
    extent_z = lower_ref.shape[1] - SEG

    def store(j, sums):
        for q in range(4):
            sums_ref[j, q] = sums[q]

    sources = [own_ref[0:rows, :], lower_ref[0:rows, extent_z:]]
    zero = (jnp.zeros((8, SEG), F32),) * 4
    pair_sums(bins_ref, own_ref, sources, 0, bin_count, lambda j: zero, store, spread, listed)


def rest_body(bin_count, last, *refs):
    bins_ref, own_ref, upper_ref, far_ref, sums_ref, node_ref, hot_ref, heat_ref = refs[:8]
    if last:
        tile_ref, flag_ref, contact_ref, partial_ref, spread, listed, push = refs[8:]
    else:
        contact_ref, total_ref, spread, listed, push = refs[8:]
    extent_z = contact_ref.shape[1]
    rows = contact_ref.shape[0] // 3
    point_rows = own_ref.shape[0] // 24 * 24
    blocks = node_ref.shape[0]
    heats = []

    def store(j, sums):
        for p in range(3):
            push[p : p + 1, j * SEG : (j + 1) * SEG] = PENALTY * jnp.sum(sums[p], axis=0, keepdims=True)
        heats.append(SHORT_GAIN * jnp.sum(sums[3], axis=0, keepdims=True))

    sources = [upper_ref[0:point_rows, extent_z:]] + [far_ref[i, 0:point_rows, :] for i in range(far_ref.shape[0])]
    sums_of = lambda j: tuple(sums_ref[j, q] for q in range(4))
    pair_sums(bins_ref, own_ref, sources, 2 * blocks, bin_count, sums_of, store, spread, listed)
    row, _ = node_split(node_ref, extent_z)
    at_row = lax.broadcasted_iota(jnp.int32, (rows, row.shape[1]), 0) == row
    for p in range(3):
        placed = jnp.where(at_row, push[p : p + 1, :], 0.0)
        contact_ref[p * rows : (p + 1) * rows, :] = sum(
            jnp.dot(piece, hot_ref[...], preferred_element_type=F32) for piece in split_two(placed)
        )
    total = heat_ref[...] + jnp.concatenate(heats, axis=0)
    if not last:
        total_ref[...] = total
        return
    flat = jnp.concatenate([total[j : j + 1, :] for j in range(blocks)], axis=1)
    side, slot = tile_ref[0:1, :], tile_ref[1:2, :]
    hot_slot = one_hot_z(slot, TILE_DEV)
    at_side = lax.broadcasted_iota(jnp.int32, (8, flat.shape[1]), 0) == side
    placed = jnp.where(at_side, flat, 0.0)
    high, low = split_two(placed)
    lowest = (placed - high.astype(F32) - low.astype(F32)).astype(BF16)
    made = sum(lax.dot_general(piece, hot_slot, NT, preferred_element_type=F32) for piece in (high, low, lowest))
    is_odd = flag_ref[4] > 0.5
    to_even = jnp.where(is_odd, made[0:1], made[2:3])
    to_odd = jnp.where(is_odd, made[2:3], made[0:1])
    partial_ref[...] = jnp.concatenate([made[1:2], to_even, to_odd, made[3:]], axis=0)


def turn_body(extent_z, node_ref, out_ref):
    node = node_ref[...]
    column = lax.rem(node, jnp.int32(extent_z)).astype(F32).T
    lane = lax.broadcasted_iota(jnp.int32, (SEG, extent_z), 1).astype(F32)
    for j in range(node.shape[0]):
        out_ref[j * SEG : (j + 1) * SEG, :] = jnp.where(lane == column[:, j : j + 1], 1.0, 0.0).astype(BF16)


def tile_body(own_ref, tiles_ref, node_ref, hot_ref, out_ref):
    extent_x, extent_y, extent_z = tiles_ref.shape
    row, _ = node_split(node_ref, extent_z)
    hot = hot_ref[...]
    tiles = tiles_ref[...].reshape(extent_x * extent_y, extent_z)
    device = lax.div(tiles, jnp.int32(TILE_DEV))
    slot = tiles - device * TILE_DEV
    offset = (device.astype(F32) - own_ref[5]).astype(BF16)
    found = gather_nodes([offset], row, hot)
    side = jnp.where(found < -0.5, 0, jnp.where(found > 0.5, 2, 1))
    found_slot = gather_nodes([slot.astype(F32).astype(BF16)], row, hot).astype(jnp.int32)
    rest = jnp.zeros((6, row.shape[1]), jnp.int32)
    out_ref[...] = jnp.concatenate([side, found_slot, rest], axis=0)


WHICH = ((0, 3, 4), (3, 1, 5), (4, 5, 2))
SCALE = -1.0 / 16.0


def ahead_z(value):
    return pltpu.roll(value, value.shape[1] - 1, 1)


def behind_z(value):
    return pltpu.roll(value, 1, 1)


def ahead_row(value):
    return pltpu.roll(value, value.shape[0] - 1, 0)


def behind_row(value):
    return pltpu.roll(value, 1, 0)


def features(near, far):
    total, change = near + far, far - near
    total_z = ahead_z(total)
    return total + total_z, change + ahead_z(change), total_z - total


def stress_of(along_x, along_y, along_z, volume_modulus, shear):
    volume = volume_modulus * (along_x[0] + along_y[1] + along_z[2])
    twice = shear + shear
    return (
        twice * along_x[0] + volume,
        twice * along_y[1] + volume,
        twice * along_z[2] + volume,
        shear * (along_y[0] + along_x[1]),
        shear * (along_z[0] + along_x[2]),
        shear * (along_z[1] + along_y[2]),
    )


def spread_z(plain, slope):
    return (plain - slope) + behind_z(plain + slope)


def inner_body(disp_ref, moduli_ref, out_ref, feature, stress):
    _, extent_x, extent_y, extent_z = disp_ref.shape

    def fill(x, carry):
        for p in range(3):
            value = disp_ref[p, x]
            for q, part in enumerate(features(value, ahead_row(value))):
                feature[x, 3 * q + p] = part
        return carry

    lax.fori_loop(0, extent_x, fill, 0)
    for c in range(6):
        stress[0, c] = jnp.zeros((extent_y, extent_z), F32)
        stress[extent_x, c] = jnp.zeros((extent_y, extent_z), F32)
    place = lax.broadcasted_iota(jnp.int32, (8, extent_z), 0)

    def load(x, carry):
        for t in range(extent_y // 8):
            rows = slice(t * 8, t * 8 + 8)
            scale = jnp.where(place == 7, 0.0, SCALE) if t == extent_y // 8 - 1 else SCALE
            along_x = [feature[x + 1, p, rows] - feature[x, p, rows] for p in range(3)]
            along_y = [feature[x + 1, 3 + p, rows] + feature[x, 3 + p, rows] for p in range(3)]
            along_z = [feature[x + 1, 6 + p, rows] + feature[x, 6 + p, rows] for p in range(3)]
            found = stress_of(along_x, along_y, along_z, moduli_ref[0, x, rows] * scale, moduli_ref[1, x, rows] * scale)
            for c in range(6):
                stress[x + 1, c, rows] = found[c]
        return carry

    lax.fori_loop(0, extent_x - 1, load, 0)

    def force(x, carry):
        for p in range(3):
            of_x, of_y, of_z = WHICH[p]
            part_x = stress[x, of_x] - stress[x + 1, of_x]
            part_y = stress[x, of_y] + stress[x + 1, of_y]
            part_z = stress[x, of_z] + stress[x + 1, of_z]
            plain = (part_x - part_y) + behind_row(part_x + part_y)
            out_ref[p, x] = spread_z(plain, part_z + behind_row(part_z))
        return carry

    lax.fori_loop(0, extent_x, force, 0)


def update_body(first, last, *refs):
    refs = list(refs)
    take = lambda count: [refs.pop(0) for _ in range(count)]
    flag_ref, disp_ref, vel_ref, mass_ref, inner_ref, contact_ref = take(6)
    own_up_ref, own_down_ref, lower_ref, upper_ref, even_ref, odd_ref, rim_ref = take(7)
    if not last:
        base_ref, node_ref, hot_ref = take(3)
    new_disp_ref, new_vel_ref = take(2)
    if not last:
        up_ref, down_ref, far_ref = take(3)
    if first:
        moduli_ref, rim_ref = rim_ref, take(1)[0]
    (side_low, side_high, face_low, face_high) = take(4)
    _, extent_x, extent_y, extent_z = disp_ref.shape
    has_lower, has_upper, has_back, has_front = [flag_ref[i] for i in range(4)]
    is_odd = flag_ref[4] > 0.5
    place = lax.broadcasted_iota(jnp.int32, (8, extent_z), 0)
    all_but_last = lax.broadcasted_iota(jnp.int32, (extent_y, extent_z), 0) < extent_y - 1
    main = 3 * extent_y

    def back(begin, count):
        rows = slice(begin, begin + count)
        return jnp.where(is_odd, even_ref[rows, :], odd_ref[rows, :]) * has_back

    def front(begin, count):
        rows = slice(begin, begin + count)
        return jnp.where(is_odd, odd_ref[rows, :], even_ref[rows, :]) * has_front

    def ring(tile, above, below):
        return jnp.concatenate([tile, jnp.where(place == 0, above, jnp.where(place == 7, below, 0.0))], axis=0)

    if first:
        for m in range(2):
            at = slice((3 + m) * extent_x, (4 + m) * extent_x)
            begin = main + 8 + m * extent_y
            of_back = back(begin, extent_y)
            high = ring(own_up_ref[at, 0:extent_z], 0.0, of_back[extent_y - 1 :])
            low = ring(lower_ref[at, 0:extent_z] * has_lower, 0.0, back(main + 6 + m, 1))
            rim_ref[m] = high * SCALE
            rim_ref[2 + m] = low * SCALE
            rim_ref[4 + m] = jnp.where(all_but_last, of_back * SCALE, 0.0)
            rim_ref[6 + m] = jnp.where(all_but_last, moduli_ref[m, extent_x - 1] * SCALE, 0.0)

    def rows_of(tile_ref, weight, row, extra):
        made = []
        for p in range(3):
            at = main + extra + p if row is None else p * extent_y + row
            tile = tile_ref[p * extent_x : (p + 1) * extent_x, 0:extent_z]
            tile = tile if weight is None else tile * weight
            made.append(ring(tile, front(at, 1), back(at, 1)))
        return made

    def side(near, far, at, sign, target):
        parts = [features(near[p], far[p]) for p in range(3)]
        along_x = [ahead_row(parts[p][0]) - parts[p][0] for p in range(3)]
        along_y = [ahead_row(parts[p][1]) + parts[p][1] for p in range(3)]
        along_z = [ahead_row(parts[p][2]) + parts[p][2] for p in range(3)]
        found = stress_of(along_x, along_y, along_z, rim_ref[at], rim_ref[at + 1])
        for p in range(3):
            of_x, of_y, of_z = [found[c] for c in WHICH[p]]
            part_x = (behind_row(of_x) - of_x)[:extent_x]
            part_y = (behind_row(of_y) + of_y)[:extent_x]
            part_z = (behind_row(of_z) + of_z)[:extent_x]
            target[p] = spread_z(part_x + sign * part_y, part_z)

    side(rows_of(own_up_ref, None, extent_y - 1, 0), rows_of(upper_ref, has_upper, None, 0), 0, -1.0, side_high)
    side(rows_of(lower_ref, has_lower, None, 3), rows_of(own_down_ref, None, 0, 0), 2, 1.0, side_low)

    def face(near, far, at, sign, target):
        parts_near = [features(value, ahead_row(value)) for value in near]
        parts_far = [features(value, ahead_row(value)) for value in far]
        along_x = [parts_far[p][0] - parts_near[p][0] for p in range(3)]
        along_y = [parts_far[p][1] + parts_near[p][1] for p in range(3)]
        along_z = [parts_far[p][2] + parts_near[p][2] for p in range(3)]
        found = stress_of(along_x, along_y, along_z, rim_ref[at], rim_ref[at + 1])
        for p in range(3):
            of_x, of_y, of_z = [found[c] for c in WHICH[p]]
            of_x = of_x * sign
            plain = (of_x - of_y) + behind_row(of_x + of_y)
            target[p] = spread_z(plain, of_z + behind_row(of_z))

    layer_of = lambda side_of: [side_of(p * extent_y, extent_y) for p in range(3)]
    own_layer = lambda x: [disp_ref[p, x] for p in range(3)]
    face(layer_of(back), own_layer(0), 4, 1.0, face_low)
    face(own_layer(extent_x - 1), layer_of(front), 6, -1.0, face_high)

    for x in range(extent_x):
        step_mass = TIME_STEP / mass_ref[x]
        for p in range(3):
            at = (p * extent_x + x) * extent_y
            load = inner_ref[p, x] + contact_ref[at : at + extent_y, :]
            if x == 0:
                load = load + face_low[p]
            if x == extent_x - 1:
                load = load + face_high[p]
            begin = load[:8] + jnp.where(place == 0, side_low[p, x : x + 1, :], 0.0)
            end = load[extent_y - 8 :] + jnp.where(place == 7, side_high[p, x : x + 1, :], 0.0)
            load = jnp.concatenate([begin, load[8 : extent_y - 8], end] if extent_y > 16 else [begin, end], axis=0)
            speed = vel_ref[p, x] + step_mass * load
            new_vel_ref[p, x] = speed
            new_disp_ref[p, x] = disp_ref[p, x] + TIME_STEP * speed
    if not last:
        store_messages(new_disp_ref, base_ref, node_ref, hot_ref[...], up_ref, down_ref, far_ref)


def per_device(displacement, velocity, moduli, nodal_mass, segment_node, segment_base, contact_bin, element_tile):
    shape = displacement.shape
    _, extent_x, extent_y, extent_z = shape
    steps = contact_bin.shape[0]
    segments = segment_node.shape[0]
    blocks = segments // SEG
    bin_count = lax.axis_size("bin")
    bin_at = lax.axis_index("bin")
    dom_at, dom_count = lax.axis_index("dom"), lax.axis_size("dom")
    own_device = dom_at * bin_count + bin_at
    checks = (bin_at > 0, bin_at < bin_count - 1, dom_at > 0, dom_at < dom_count - 1, (dom_at & 1) == 1)
    flags = jnp.concatenate([jnp.stack(checks).astype(F32), own_device[None].astype(F32)])
    node = segment_node.reshape(blocks, SEG)
    bins = contact_bin[:, :, 0]
    rows = 3 * extent_x
    wide = extent_z + SEG
    struct = lambda *dims: jax.ShapeDtypeStruct(dims, F32)
    layer_rows = 3 * extent_y + 8
    full = lambda *dims: pl.BlockSpec(dims, lambda i: (0,) * len(dims))

    first_outs = [
        struct(rows + 16, wide),
        struct(rows + 8, wide),
        struct(rows + 8, SEG),
        jax.ShapeDtypeStruct((extent_z, segments), BF16),
    ]
    first_args = (flags, displacement, segment_base, node, moduli, bins)
    first_specs = [SCALARS] + [full(*v.shape) for v in first_args[1:]]
    first_specs[4] = pl.BlockSpec((2, extent_x, 8, extent_z), lambda i: (0, 0, extent_y // 8 - 1, 0))
    up, down, far, hot = pl.pallas_call(
        first_body,
        grid=(1,),
        out_shape=first_outs,
        in_specs=first_specs,
        out_specs=[full(*v.shape) for v in first_outs],
        compiler_params=pltpu.CompilerParams(vmem_limit_bytes=60 * 1024 * 1024),
        cost_estimate=pl.CostEstimate(flops=1_000, bytes_accessed=1_000, transcendentals=0),
    )(*first_args)
    (turned,) = call(
        functools.partial(turn_body, extent_z),
        [jax.ShapeDtypeStruct((segments, extent_z), BF16)],
        specs=[WHOLE],
    )(node)
    (tile_places,) = call(
        tile_body, [jax.ShapeDtypeStruct((8, segments), jnp.int32)], specs=[SCALARS] + [WHOLE] * 3
    )(flags, element_tile, node, hot)
    heat = jnp.zeros((blocks, SEG), F32)
    rim = moduli
    for step in range(steps):
        lower = cycled(up, "bin", 1)
        upper = cycled(down, "bin", -1)
        others = jnp.stack([cycled(far, "bin", shift) for shift in range(2, bin_count - 1)])
        first, last = step == 0, step == steps - 1
        (inner,) = call(
            inner_body,
            [struct(*shape)],
            [pltpu.VMEM((extent_x, 9, extent_y, extent_z), F32), pltpu.VMEM((extent_x + 1, 6, extent_y, extent_z), F32)],
            [WHOLE] * 2,
        )(displacement, moduli)
        if first:
            of_bins = [far[rows : rows + steps, :blocks]]
            of_bins += [v[rows : rows + steps, extent_z : extent_z + blocks] for v in (lower, upper)]
            of_bins += [v[rows : rows + steps, :blocks] for v in others]
            all_bins = jnp.concatenate(of_bins, axis=1).astype(jnp.int32)
        layer = lambda at, count=3: pl.BlockSpec((count, 1, extent_y, extent_z), lambda i: (0, at, 0, 0))
        send_rows = layer_rows + (2 * extent_y if first else 0)
        layer_args = [flags, displacement, displacement, lower, upper, inner, others]
        layer_specs = [SCALARS, layer(0), layer(extent_x - 1), full(*lower.shape), full(*upper.shape)]
        layer_specs += [pl.BlockSpec(memory_space=pl.ANY)] * 2
        if first:
            layer_args.append(moduli)
            layer_specs.append(layer(extent_x - 1, 2))
        to_even, to_odd = pl.pallas_call(
            functools.partial(layer_body, first),
            grid=(1,),
            out_shape=[struct(send_rows, extent_z)] * 2,
            in_specs=layer_specs,
            out_specs=[full(send_rows, extent_z)] * 2,
            compiler_params=pltpu.CompilerParams(vmem_limit_bytes=VMEM_BYTES),
            cost_estimate=pl.CostEstimate(flops=1_000, bytes_accessed=1_000, transcendentals=0),
        )(*layer_args)
        relay = swapped(to_odd, "dom")
        near_blocks = 2 * blocks
        far_blocks = blocks * (bin_count - 2)
        pair_scratch = lambda count: [
            pltpu.VMEM((count + 1, 3, SEG, SEG), F32),
            pltpu.SMEM((bin_count * (count + 2),), jnp.int32),
        ]
        (sums,) = call(
            functools.partial(near_body, bin_count),
            [struct(blocks, 4, 8, SEG)],
            pair_scratch(near_blocks),
            [SCALARS, WHOLE, WHOLE, pl.BlockSpec(memory_space=pl.ANY)],
        )(all_bins[step], far, lower, to_odd)
        to_even, sums, relay = lax.optimization_barrier((to_even, sums, relay))
        of_odd = relayed(relay, "dom")
        of_even = swapped(to_even, "dom")
        pair_args = [all_bins[step], far, upper, others, sums, node, turned, heat]
        if last:
            pair_args += [tile_places, flags]
        contact, heat = call(
            functools.partial(rest_body, bin_count, last),
            [struct(3 * extent_x * extent_y, extent_z), struct(8, TILE_DEV) if last else struct(blocks, SEG)],
            pair_scratch(far_blocks) + [pltpu.VMEM((8, segments), F32)],
            [SCALARS] + [WHOLE] * (len(pair_args) - 2) + [SCALARS if last else WHOLE],
        )(*pair_args)
        if last:
            heat, of_even, of_odd = lax.optimization_barrier((heat, of_even, of_odd))
        update_args = [flags, displacement, velocity, nodal_mass, inner, contact, up, down, lower, upper]
        update_args += [of_even, of_odd, rim]
        update_outs = [struct(*shape), struct(*shape)]
        if not last:
            update_args += [segment_base, node, hot]
            update_outs += [struct(rows, wide), struct(rows, wide), struct(rows, SEG)]
        if first:
            update_outs.append(struct(8, extent_y, extent_z))
        made = call(
            functools.partial(update_body, first, last),
            update_outs,
            [pltpu.VMEM((3, extent_x, extent_z), F32)] * 2 + [pltpu.VMEM((3, extent_y, extent_z), F32)] * 2,
            [SCALARS] + [WHOLE] * (len(update_args) - 1),
        )(*update_args)
        displacement, velocity = made[:2]
        if not last:
            up, down, far = made[2:5]
        if first:
            rim = made[-1]
    got = swapped(heat[1:3], "dom")
    passed = relayed(got[1], "dom")
    tile_heat = heat[0] + got[0] + passed
    return displacement, velocity, tile_heat


def solution(mesh):
    placed = (
        P(None, "dom", "bin", None),
        P(None, "dom", "bin", None),
        P(None, "dom", "bin", None),
        P("dom", "bin", None),
        P(("dom", "bin")),
        P(None, ("dom", "bin")),
        P(None, ("dom", "bin"), None),
        P("dom", "bin", None),
    )
    return jax.shard_map(
        per_device,
        mesh=mesh,
        in_specs=placed,
        out_specs=(P(None, "dom", "bin", None), P(None, "dom", "bin", None), P(("dom", "bin"))),
        check_vma=False,
    )
```

```python
import functools
import jax
import jax.numpy as jnp
from jax import lax
from jax.experimental import pallas as pl
from jax.experimental.pallas import tpu as pltpu
from jax.sharding import PartitionSpec as P

SEG = 128
TILE_DEV = 256
RADIUS = 0.09
PENALTY = 4.0
SHORT_GAIN = 100.0
TIME_STEP = 0.2
VMEM_BYTES = 40 * 1024 * 1024
F32 = jnp.float32
BF16 = jnp.bfloat16
WHOLE = pl.BlockSpec(memory_space=pltpu.VMEM)
SCALARS = pl.BlockSpec(memory_space=pltpu.SMEM)
NT = (((1,), (1,)), ((), ()))


def swapped(value, axis):
    count = lax.axis_size(axis)
    return lax.ppermute(value, axis, [(i, i ^ 1) for i in range(count)])


def relayed(value, axis):
    count = lax.axis_size(axis)
    target = [i + 2 if i % 2 == 0 else i - 2 for i in range(count)]
    target[count - 2], target[1] = count - 1, 0
    return lax.ppermute(value, axis, list(enumerate(target)))


def cycled(value, axis, steps):
    count = lax.axis_size(axis)
    return lax.ppermute(value, axis, [(source, (source + steps) % count) for source in range(count)])


def call(body, outs, scratch=(), specs=None):
    return functools.partial(
        pl.pallas_call,
        body,
        out_shape=outs,
        out_specs=[WHOLE] * len(outs),
        scratch_shapes=list(scratch),
        compiler_params=pltpu.CompilerParams(vmem_limit_bytes=VMEM_BYTES),
        cost_estimate=pl.CostEstimate(flops=1_000, bytes_accessed=1_000, transcendentals=0),
    )(in_specs=specs)


def split_two(value):
    high = value.astype(BF16)
    return high, (value - high.astype(F32)).astype(BF16)


def node_split(node_ref, extent_z):
    node = jnp.concatenate([node_ref[j : j + 1, :] for j in range(node_ref.shape[0])], axis=1)
    return lax.div(node, jnp.int32(extent_z)), lax.rem(node, jnp.int32(extent_z))


def one_hot_z(column, extent_z):
    depth = lax.broadcasted_iota(jnp.int32, (extent_z, column.shape[1]), 0)
    return jnp.where(depth == column, 1.0, 0.0).astype(BF16)


def gather_nodes(pieces, row, hot):
    rows = pieces[0].shape[0]
    picked = sum(jnp.dot(piece, hot, preferred_element_type=F32) for piece in pieces)
    at_row = lax.broadcasted_iota(jnp.int32, (rows, row.shape[1]), 0) == row
    return jnp.sum(jnp.where(at_row, picked, 0.0), axis=0, keepdims=True)


def store_positions(disp_ref, base_ref, node_ref, hot, targets):
    extent_x, extent_y, extent_z = disp_ref.shape[1:]
    rows = extent_x * extent_y
    blocks = node_ref.shape[0]
    row, _ = node_split(node_ref, extent_z)
    for p in range(3):
        plane = disp_ref[p].reshape(rows, extent_z)
        points = base_ref[p : p + 1, :] + gather_nodes(split_two(plane), row, hot)
        tile = jnp.concatenate([points[:, j * SEG : (j + 1) * SEG] for j in range(blocks)], axis=0)
        for ref, lane in targets:
            ref[p * blocks : (p + 1) * blocks, lane : lane + SEG] = tile


def store_column(source_ref, at, target_ref, first):
    count, extent_x, _, extent_z = source_ref.shape
    for p in range(count):
        tile = jnp.concatenate([source_ref[p, x, at : at + 1, :] for x in range(extent_x)], axis=0)
        target_ref[first + p * extent_x : first + (p + 1) * extent_x, 0:extent_z] = tile


def store_messages(flag_ref, disp_ref, base_ref, node_ref, hot, even_ref, odd_ref, up_ref, down_ref, point_ref):
    _, extent_x, extent_y, _ = disp_ref.shape
    is_odd = flag_ref[4] > 0.5
    for p in range(3):
        low, high = disp_ref[p, 0], disp_ref[p, extent_x - 1]
        even_ref[p * extent_y : (p + 1) * extent_y, :] = jnp.where(is_odd, low, high)
        odd_ref[p * extent_y : (p + 1) * extent_y, :] = jnp.where(is_odd, high, low)
    store_column(disp_ref, extent_y - 1, up_ref, 0)
    store_column(disp_ref, 0, down_ref, 0)
    store_positions(disp_ref, base_ref, node_ref, hot, [(point_ref, 0)])


def first_body(flag_ref, disp_ref, base_ref, node_ref, moduli_ref, layer_ref, bins_ref, *outs):
    even_ref, odd_ref, up_ref, down_ref, point_ref, hot_ref = outs
    _, extent_x, extent_y, extent_z = disp_ref.shape
    _, column = node_split(node_ref, extent_z)
    hot_ref[...] = one_hot_z(column, extent_z)
    for m in range(2):
        for target_ref in (even_ref, odd_ref):
            target_ref[(3 + m) * extent_y : (4 + m) * extent_y, :] = layer_ref[m, 0]
    store_messages(flag_ref, disp_ref, base_ref, node_ref, hot_ref[...], *outs[:5])
    rows = 3 * extent_x
    store_column(moduli_ref, moduli_ref.shape[2] - 1, up_ref, rows)
    steps, blocks = bins_ref.shape
    point_ref[rows : rows + 8, :] = jnp.zeros((8, SEG), F32)
    point_ref[rows : rows + steps, 0:blocks] = bins_ref[...].astype(F32)


def layers_of(flag_ref, even_ref, odd_ref):
    has_back, has_front, is_odd = flag_ref[2], flag_ref[3], flag_ref[4] > 0.5

    def back(begin, count):
        rows = slice(begin, begin + count)
        return jnp.where(is_odd, even_ref[rows, :], odd_ref[rows, :]) * has_back

    def front(begin, count):
        rows = slice(begin, begin + count)
        return jnp.where(is_odd, odd_ref[rows, :], even_ref[rows, :]) * has_front

    return back, front


def column_body(with_moduli, extent_y, flag_ref, own_up_ref, own_down_ref, even_ref, odd_ref, _, up_ref, down_ref):
    back, front = layers_of(flag_ref, even_ref, odd_ref)
    rows = own_down_ref.shape[0]
    for own_ref, target_ref, y in ((own_up_ref, up_ref, extent_y - 1), (own_down_ref, down_ref, 0)):
        target_ref[0:rows, :] = own_ref[0:rows, :]
        made = [front(p * extent_y + y, 1) for p in range(3)] + [back(p * extent_y + y, 1) for p in range(3)]
        made += [back((3 + m) * extent_y + y if with_moduli else 0, 1) for m in range(2)]
        target_ref[rows : rows + 8, :] = jnp.concatenate(made, axis=0)
    if with_moduli:
        up_ref[rows + 8 :, :] = own_up_ref[rows:, :]


def pair_sums(bins_ref, own_ref, sources, begin, bin_count, sums_of, store, spread, listed):
    rows = own_ref.shape[0] // 24 * 24
    blocks = rows // 3
    total_blocks = blocks * len(sources)
    stride = total_blocks + 2
    counts = [jnp.int32(0)] * bin_count
    for i in range(total_blocks):
        named = bins_ref[begin + i]
        taken = counts[0]
        for b in range(1, bin_count):
            taken = jnp.where(named == b, counts[b], taken)
        listed[named * stride + taken] = i
        counts = [count + (named == b).astype(jnp.int32) for b, count in enumerate(counts)]
    for b in range(bin_count):
        listed[b * stride + counts[b]] = total_blocks
    spread[total_blocks] = jnp.full((3, SEG, SEG), 1000.0, F32)
    for d, source in enumerate(sources):
        turned = source.T
        for p in range(3):
            for j in range(blocks):
                at = p * blocks + j
                spread[d * blocks + j, p] = jnp.broadcast_to(turned[:, at : at + 1], (SEG, SEG))
    for j in range(blocks):
        named = bins_ref[j]
        count = counts[0]
        for b in range(1, bin_count):
            count = jnp.where(named == b, counts[b], count)
        point = [jnp.broadcast_to(own_ref[p * blocks + j : p * blocks + j + 1, :], (8, SEG)) for p in range(3)]

        def against(i, sums):
            sums = list(sums)
            others = [listed[named * stride + 2 * i + half] for half in range(2)]
            for other, g in [(other, g) for other in others for g in range(SEG // 8)]:
                delta = [point[p] - spread[other, p, g * 8 : (g + 1) * 8, :] for p in range(3)]
                square = delta[0] * delta[0] + delta[1] * delta[1] + delta[2] * delta[2]
                inverse = lax.rsqrt(jnp.maximum(square, 1e-30))
                pressure = jnp.maximum(RADIUS - square * inverse, 0.0)
                factor = pressure * jnp.minimum(inverse, 1.0 / (0.25 * RADIUS))
                for p in range(3):
                    sums[p] = sums[p] + factor * delta[p]
                sums[3] = sums[3] + pressure * pressure
            return tuple(sums)

        store(j, lax.fori_loop(0, (count + 1) // 2, against, sums_of(j)))


def near_body(bin_count, bins_ref, own_ref, lower_ref, upper_ref, _, sums_ref, spread, listed):
    rows = own_ref.shape[0] // 24 * 24

    def store(j, sums):
        for q in range(4):
            sums_ref[j, q] = sums[q]

    sources = [ref[0:rows, :] for ref in (own_ref, lower_ref, upper_ref)]
    zero = (jnp.zeros((8, SEG), F32),) * 4
    pair_sums(bins_ref, own_ref, sources, 0, bin_count, lambda j: zero, store, spread, listed)


def rest_body(bin_count, last, *refs):
    bins_ref, own_ref, far_ref, sums_ref, node_ref, hot_ref, heat_ref = refs[:7]
    if last:
        tile_ref, flag_ref, contact_ref, partial_ref, spread, listed, push = refs[7:]
    else:
        contact_ref, total_ref, spread, listed, push = refs[7:]
    rows = contact_ref.shape[0] // 3
    point_rows = own_ref.shape[0] // 24 * 24
    blocks = node_ref.shape[0]
    heats = []

    def store(j, sums):
        for p in range(3):
            push[p : p + 1, j * SEG : (j + 1) * SEG] = PENALTY * jnp.sum(sums[p], axis=0, keepdims=True)
        heats.append(SHORT_GAIN * jnp.sum(sums[3], axis=0, keepdims=True))

    sources = [far_ref[i, 0:point_rows, :] for i in range(far_ref.shape[0])]
    sums_of = lambda j: tuple(sums_ref[j, q] for q in range(4))
    pair_sums(bins_ref, own_ref, sources, 3 * blocks, bin_count, sums_of, store, spread, listed)
    row, _ = node_split(node_ref, contact_ref.shape[1])
    at_row = lax.broadcasted_iota(jnp.int32, (rows, row.shape[1]), 0) == row
    for p in range(3):
        placed = jnp.where(at_row, push[p : p + 1, :], 0.0)
        contact_ref[p * rows : (p + 1) * rows, :] = sum(
            jnp.dot(piece, hot_ref[...], preferred_element_type=F32) for piece in split_two(placed)
        )
    total = heat_ref[...] + jnp.concatenate(heats, axis=0)
    if not last:
        total_ref[...] = total
        return
    flat = jnp.concatenate([total[j : j + 1, :] for j in range(blocks)], axis=1)
    side, slot = tile_ref[0:1, :], tile_ref[1:2, :]
    hot_slot = one_hot_z(slot, TILE_DEV)
    at_side = lax.broadcasted_iota(jnp.int32, (8, flat.shape[1]), 0) == side
    placed = jnp.where(at_side, flat, 0.0)
    high, low = split_two(placed)
    lowest = (placed - high.astype(F32) - low.astype(F32)).astype(BF16)
    made = sum(lax.dot_general(piece, hot_slot, NT, preferred_element_type=F32) for piece in (high, low, lowest))
    is_odd = flag_ref[4] > 0.5
    to_even = jnp.where(is_odd, made[0:1], made[2:3])
    to_odd = jnp.where(is_odd, made[2:3], made[0:1])
    partial_ref[...] = jnp.concatenate([made[1:2], to_even, to_odd, made[3:]], axis=0)


def turn_body(extent_z, node_ref, out_ref):
    node = node_ref[...]
    column = lax.rem(node, jnp.int32(extent_z)).astype(F32).T
    lane = lax.broadcasted_iota(jnp.int32, (SEG, extent_z), 1).astype(F32)
    for j in range(node.shape[0]):
        out_ref[j * SEG : (j + 1) * SEG, :] = jnp.where(lane == column[:, j : j + 1], 1.0, 0.0).astype(BF16)


def tile_body(own_ref, tiles_ref, node_ref, hot_ref, out_ref):
    extent_x, extent_y, extent_z = tiles_ref.shape
    row, _ = node_split(node_ref, extent_z)
    hot = hot_ref[...]
    tiles = tiles_ref[...].reshape(extent_x * extent_y, extent_z)
    device = lax.div(tiles, jnp.int32(TILE_DEV))
    slot = tiles - device * TILE_DEV
    offset = (device.astype(F32) - own_ref[5]).astype(BF16)
    found = gather_nodes([offset], row, hot)
    side = jnp.where(found < -0.5, 0, jnp.where(found > 0.5, 2, 1))
    found_slot = gather_nodes([slot.astype(F32).astype(BF16)], row, hot).astype(jnp.int32)
    rest = jnp.zeros((6, row.shape[1]), jnp.int32)
    out_ref[...] = jnp.concatenate([side, found_slot, rest], axis=0)


WHICH = ((0, 3, 4), (3, 1, 5), (4, 5, 2))
SCALE = -1.0 / 16.0


def ahead_z(value):
    return pltpu.roll(value, value.shape[1] - 1, 1)


def behind_z(value):
    return pltpu.roll(value, 1, 1)


def ahead_row(value):
    return pltpu.roll(value, value.shape[0] - 1, 0)


def behind_row(value):
    return pltpu.roll(value, 1, 0)


def features(near, far):
    total, change = near + far, far - near
    total_z = ahead_z(total)
    return total + total_z, change + ahead_z(change), total_z - total


def stress_of(along_x, along_y, along_z, volume_modulus, shear):
    volume = volume_modulus * (along_x[0] + along_y[1] + along_z[2])
    twice = shear + shear
    return (
        twice * along_x[0] + volume,
        twice * along_y[1] + volume,
        twice * along_z[2] + volume,
        shear * (along_y[0] + along_x[1]),
        shear * (along_z[0] + along_x[2]),
        shear * (along_z[1] + along_y[2]),
    )


def spread_z(plain, slope):
    return (plain - slope) + behind_z(plain + slope)


def inner_body(disp_ref, moduli_ref, out_ref, feature, stress):
    _, extent_x, extent_y, extent_z = disp_ref.shape

    def fill(x, carry):
        for p in range(3):
            value = disp_ref[p, x]
            for q, part in enumerate(features(value, ahead_row(value))):
                feature[x, 3 * q + p] = part
        return carry

    lax.fori_loop(0, extent_x, fill, 0)
    for c in range(6):
        stress[0, c] = jnp.zeros((extent_y, extent_z), F32)
        stress[extent_x, c] = jnp.zeros((extent_y, extent_z), F32)
    place = lax.broadcasted_iota(jnp.int32, (8, extent_z), 0)

    def load(x, carry):
        for t in range(extent_y // 8):
            rows = slice(t * 8, t * 8 + 8)
            scale = jnp.where(place == 7, 0.0, SCALE) if t == extent_y // 8 - 1 else SCALE
            along_x = [feature[x + 1, p, rows] - feature[x, p, rows] for p in range(3)]
            along_y = [feature[x + 1, 3 + p, rows] + feature[x, 3 + p, rows] for p in range(3)]
            along_z = [feature[x + 1, 6 + p, rows] + feature[x, 6 + p, rows] for p in range(3)]
            found = stress_of(along_x, along_y, along_z, moduli_ref[0, x, rows] * scale, moduli_ref[1, x, rows] * scale)
            for c in range(6):
                stress[x + 1, c, rows] = found[c]
        return carry

    lax.fori_loop(0, extent_x - 1, load, 0)

    def force(x, carry):
        for p in range(3):
            of_x, of_y, of_z = WHICH[p]
            part_x = stress[x, of_x] - stress[x + 1, of_x]
            part_y = stress[x, of_y] + stress[x + 1, of_y]
            part_z = stress[x, of_z] + stress[x + 1, of_z]
            plain = (part_x - part_y) + behind_row(part_x + part_y)
            out_ref[p, x] = spread_z(plain, part_z + behind_row(part_z))
        return carry

    lax.fori_loop(0, extent_x, force, 0)


def update_body(first, last, *refs):
    refs = list(refs)
    take = lambda count: [refs.pop(0) for _ in range(count)]
    flag_ref, disp_ref, vel_ref, mass_ref, inner_ref, contact_ref = take(6)
    own_up_ref, own_down_ref, lower_ref, upper_ref, even_ref, odd_ref, rim_ref = take(7)
    if not last:
        base_ref, node_ref, hot_ref = take(3)
    new_disp_ref, new_vel_ref = take(2)
    if not last:
        messages = take(5)
    if first:
        moduli_ref, rim_ref = rim_ref, take(1)[0]
    (side_low, side_high, face_low, face_high) = take(4)
    _, extent_x, extent_y, extent_z = disp_ref.shape
    has_lower, has_upper = flag_ref[0], flag_ref[1]
    back, front = layers_of(flag_ref, even_ref, odd_ref)
    column = 3 * extent_x
    place = lax.broadcasted_iota(jnp.int32, (8, extent_z), 0)
    all_but_last = lax.broadcasted_iota(jnp.int32, (extent_y, extent_z), 0) < extent_y - 1
    main = 3 * extent_y

    def ring(tile, above, below):
        return jnp.concatenate([tile, jnp.where(place == 0, above, jnp.where(place == 7, below, 0.0))], axis=0)

    if first:
        for m in range(2):
            at = slice((3 + m) * extent_x, (4 + m) * extent_x)
            below = slice(column + 8 + m * extent_x, column + 8 + (m + 1) * extent_x)
            of_back = back(main + m * extent_y, extent_y)
            high = ring(own_up_ref[at, :], 0.0, of_back[extent_y - 1 :])
            low = ring(lower_ref[below, :], 0.0, lower_ref[column + 6 + m : column + 7 + m, :]) * has_lower
            rim_ref[m] = high * SCALE
            rim_ref[2 + m] = low * SCALE
            rim_ref[4 + m] = jnp.where(all_but_last, of_back * SCALE, 0.0)
            rim_ref[6 + m] = jnp.where(all_but_last, moduli_ref[m, extent_x - 1] * SCALE, 0.0)

    def own_rows(tile_ref, y):
        at = [p * extent_y + y for p in range(3)]
        tiles = [tile_ref[p * extent_x : (p + 1) * extent_x, :] for p in range(3)]
        return [ring(tiles[p], front(at[p], 1), back(at[p], 1)) for p in range(3)]

    def halo_rows(ref, weight):
        made = []
        for p in range(3):
            above, below = ref[column + p : column + p + 1, :], ref[column + 3 + p : column + 4 + p, :]
            made.append(ring(ref[p * extent_x : (p + 1) * extent_x, :], above, below) * weight)
        return made

    def side(near, far, at, sign, target):
        parts = [features(near[p], far[p]) for p in range(3)]
        along_x = [ahead_row(parts[p][0]) - parts[p][0] for p in range(3)]
        along_y = [ahead_row(parts[p][1]) + parts[p][1] for p in range(3)]
        along_z = [ahead_row(parts[p][2]) + parts[p][2] for p in range(3)]
        found = stress_of(along_x, along_y, along_z, rim_ref[at], rim_ref[at + 1])
        for p in range(3):
            of_x, of_y, of_z = [found[c] for c in WHICH[p]]
            part_x = (behind_row(of_x) - of_x)[:extent_x]
            part_y = (behind_row(of_y) + of_y)[:extent_x]
            part_z = (behind_row(of_z) + of_z)[:extent_x]
            target[p] = spread_z(part_x + sign * part_y, part_z)

    side(own_rows(own_up_ref, extent_y - 1), halo_rows(upper_ref, has_upper), 0, -1.0, side_high)
    side(halo_rows(lower_ref, has_lower), own_rows(own_down_ref, 0), 2, 1.0, side_low)

    def face(near, far, at, sign, target):
        parts_near = [features(value, ahead_row(value)) for value in near]
        parts_far = [features(value, ahead_row(value)) for value in far]
        along_x = [parts_far[p][0] - parts_near[p][0] for p in range(3)]
        along_y = [parts_far[p][1] + parts_near[p][1] for p in range(3)]
        along_z = [parts_far[p][2] + parts_near[p][2] for p in range(3)]
        found = stress_of(along_x, along_y, along_z, rim_ref[at], rim_ref[at + 1])
        for p in range(3):
            of_x, of_y, of_z = [found[c] for c in WHICH[p]]
            of_x = of_x * sign
            plain = (of_x - of_y) + behind_row(of_x + of_y)
            target[p] = spread_z(plain, of_z + behind_row(of_z))

    layer_of = lambda side_of: [side_of(p * extent_y, extent_y) for p in range(3)]
    own_layer = lambda x: [disp_ref[p, x] for p in range(3)]
    face(layer_of(back), own_layer(0), 4, 1.0, face_low)
    face(own_layer(extent_x - 1), layer_of(front), 6, -1.0, face_high)

    for x in range(extent_x):
        step_mass = TIME_STEP / mass_ref[x]
        for p in range(3):
            at = (p * extent_x + x) * extent_y
            load = inner_ref[p, x] + contact_ref[at : at + extent_y, :]
            if x == 0:
                load = load + face_low[p]
            if x == extent_x - 1:
                load = load + face_high[p]
            begin = load[:8] + jnp.where(place == 0, side_low[p, x : x + 1, :], 0.0)
            end = load[extent_y - 8 :] + jnp.where(place == 7, side_high[p, x : x + 1, :], 0.0)
            load = jnp.concatenate([begin, load[8 : extent_y - 8], end] if extent_y > 16 else [begin, end], axis=0)
            speed = vel_ref[p, x] + step_mass * load
            new_vel_ref[p, x] = speed
            new_disp_ref[p, x] = disp_ref[p, x] + TIME_STEP * speed
    if not last:
        store_messages(flag_ref, new_disp_ref, base_ref, node_ref, hot_ref[...], *messages)


def per_device(displacement, velocity, moduli, nodal_mass, segment_node, segment_base, contact_bin, element_tile):
    shape = displacement.shape
    _, extent_x, extent_y, extent_z = shape
    steps = contact_bin.shape[0]
    segments = segment_node.shape[0]
    blocks = segments // SEG
    bin_count = lax.axis_size("bin")
    bin_at = lax.axis_index("bin")
    dom_at, dom_count = lax.axis_index("dom"), lax.axis_size("dom")
    own_device = dom_at * bin_count + bin_at
    checks = (bin_at > 0, bin_at < bin_count - 1, dom_at > 0, dom_at < dom_count - 1, (dom_at & 1) == 1)
    flags = jnp.stack([check.astype(F32) for check in checks + (own_device,)])
    node = segment_node.reshape(blocks, SEG)
    bins = contact_bin[:, :, 0]
    rows = 3 * extent_x
    struct = lambda *dims: jax.ShapeDtypeStruct(dims, F32)
    full = lambda *dims: pl.BlockSpec(dims, lambda i: (0,) * len(dims))
    sent = lambda moduli_too, bins_too: [
        struct((3 + 2 * moduli_too) * extent_y, extent_z),
        struct((3 + 2 * moduli_too) * extent_y, extent_z),
        struct((3 + 2 * moduli_too) * extent_x, extent_z),
        struct(rows, extent_z),
        struct(rows + 8 * bins_too, SEG),
    ]

    first_outs = sent(1, 1) + [jax.ShapeDtypeStruct((extent_z, segments), BF16)]
    first_args = (flags, displacement, segment_base, node, moduli, moduli, bins)
    first_specs = [SCALARS] + [full(*v.shape) for v in first_args[1:]]
    first_specs[4] = pl.BlockSpec((2, extent_x, 8, extent_z), lambda i: (0, 0, extent_y // 8 - 1, 0))
    first_specs[5] = pl.BlockSpec((2, 1, extent_y, extent_z), lambda i: (0, extent_x - 1, 0, 0))
    to_even, to_odd, up, down, far, hot = pl.pallas_call(
        first_body,
        grid=(1,),
        out_shape=first_outs,
        in_specs=first_specs,
        out_specs=[full(*v.shape) for v in first_outs],
        compiler_params=pltpu.CompilerParams(vmem_limit_bytes=60 * 1024 * 1024),
        cost_estimate=pl.CostEstimate(flops=1_000, bytes_accessed=1_000, transcendentals=0),
    )(*first_args)
    (turned,) = call(
        functools.partial(turn_body, extent_z),
        [jax.ShapeDtypeStruct((segments, extent_z), BF16)],
        specs=[WHOLE],
    )(node)
    (tile_places,) = call(
        tile_body, [jax.ShapeDtypeStruct((8, segments), jnp.int32)], specs=[SCALARS] + [WHOLE] * 3
    )(flags, element_tile, node, hot)
    heat = jnp.zeros((blocks, SEG), F32)
    rim = moduli
    for step in range(steps):
        relay = swapped(to_odd, "dom")
        lower_points, upper_points = cycled(far, "bin", 1), cycled(far, "bin", -1)
        others = jnp.stack([cycled(far, "bin", shift) for shift in range(2, bin_count - 1)])
        first, last = step == 0, step == steps - 1
        (inner,) = call(
            inner_body,
            [struct(*shape)],
            [pltpu.VMEM((extent_x, 9, extent_y, extent_z), F32), pltpu.VMEM((extent_x + 1, 6, extent_y, extent_z), F32)],
            [WHOLE] * 2,
        )(displacement, moduli)
        if first:
            of_bins = [far[rows : rows + steps, :blocks]]
            of_bins += [v[rows : rows + steps, :blocks] for v in (lower_points, upper_points, *others)]
            all_bins = jnp.concatenate(of_bins, axis=1).astype(jnp.int32)
        relay, to_even, inner, lower_points, upper_points, others = lax.optimization_barrier(
            (relay, to_even, inner, lower_points, upper_points, others)
        )
        of_odd = relayed(relay, "dom")
        of_even = swapped(to_even, "dom")
        near_blocks = 3 * blocks
        far_blocks = blocks * (bin_count - 3)
        pair_scratch = lambda count: [
            pltpu.VMEM((count + 1, 3, SEG, SEG), F32),
            pltpu.SMEM((bin_count * (count + 2),), jnp.int32),
        ]
        (sums,) = call(
            functools.partial(near_body, bin_count),
            [struct(blocks, 4, 8, SEG)],
            pair_scratch(near_blocks),
            [SCALARS] + [WHOLE] * 3 + [pl.BlockSpec(memory_space=pl.ANY)],
        )(all_bins[step], far, lower_points, upper_points, others)
        sums, of_even, of_odd = lax.optimization_barrier((sums, of_even, of_odd))
        column_rows = rows + 8 + (2 * extent_x if first else 0)
        column_up, column_down = call(
            functools.partial(column_body, first, extent_y),
            [struct(column_rows, extent_z), struct(rows + 8, extent_z)],
            (),
            [SCALARS] + [WHOLE] * 4 + [pl.BlockSpec(memory_space=pl.ANY)],
        )(flags, up, down, of_even, of_odd, sums)
        lower = cycled(column_up, "bin", 1)
        upper = cycled(column_down, "bin", -1)
        pair_args = [all_bins[step], far, others, sums, node, turned, heat]
        if last:
            pair_args += [tile_places, flags]
        contact, heat = call(
            functools.partial(rest_body, bin_count, last),
            [struct(3 * extent_x * extent_y, extent_z), struct(8, TILE_DEV) if last else struct(blocks, SEG)],
            pair_scratch(far_blocks) + [pltpu.VMEM((8, segments), F32)],
            [SCALARS] + [WHOLE] * (len(pair_args) - 2) + [SCALARS if last else WHOLE],
        )(*pair_args)
        if last:
            heat, lower, upper = lax.optimization_barrier((heat, lower, upper))
        update_args = [flags, displacement, velocity, nodal_mass, inner, contact, up, down, lower, upper]
        update_args += [of_even, of_odd, rim]
        update_outs = [struct(*shape), struct(*shape)]
        if not last:
            update_args += [segment_base, node, hot]
            update_outs += sent(0, 0)
        if first:
            update_outs.append(struct(8, extent_y, extent_z))
        made = call(
            functools.partial(update_body, first, last),
            update_outs,
            [pltpu.VMEM((3, extent_x, extent_z), F32)] * 2 + [pltpu.VMEM((3, extent_y, extent_z), F32)] * 2,
            [SCALARS] + [WHOLE] * (len(update_args) - 1),
        )(*update_args)
        displacement, velocity = made[:2]
        if not last:
            to_even, to_odd, up, down, far = made[2:7]
        if first:
            rim = made[-1]
    got = swapped(heat[1:3], "dom")
    passed = relayed(got[1], "dom")
    tile_heat = heat[0] + got[0] + passed
    return displacement, velocity, tile_heat


def solution(mesh):
    placed = (
        P(None, "dom", "bin", None),
        P(None, "dom", "bin", None),
        P(None, "dom", "bin", None),
        P("dom", "bin", None),
        P(("dom", "bin")),
        P(None, ("dom", "bin")),
        P(None, ("dom", "bin"), None),
        P("dom", "bin", None),
    )
    return jax.shard_map(
        per_device,
        mesh=mesh,
        in_specs=placed,
        out_specs=(P(None, "dom", "bin", None), P(None, "dom", "bin", None), P(("dom", "bin"))),
        check_vma=False,
    )
```

```python
import functools
import jax
import jax.numpy as jnp
from jax import lax
from jax.experimental import pallas as pl
from jax.experimental.pallas import tpu as pltpu
from jax.sharding import PartitionSpec as P

SEG = 128
TILE_DEV = 256
RADIUS = 0.09
PENALTY = 4.0
SHORT_GAIN = 100.0
TIME_STEP = 0.2
VMEM_BYTES = 40 * 1024 * 1024
F32 = jnp.float32
BF16 = jnp.bfloat16
WHOLE = pl.BlockSpec(memory_space=pltpu.VMEM)
SCALARS = pl.BlockSpec(memory_space=pltpu.SMEM)
NT = (((1,), (1,)), ((), ()))


def swapped(value, axis):
    count = lax.axis_size(axis)
    return lax.ppermute(value, axis, [(i, i ^ 1) for i in range(count)])


def relayed(value, axis):
    count = lax.axis_size(axis)
    target = [i + 2 if i % 2 == 0 else i - 2 for i in range(count)]
    target[count - 2], target[1] = count - 1, 0
    return lax.ppermute(value, axis, list(enumerate(target)))


def cycled(value, axis, steps):
    count = lax.axis_size(axis)
    return lax.ppermute(value, axis, [(source, (source + steps) % count) for source in range(count)])


def call(body, outs, scratch=(), specs=None):
    return functools.partial(
        pl.pallas_call,
        body,
        out_shape=outs,
        out_specs=[WHOLE] * len(outs),
        scratch_shapes=list(scratch),
        compiler_params=pltpu.CompilerParams(vmem_limit_bytes=VMEM_BYTES),
        cost_estimate=pl.CostEstimate(flops=1_000, bytes_accessed=1_000, transcendentals=0),
    )(in_specs=specs)


def split_two(value):
    high = value.astype(BF16)
    return high, (value - high.astype(F32)).astype(BF16)


def node_split(node_ref, extent_z):
    node = jnp.concatenate([node_ref[j : j + 1, :] for j in range(node_ref.shape[0])], axis=1)
    return lax.div(node, jnp.int32(extent_z)), lax.rem(node, jnp.int32(extent_z))


def one_hot_z(column, extent_z):
    depth = lax.broadcasted_iota(jnp.int32, (extent_z, column.shape[1]), 0)
    return jnp.where(depth == column, 1.0, 0.0).astype(BF16)


def gather_nodes(pieces, row, hot):
    rows = pieces[0].shape[0]
    picked = sum(jnp.dot(piece, hot, preferred_element_type=F32) for piece in pieces)
    at_row = lax.broadcasted_iota(jnp.int32, (rows, row.shape[1]), 0) == row
    return jnp.sum(jnp.where(at_row, picked, 0.0), axis=0, keepdims=True)


def store_positions(disp_ref, base_ref, node_ref, hot, targets):
    extent_x, extent_y, extent_z = disp_ref.shape[1:]
    rows = extent_x * extent_y
    blocks = node_ref.shape[0]
    row, _ = node_split(node_ref, extent_z)
    for p in range(3):
        plane = disp_ref[p].reshape(rows, extent_z)
        points = base_ref[p : p + 1, :] + gather_nodes(split_two(plane), row, hot)
        tile = jnp.concatenate([points[:, j * SEG : (j + 1) * SEG] for j in range(blocks)], axis=0)
        for ref, lane in targets:
            ref[p * blocks : (p + 1) * blocks, lane : lane + SEG] = tile


def store_column(source_ref, at, target_ref, first):
    count, extent_x, _, extent_z = source_ref.shape
    for p in range(count):
        tile = jnp.concatenate([source_ref[p, x, at : at + 1, :] for x in range(extent_x)], axis=0)
        target_ref[first + p * extent_x : first + (p + 1) * extent_x, 0:extent_z] = tile


def store_messages(disp_ref, base_ref, node_ref, hot, up_ref, down_ref, far_ref):
    extent_y, extent_z = disp_ref.shape[2:]
    store_column(disp_ref, extent_y - 1, up_ref, 0)
    store_column(disp_ref, 0, down_ref, 0)
    store_positions(disp_ref, base_ref, node_ref, hot, [(up_ref, extent_z), (down_ref, extent_z), (far_ref, 0)])


def first_body(_, disp_ref, base_ref, node_ref, moduli_ref, bins_ref, up_ref, down_ref, far_ref, hot_ref):
    _, extent_x, extent_y, extent_z = disp_ref.shape
    _, column = node_split(node_ref, extent_z)
    hot_ref[...] = one_hot_z(column, extent_z)
    store_messages(disp_ref, base_ref, node_ref, hot_ref[...], up_ref, down_ref, far_ref)
    rows = 3 * extent_x
    store_column(moduli_ref, moduli_ref.shape[2] - 1, up_ref, rows)
    steps, blocks = bins_ref.shape
    bins = bins_ref[...].astype(F32)
    zeros = jnp.zeros((8, SEG), F32)
    up_ref[rows + 8 : rows + 16, extent_z:] = zeros
    down_ref[rows : rows + 8, 0:extent_z] = jnp.zeros((8, extent_z), F32)
    for ref, lane in ((up_ref, extent_z), (down_ref, extent_z), (far_ref, 0)):
        ref[rows : rows + 8, lane : lane + SEG] = zeros
        ref[rows : rows + steps, lane : lane + blocks] = bins


def layer_body(with_moduli, *refs):
    flag_ref, first_ref, last_ref, lower_ref, upper_ref = refs[:5]
    if with_moduli:
        moduli_ref, even_ref, odd_ref = refs[7:]
    else:
        even_ref, odd_ref = refs[7:]
    extent_y, extent_z = first_ref.shape[2:]
    main = 3 * extent_y
    extent_x = lower_ref.shape[0] // (5 if with_moduli else 3)
    has_lower, has_upper, is_odd = flag_ref[0], flag_ref[1], flag_ref[4] > 0.5
    for p in range(3):
        low, high = first_ref[p, 0], last_ref[p, 0]
        even_ref[p * extent_y : (p + 1) * extent_y, :] = jnp.where(is_odd, low, high)
        odd_ref[p * extent_y : (p + 1) * extent_y, :] = jnp.where(is_odd, high, low)
    edges = []
    for x in (0, extent_x - 1):
        at = [p * extent_x + x for p in range(3)]
        above = [upper_ref[i : i + 1, 0:extent_z] * has_upper for i in at]
        below = [lower_ref[i : i + 1, 0:extent_z] * has_lower for i in at]
        if with_moduli:
            at = [(3 + m) * extent_x + x for m in range(2)]
            rest = [lower_ref[i : i + 1, 0:extent_z] * has_lower for i in at]
        else:
            rest = [jnp.zeros((2, extent_z), F32)]
        edges.append(jnp.concatenate(above + below + rest, axis=0))
    even_ref[main : main + 8, :] = jnp.where(is_odd, edges[0], edges[1])
    odd_ref[main : main + 8, :] = jnp.where(is_odd, edges[1], edges[0])
    if with_moduli:
        for m in range(2):
            for target_ref in (even_ref, odd_ref):
                target_ref[main + 8 + m * extent_y : main + 8 + (m + 1) * extent_y, :] = moduli_ref[m, 0]


def pair_sums(bins_ref, own_ref, sources, begin, bin_count, sums_of, store, spread, listed):
    rows = own_ref.shape[0] // 24 * 24
    blocks = rows // 3
    total_blocks = sum(len(taken) for _, taken in sources)
    stride = total_blocks + 2
    counts = [jnp.int32(0)] * bin_count
    for i in range(total_blocks):
        named = bins_ref[begin + i]
        taken = counts[0]
        for b in range(1, bin_count):
            taken = jnp.where(named == b, counts[b], taken)
        listed[named * stride + taken] = i
        counts = [count + (named == b).astype(jnp.int32) for b, count in enumerate(counts)]
    for b in range(bin_count):
        listed[b * stride + counts[b]] = total_blocks
    spread[total_blocks] = jnp.full((3, SEG, SEG), 1000.0, F32)
    filled = 0
    for source, taken in sources:
        turned = source.T
        for i, j in enumerate(taken):
            for p in range(3):
                at = p * blocks + j
                spread[filled + i, p] = jnp.broadcast_to(turned[:, at : at + 1], (SEG, SEG))
        filled += len(taken)
    for j in range(blocks):
        named = bins_ref[j]
        count = counts[0]
        for b in range(1, bin_count):
            count = jnp.where(named == b, counts[b], count)
        point = [jnp.broadcast_to(own_ref[p * blocks + j : p * blocks + j + 1, :], (8, SEG)) for p in range(3)]

        def against(i, sums):
            sums = list(sums)
            others = [listed[named * stride + 2 * i + half] for half in range(2)]
            for other, g in [(other, g) for other in others for g in range(SEG // 8)]:
                delta = [point[p] - spread[other, p, g * 8 : (g + 1) * 8, :] for p in range(3)]
                square = delta[0] * delta[0] + delta[1] * delta[1] + delta[2] * delta[2]
                inverse = lax.rsqrt(jnp.maximum(square, 1e-30))
                pressure = jnp.maximum(RADIUS - square * inverse, 0.0)
                factor = pressure * jnp.minimum(inverse, 1.0 / (0.25 * RADIUS))
                for p in range(3):
                    sums[p] = sums[p] + factor * delta[p]
                sums[3] = sums[3] + pressure * pressure
            return tuple(sums)

        store(j, lax.fori_loop(0, (count + 1) // 2, against, sums_of(j)))


def upper_share(blocks):
    return blocks * 3 // 8


def near_body(bin_count, bins_ref, own_ref, lower_ref, upper_ref, _, sums_ref, spread, listed):
    rows = own_ref.shape[0] // 24 * 24
    blocks = rows // 3
    extent_z = lower_ref.shape[1] - SEG

    def store(j, sums):
        for q in range(4):
            sums_ref[j, q] = sums[q]

    sources = [(own_ref[0:rows, :], range(blocks)), (lower_ref[0:rows, extent_z:], range(blocks))]
    sources.append((upper_ref[0:rows, extent_z:], range(upper_share(blocks))))
    zero = (jnp.zeros((8, SEG), F32),) * 4
    pair_sums(bins_ref, own_ref, sources, 0, bin_count, lambda j: zero, store, spread, listed)


def rest_body(bin_count, last, *refs):
    bins_ref, own_ref, upper_ref, far_ref, sums_ref, node_ref, hot_ref, heat_ref = refs[:8]
    if last:
        tile_ref, flag_ref, contact_ref, partial_ref, spread, listed, push = refs[8:]
    else:
        contact_ref, total_ref, spread, listed, push = refs[8:]
    extent_z = contact_ref.shape[1]
    rows = contact_ref.shape[0] // 3
    point_rows = own_ref.shape[0] // 24 * 24
    blocks = node_ref.shape[0]
    heats = []

    def store(j, sums):
        for p in range(3):
            push[p : p + 1, j * SEG : (j + 1) * SEG] = PENALTY * jnp.sum(sums[p], axis=0, keepdims=True)
        heats.append(SHORT_GAIN * jnp.sum(sums[3], axis=0, keepdims=True))

    share = upper_share(blocks)
    sources = [(upper_ref[0:point_rows, extent_z:], range(share, blocks))]
    sources += [(far_ref[i, 0:point_rows, :], range(blocks)) for i in range(far_ref.shape[0])]
    sums_of = lambda j: tuple(sums_ref[j, q] for q in range(4))
    pair_sums(bins_ref, own_ref, sources, 2 * blocks + share, bin_count, sums_of, store, spread, listed)
    row, _ = node_split(node_ref, extent_z)
    at_row = lax.broadcasted_iota(jnp.int32, (rows, row.shape[1]), 0) == row
    for p in range(3):
        placed = jnp.where(at_row, push[p : p + 1, :], 0.0)
        contact_ref[p * rows : (p + 1) * rows, :] = sum(
            jnp.dot(piece, hot_ref[...], preferred_element_type=F32) for piece in split_two(placed)
        )
    total = heat_ref[...] + jnp.concatenate(heats, axis=0)
    if not last:
        total_ref[...] = total
        return
    flat = jnp.concatenate([total[j : j + 1, :] for j in range(blocks)], axis=1)
    side, slot = tile_ref[0:1, :], tile_ref[1:2, :]
    hot_slot = one_hot_z(slot, TILE_DEV)
    at_side = lax.broadcasted_iota(jnp.int32, (8, flat.shape[1]), 0) == side
    placed = jnp.where(at_side, flat, 0.0)
    high, low = split_two(placed)
    lowest = (placed - high.astype(F32) - low.astype(F32)).astype(BF16)
    made = sum(lax.dot_general(piece, hot_slot, NT, preferred_element_type=F32) for piece in (high, low, lowest))
    is_odd = flag_ref[4] > 0.5
    to_even = jnp.where(is_odd, made[0:1], made[2:3])
    to_odd = jnp.where(is_odd, made[2:3], made[0:1])
    partial_ref[...] = jnp.concatenate([made[1:2], to_even, to_odd, made[3:]], axis=0)


def turn_body(extent_z, node_ref, out_ref):
    node = node_ref[...]
    column = lax.rem(node, jnp.int32(extent_z)).astype(F32).T
    lane = lax.broadcasted_iota(jnp.int32, (SEG, extent_z), 1).astype(F32)
    for j in range(node.shape[0]):
        out_ref[j * SEG : (j + 1) * SEG, :] = jnp.where(lane == column[:, j : j + 1], 1.0, 0.0).astype(BF16)


def tile_body(own_ref, tiles_ref, node_ref, hot_ref, out_ref):
    extent_x, extent_y, extent_z = tiles_ref.shape
    row, _ = node_split(node_ref, extent_z)
    hot = hot_ref[...]
    tiles = tiles_ref[...].reshape(extent_x * extent_y, extent_z)
    device = lax.div(tiles, jnp.int32(TILE_DEV))
    slot = tiles - device * TILE_DEV
    offset = (device.astype(F32) - own_ref[5]).astype(BF16)
    found = gather_nodes([offset], row, hot)
    side = jnp.where(found < -0.5, 0, jnp.where(found > 0.5, 2, 1))
    found_slot = gather_nodes([slot.astype(F32).astype(BF16)], row, hot).astype(jnp.int32)
    rest = jnp.zeros((6, row.shape[1]), jnp.int32)
    out_ref[...] = jnp.concatenate([side, found_slot, rest], axis=0)


WHICH = ((0, 3, 4), (3, 1, 5), (4, 5, 2))
SCALE = -1.0 / 16.0


def ahead_z(value):
    return pltpu.roll(value, value.shape[1] - 1, 1)


def behind_z(value):
    return pltpu.roll(value, 1, 1)


def ahead_row(value):
    return pltpu.roll(value, value.shape[0] - 1, 0)


def behind_row(value):
    return pltpu.roll(value, 1, 0)


def features(near, far):
    total, change = near + far, far - near
    total_z = ahead_z(total)
    return total + total_z, change + ahead_z(change), total_z - total


def stress_of(along_x, along_y, along_z, volume_modulus, shear):
    volume = volume_modulus * (along_x[0] + along_y[1] + along_z[2])
    twice = shear + shear
    return (
        twice * along_x[0] + volume,
        twice * along_y[1] + volume,
        twice * along_z[2] + volume,
        shear * (along_y[0] + along_x[1]),
        shear * (along_z[0] + along_x[2]),
        shear * (along_z[1] + along_y[2]),
    )


def spread_z(plain, slope):
    return (plain - slope) + behind_z(plain + slope)


def inner_body(disp_ref, moduli_ref, out_ref, feature, stress):
    _, extent_x, extent_y, extent_z = disp_ref.shape

    def fill(x, carry):
        for p in range(3):
            value = disp_ref[p, x]
            for q, part in enumerate(features(value, ahead_row(value))):
                feature[x, 3 * q + p] = part
        return carry

    lax.fori_loop(0, extent_x, fill, 0)
    for c in range(6):
        stress[0, c] = jnp.zeros((extent_y, extent_z), F32)
        stress[extent_x, c] = jnp.zeros((extent_y, extent_z), F32)
    place = lax.broadcasted_iota(jnp.int32, (8, extent_z), 0)

    def load(x, carry):
        for t in range(extent_y // 8):
            rows = slice(t * 8, t * 8 + 8)
            scale = jnp.where(place == 7, 0.0, SCALE) if t == extent_y // 8 - 1 else SCALE
            along_x = [feature[x + 1, p, rows] - feature[x, p, rows] for p in range(3)]
            along_y = [feature[x + 1, 3 + p, rows] + feature[x, 3 + p, rows] for p in range(3)]
            along_z = [feature[x + 1, 6 + p, rows] + feature[x, 6 + p, rows] for p in range(3)]
            found = stress_of(along_x, along_y, along_z, moduli_ref[0, x, rows] * scale, moduli_ref[1, x, rows] * scale)
            for c in range(6):
                stress[x + 1, c, rows] = found[c]
        return carry

    lax.fori_loop(0, extent_x - 1, load, 0)

    def force(x, carry):
        for p in range(3):
            of_x, of_y, of_z = WHICH[p]
            part_x = stress[x, of_x] - stress[x + 1, of_x]
            part_y = stress[x, of_y] + stress[x + 1, of_y]
            part_z = stress[x, of_z] + stress[x + 1, of_z]
            plain = (part_x - part_y) + behind_row(part_x + part_y)
            out_ref[p, x] = spread_z(plain, part_z + behind_row(part_z))
        return carry

    lax.fori_loop(0, extent_x, force, 0)


def update_body(first, last, *refs):
    refs = list(refs)
    take = lambda count: [refs.pop(0) for _ in range(count)]
    flag_ref, disp_ref, vel_ref, mass_ref, inner_ref, contact_ref = take(6)
    own_up_ref, own_down_ref, lower_ref, upper_ref, even_ref, odd_ref, rim_ref = take(7)
    if not last:
        base_ref, node_ref, hot_ref = take(3)
    new_disp_ref, new_vel_ref = take(2)
    if not last:
        up_ref, down_ref, far_ref = take(3)
    if first:
        moduli_ref, rim_ref = rim_ref, take(1)[0]
    (side_low, side_high, face_low, face_high) = take(4)
    _, extent_x, extent_y, extent_z = disp_ref.shape
    has_lower, has_upper, has_back, has_front = [flag_ref[i] for i in range(4)]
    is_odd = flag_ref[4] > 0.5
    place = lax.broadcasted_iota(jnp.int32, (8, extent_z), 0)
    all_but_last = lax.broadcasted_iota(jnp.int32, (extent_y, extent_z), 0) < extent_y - 1
    main = 3 * extent_y

    def back(begin, count):
        rows = slice(begin, begin + count)
        return jnp.where(is_odd, even_ref[rows, :], odd_ref[rows, :]) * has_back

    def front(begin, count):
        rows = slice(begin, begin + count)
        return jnp.where(is_odd, odd_ref[rows, :], even_ref[rows, :]) * has_front

    def ring(tile, above, below):
        return jnp.concatenate([tile, jnp.where(place == 0, above, jnp.where(place == 7, below, 0.0))], axis=0)

    if first:
        for m in range(2):
            at = slice((3 + m) * extent_x, (4 + m) * extent_x)
            begin = main + 8 + m * extent_y
            of_back = back(begin, extent_y)
            high = ring(own_up_ref[at, 0:extent_z], 0.0, of_back[extent_y - 1 :])
            low = ring(lower_ref[at, 0:extent_z] * has_lower, 0.0, back(main + 6 + m, 1))
            rim_ref[m] = high * SCALE
            rim_ref[2 + m] = low * SCALE
            rim_ref[4 + m] = jnp.where(all_but_last, of_back * SCALE, 0.0)
            rim_ref[6 + m] = jnp.where(all_but_last, moduli_ref[m, extent_x - 1] * SCALE, 0.0)

    def rows_of(tile_ref, weight, row, extra):
        made = []
        for p in range(3):
            at = main + extra + p if row is None else p * extent_y + row
            tile = tile_ref[p * extent_x : (p + 1) * extent_x, 0:extent_z]
            tile = tile if weight is None else tile * weight
            made.append(ring(tile, front(at, 1), back(at, 1)))
        return made

    def side(near, far, at, sign, target):
        parts = [features(near[p], far[p]) for p in range(3)]
        along_x = [ahead_row(parts[p][0]) - parts[p][0] for p in range(3)]
        along_y = [ahead_row(parts[p][1]) + parts[p][1] for p in range(3)]
        along_z = [ahead_row(parts[p][2]) + parts[p][2] for p in range(3)]
        found = stress_of(along_x, along_y, along_z, rim_ref[at], rim_ref[at + 1])
        for p in range(3):
            of_x, of_y, of_z = [found[c] for c in WHICH[p]]
            part_x = (behind_row(of_x) - of_x)[:extent_x]
            part_y = (behind_row(of_y) + of_y)[:extent_x]
            part_z = (behind_row(of_z) + of_z)[:extent_x]
            target[p] = spread_z(part_x + sign * part_y, part_z)

    side(rows_of(own_up_ref, None, extent_y - 1, 0), rows_of(upper_ref, has_upper, None, 0), 0, -1.0, side_high)
    side(rows_of(lower_ref, has_lower, None, 3), rows_of(own_down_ref, None, 0, 0), 2, 1.0, side_low)

    def face(near, far, at, sign, target):
        parts_near = [features(value, ahead_row(value)) for value in near]
        parts_far = [features(value, ahead_row(value)) for value in far]
        along_x = [parts_far[p][0] - parts_near[p][0] for p in range(3)]
        along_y = [parts_far[p][1] + parts_near[p][1] for p in range(3)]
        along_z = [parts_far[p][2] + parts_near[p][2] for p in range(3)]
        found = stress_of(along_x, along_y, along_z, rim_ref[at], rim_ref[at + 1])
        for p in range(3):
            of_x, of_y, of_z = [found[c] for c in WHICH[p]]
            of_x = of_x * sign
            plain = (of_x - of_y) + behind_row(of_x + of_y)
            target[p] = spread_z(plain, of_z + behind_row(of_z))

    layer_of = lambda side_of: [side_of(p * extent_y, extent_y) for p in range(3)]
    own_layer = lambda x: [disp_ref[p, x] for p in range(3)]
    face(layer_of(back), own_layer(0), 4, 1.0, face_low)
    face(own_layer(extent_x - 1), layer_of(front), 6, -1.0, face_high)

    for x in range(extent_x):
        step_mass = TIME_STEP / mass_ref[x]
        for p in range(3):
            at = (p * extent_x + x) * extent_y
            load = inner_ref[p, x] + contact_ref[at : at + extent_y, :]
            if x == 0:
                load = load + face_low[p]
            if x == extent_x - 1:
                load = load + face_high[p]
            begin = load[:8] + jnp.where(place == 0, side_low[p, x : x + 1, :], 0.0)
            end = load[extent_y - 8 :] + jnp.where(place == 7, side_high[p, x : x + 1, :], 0.0)
            load = jnp.concatenate([begin, load[8 : extent_y - 8], end] if extent_y > 16 else [begin, end], axis=0)
            speed = vel_ref[p, x] + step_mass * load
            new_vel_ref[p, x] = speed
            new_disp_ref[p, x] = disp_ref[p, x] + TIME_STEP * speed
    if not last:
        store_messages(new_disp_ref, base_ref, node_ref, hot_ref[...], up_ref, down_ref, far_ref)


def per_device(displacement, velocity, moduli, nodal_mass, segment_node, segment_base, contact_bin, element_tile):
    shape = displacement.shape
    _, extent_x, extent_y, extent_z = shape
    steps = contact_bin.shape[0]
    segments = segment_node.shape[0]
    blocks = segments // SEG
    bin_count = lax.axis_size("bin")
    bin_at = lax.axis_index("bin")
    dom_at, dom_count = lax.axis_index("dom"), lax.axis_size("dom")
    own_device = dom_at * bin_count + bin_at
    checks = (bin_at > 0, bin_at < bin_count - 1, dom_at > 0, dom_at < dom_count - 1, (dom_at & 1) == 1)
    flags = jnp.concatenate([jnp.stack(checks).astype(F32), own_device[None].astype(F32)])
    node = segment_node.reshape(blocks, SEG)
    bins = contact_bin[:, :, 0]
    rows = 3 * extent_x
    wide = extent_z + SEG
    struct = lambda *dims: jax.ShapeDtypeStruct(dims, F32)
    layer_rows = 3 * extent_y + 8
    full = lambda *dims: pl.BlockSpec(dims, lambda i: (0,) * len(dims))

    first_outs = [
        struct(rows + 16, wide),
        struct(rows + 8, wide),
        struct(rows + 8, SEG),
        jax.ShapeDtypeStruct((extent_z, segments), BF16),
    ]
    first_args = (flags, displacement, segment_base, node, moduli, bins)
    first_specs = [SCALARS] + [full(*v.shape) for v in first_args[1:]]
    first_specs[4] = pl.BlockSpec((2, extent_x, 8, extent_z), lambda i: (0, 0, extent_y // 8 - 1, 0))
    up, down, far, hot = pl.pallas_call(
        first_body,
        grid=(1,),
        out_shape=first_outs,
        in_specs=first_specs,
        out_specs=[full(*v.shape) for v in first_outs],
        compiler_params=pltpu.CompilerParams(vmem_limit_bytes=60 * 1024 * 1024),
        cost_estimate=pl.CostEstimate(flops=1_000, bytes_accessed=1_000, transcendentals=0),
    )(*first_args)
    (turned,) = call(
        functools.partial(turn_body, extent_z),
        [jax.ShapeDtypeStruct((segments, extent_z), BF16)],
        specs=[WHOLE],
    )(node)
    (tile_places,) = call(
        tile_body, [jax.ShapeDtypeStruct((8, segments), jnp.int32)], specs=[SCALARS] + [WHOLE] * 3
    )(flags, element_tile, node, hot)
    heat = jnp.zeros((blocks, SEG), F32)
    rim = moduli
    for step in range(steps):
        lower = cycled(up, "bin", 1)
        upper = cycled(down, "bin", -1)
        others = jnp.stack([cycled(far, "bin", shift) for shift in range(2, bin_count - 1)])
        first, last = step == 0, step == steps - 1
        (inner,) = call(
            inner_body,
            [struct(*shape)],
            [pltpu.VMEM((extent_x, 9, extent_y, extent_z), F32), pltpu.VMEM((extent_x + 1, 6, extent_y, extent_z), F32)],
            [WHOLE] * 2,
        )(displacement, moduli)
        if first:
            of_bins = [far[rows : rows + steps, :blocks]]
            of_bins += [v[rows : rows + steps, extent_z : extent_z + blocks] for v in (lower, upper)]
            of_bins += [v[rows : rows + steps, :blocks] for v in others]
            all_bins = jnp.concatenate(of_bins, axis=1).astype(jnp.int32)
        layer = lambda at, count=3: pl.BlockSpec((count, 1, extent_y, extent_z), lambda i: (0, at, 0, 0))
        send_rows = layer_rows + (2 * extent_y if first else 0)
        layer_args = [flags, displacement, displacement, lower, upper, inner, others]
        layer_specs = [SCALARS, layer(0), layer(extent_x - 1), full(*lower.shape), full(*upper.shape)]
        layer_specs += [pl.BlockSpec(memory_space=pl.ANY)] * 2
        if first:
            layer_args.append(moduli)
            layer_specs.append(layer(extent_x - 1, 2))
        to_even, to_odd = pl.pallas_call(
            functools.partial(layer_body, first),
            grid=(1,),
            out_shape=[struct(send_rows, extent_z)] * 2,
            in_specs=layer_specs,
            out_specs=[full(send_rows, extent_z)] * 2,
            compiler_params=pltpu.CompilerParams(vmem_limit_bytes=VMEM_BYTES),
            cost_estimate=pl.CostEstimate(flops=1_000, bytes_accessed=1_000, transcendentals=0),
        )(*layer_args)
        relay = swapped(to_odd, "dom")
        near_blocks = 2 * blocks + upper_share(blocks)
        far_blocks = blocks * bin_count - near_blocks
        pair_scratch = lambda count: [
            pltpu.VMEM((count + 1, 3, SEG, SEG), F32),
            pltpu.SMEM((bin_count * (count + 2),), jnp.int32),
        ]
        (sums,) = call(
            functools.partial(near_body, bin_count),
            [struct(blocks, 4, 8, SEG)],
            pair_scratch(near_blocks),
            [SCALARS] + [WHOLE] * 3 + [pl.BlockSpec(memory_space=pl.ANY)],
        )(all_bins[step], far, lower, upper, to_odd)
        if step == 1:
            tile_places, sums = lax.optimization_barrier((tile_places, sums))
        to_even, sums, relay = lax.optimization_barrier((to_even, sums, relay))
        of_odd = relayed(relay, "dom")
        of_even = swapped(to_even, "dom")
        pair_args = [all_bins[step], far, upper, others, sums, node, turned, heat]
        if last:
            pair_args += [tile_places, flags]
        contact, heat = call(
            functools.partial(rest_body, bin_count, last),
            [struct(3 * extent_x * extent_y, extent_z), struct(8, TILE_DEV) if last else struct(blocks, SEG)],
            pair_scratch(far_blocks) + [pltpu.VMEM((8, segments), F32)],
            [SCALARS] + [WHOLE] * (len(pair_args) - 2) + [SCALARS if last else WHOLE],
        )(*pair_args)
        if last:
            heat, of_even, of_odd = lax.optimization_barrier((heat, of_even, of_odd))
        update_args = [flags, displacement, velocity, nodal_mass, inner, contact, up, down, lower, upper]
        update_args += [of_even, of_odd, rim]
        update_outs = [struct(*shape), struct(*shape)]
        if not last:
            update_args += [segment_base, node, hot]
            update_outs += [struct(rows, wide), struct(rows, wide), struct(rows, SEG)]
        if first:
            update_outs.append(struct(8, extent_y, extent_z))
        made = call(
            functools.partial(update_body, first, last),
            update_outs,
            [pltpu.VMEM((3, extent_x, extent_z), F32)] * 2 + [pltpu.VMEM((3, extent_y, extent_z), F32)] * 2,
            [SCALARS] + [WHOLE] * (len(update_args) - 1),
        )(*update_args)
        displacement, velocity = made[:2]
        if not last:
            up, down, far = made[2:5]
        if first:
            rim = made[-1]
    got = swapped(heat[1:3], "dom")
    passed = relayed(got[1], "dom")
    tile_heat = heat[0] + got[0] + passed
    return displacement, velocity, tile_heat


def solution(mesh):
    placed = (
        P(None, "dom", "bin", None),
        P(None, "dom", "bin", None),
        P(None, "dom", "bin", None),
        P("dom", "bin", None),
        P(("dom", "bin")),
        P(None, ("dom", "bin")),
        P(None, ("dom", "bin"), None),
        P("dom", "bin", None),
    )
    return jax.shard_map(
        per_device,
        mesh=mesh,
        in_specs=placed,
        out_specs=(P(None, "dom", "bin", None), P(None, "dom", "bin", None), P(("dom", "bin"))),
        check_vma=False,
    )
```

```python
import functools
import jax
import jax.numpy as jnp
from jax import lax
from jax.experimental import pallas as pl
from jax.experimental.pallas import tpu as pltpu
from jax.sharding import PartitionSpec as P

SEG = 128
TILE_DEV = 256
RADIUS = 0.09
PENALTY = 4.0
SHORT_GAIN = 100.0
TIME_STEP = 0.2
VMEM_BYTES = 40 * 1024 * 1024
F32 = jnp.float32
BF16 = jnp.bfloat16
WHOLE = pl.BlockSpec(memory_space=pltpu.VMEM)
SCALARS = pl.BlockSpec(memory_space=pltpu.SMEM)
NT = (((1,), (1,)), ((), ()))


def swapped(value, axis):
    count = lax.axis_size(axis)
    return lax.ppermute(value, axis, [(i, i ^ 1) for i in range(count)])


def relayed(value, axis):
    count = lax.axis_size(axis)
    target = [i + 2 if i % 2 == 0 else i - 2 for i in range(count)]
    target[count - 2], target[1] = count - 1, 0
    return lax.ppermute(value, axis, list(enumerate(target)))


def cycled(value, axis, steps):
    count = lax.axis_size(axis)
    return lax.ppermute(value, axis, [(source, (source + steps) % count) for source in range(count)])


def call(body, outs, scratch=(), specs=None):
    return functools.partial(
        pl.pallas_call,
        body,
        out_shape=outs,
        out_specs=[WHOLE] * len(outs),
        scratch_shapes=list(scratch),
        compiler_params=pltpu.CompilerParams(vmem_limit_bytes=VMEM_BYTES),
        cost_estimate=pl.CostEstimate(flops=1_000, bytes_accessed=1_000, transcendentals=0),
    )(in_specs=specs)


def split_two(value):
    high = value.astype(BF16)
    return high, (value - high.astype(F32)).astype(BF16)


def node_split(node_ref, extent_z):
    node = jnp.concatenate([node_ref[j : j + 1, :] for j in range(node_ref.shape[0])], axis=1)
    return lax.div(node, jnp.int32(extent_z)), lax.rem(node, jnp.int32(extent_z))


def one_hot_z(column, extent_z):
    depth = lax.broadcasted_iota(jnp.int32, (extent_z, column.shape[1]), 0)
    return jnp.where(depth == column, 1.0, 0.0).astype(BF16)


def gather_nodes(pieces, row, hot):
    rows = pieces[0].shape[0]
    picked = sum(jnp.dot(piece, hot, preferred_element_type=F32) for piece in pieces)
    at_row = lax.broadcasted_iota(jnp.int32, (rows, row.shape[1]), 0) == row
    return jnp.sum(jnp.where(at_row, picked, 0.0), axis=0, keepdims=True)


def store_positions(disp_ref, base_ref, node_ref, hot, targets):
    extent_x, extent_y, extent_z = disp_ref.shape[1:]
    rows = extent_x * extent_y
    blocks = node_ref.shape[0]
    row, _ = node_split(node_ref, extent_z)
    for p in range(3):
        plane = disp_ref[p].reshape(rows, extent_z)
        points = base_ref[p : p + 1, :] + gather_nodes(split_two(plane), row, hot)
        tile = jnp.concatenate([points[:, j * SEG : (j + 1) * SEG] for j in range(blocks)], axis=0)
        for ref, lane in targets:
            ref[p * blocks : (p + 1) * blocks, lane : lane + SEG] = tile


def store_column(source_ref, at, target_ref, first):
    count, extent_x, _, extent_z = source_ref.shape
    for p in range(count):
        tile = jnp.concatenate([source_ref[p, x, at : at + 1, :] for x in range(extent_x)], axis=0)
        target_ref[first + p * extent_x : first + (p + 1) * extent_x, 0:extent_z] = tile


def store_messages(disp_ref, base_ref, node_ref, hot, up_ref, down_ref, far_ref):
    extent_y, extent_z = disp_ref.shape[2:]
    store_column(disp_ref, extent_y - 1, up_ref, 0)
    store_column(disp_ref, 0, down_ref, 0)
    store_positions(disp_ref, base_ref, node_ref, hot, [(up_ref, extent_z), (down_ref, extent_z), (far_ref, 0)])


def first_body(_, disp_ref, base_ref, node_ref, moduli_ref, bins_ref, up_ref, down_ref, far_ref, hot_ref):
    _, extent_x, extent_y, extent_z = disp_ref.shape
    _, column = node_split(node_ref, extent_z)
    hot_ref[...] = one_hot_z(column, extent_z)
    store_messages(disp_ref, base_ref, node_ref, hot_ref[...], up_ref, down_ref, far_ref)
    rows = 3 * extent_x
    store_column(moduli_ref, moduli_ref.shape[2] - 1, up_ref, rows)
    steps, blocks = bins_ref.shape
    bins = bins_ref[...].astype(F32)
    zeros = jnp.zeros((8, SEG), F32)
    up_ref[rows + 8 : rows + 16, extent_z:] = zeros
    down_ref[rows : rows + 8, 0:extent_z] = jnp.zeros((8, extent_z), F32)
    for ref, lane in ((up_ref, extent_z), (down_ref, extent_z), (far_ref, 0)):
        ref[rows : rows + 8, lane : lane + SEG] = zeros
        ref[rows : rows + steps, lane : lane + blocks] = bins


def layer_body(with_moduli, *refs):
    flag_ref, first_ref, last_ref, lower_ref, upper_ref = refs[:5]
    if with_moduli:
        moduli_ref, even_ref, odd_ref = refs[7:]
    else:
        even_ref, odd_ref = refs[7:]
    extent_y, extent_z = first_ref.shape[2:]
    main = 3 * extent_y
    extent_x = lower_ref.shape[0] // (5 if with_moduli else 3)
    has_lower, has_upper, is_odd = flag_ref[0], flag_ref[1], flag_ref[4] > 0.5
    for p in range(3):
        low, high = first_ref[p, 0], last_ref[p, 0]
        even_ref[p * extent_y : (p + 1) * extent_y, :] = jnp.where(is_odd, low, high)
        odd_ref[p * extent_y : (p + 1) * extent_y, :] = jnp.where(is_odd, high, low)
    edges = []
    for x in (0, extent_x - 1):
        at = [p * extent_x + x for p in range(3)]
        above = [upper_ref[i : i + 1, 0:extent_z] * has_upper for i in at]
        below = [lower_ref[i : i + 1, 0:extent_z] * has_lower for i in at]
        if with_moduli:
            at = [(3 + m) * extent_x + x for m in range(2)]
            rest = [lower_ref[i : i + 1, 0:extent_z] * has_lower for i in at]
        else:
            rest = [jnp.zeros((2, extent_z), F32)]
        edges.append(jnp.concatenate(above + below + rest, axis=0))
    even_ref[main : main + 8, :] = jnp.where(is_odd, edges[0], edges[1])
    odd_ref[main : main + 8, :] = jnp.where(is_odd, edges[1], edges[0])
    if with_moduli:
        for m in range(2):
            for target_ref in (even_ref, odd_ref):
                target_ref[main + 8 + m * extent_y : main + 8 + (m + 1) * extent_y, :] = moduli_ref[m, 0]


def pair_sums(bins_ref, own_ref, sources, begin, bin_count, sums_of, store, spread, listed):
    rows = own_ref.shape[0] // 24 * 24
    blocks = rows // 3
    total_blocks = blocks * len(sources)
    stride = total_blocks + 2
    counts = [jnp.int32(0)] * bin_count
    for i in range(total_blocks):
        named = bins_ref[begin + i]
        taken = counts[0]
        for b in range(1, bin_count):
            taken = jnp.where(named == b, counts[b], taken)
        listed[named * stride + taken] = i
        counts = [count + (named == b).astype(jnp.int32) for b, count in enumerate(counts)]
    for b in range(bin_count):
        listed[b * stride + counts[b]] = total_blocks
    spread[total_blocks] = jnp.full((3, SEG, SEG), 1000.0, F32)
    for d, source in enumerate(sources):
        turned = source.T
        for p in range(3):
            for j in range(blocks):
                at = p * blocks + j
                spread[d * blocks + j, p] = jnp.broadcast_to(turned[:, at : at + 1], (SEG, SEG))
    for j in range(blocks):
        named = bins_ref[j]
        count = counts[0]
        for b in range(1, bin_count):
            count = jnp.where(named == b, counts[b], count)
        point = [jnp.broadcast_to(own_ref[p * blocks + j : p * blocks + j + 1, :], (8, SEG)) for p in range(3)]

        def against(i, sums):
            sums = list(sums)
            others = [listed[named * stride + 2 * i + half] for half in range(2)]
            for other, g in [(other, g) for other in others for g in range(SEG // 8)]:
                delta = [point[p] - spread[other, p, g * 8 : (g + 1) * 8, :] for p in range(3)]
                square = delta[0] * delta[0] + delta[1] * delta[1] + delta[2] * delta[2]
                inverse = lax.rsqrt(jnp.maximum(square, 1e-30))
                pressure = jnp.maximum(RADIUS - square * inverse, 0.0)
                factor = pressure * jnp.minimum(inverse, 1.0 / (0.25 * RADIUS))
                for p in range(3):
                    sums[p] = sums[p] + factor * delta[p]
                sums[3] = sums[3] + pressure * pressure
            return tuple(sums)

        store(j, lax.fori_loop(0, (count + 1) // 2, against, sums_of(j)))


def near_body(bin_count, bins_ref, own_ref, lower_ref, _, sums_ref, spread, listed):
    rows = own_ref.shape[0] // 24 * 24
    extent_z = lower_ref.shape[1] - SEG

    def store(j, sums):
        for q in range(4):
            sums_ref[j, q] = sums[q]

    sources = [own_ref[0:rows, :], lower_ref[0:rows, extent_z:]]
    zero = (jnp.zeros((8, SEG), F32),) * 4
    pair_sums(bins_ref, own_ref, sources, 0, bin_count, lambda j: zero, store, spread, listed)


def rest_body(bin_count, last, *refs):
    bins_ref, own_ref, upper_ref, far_ref, sums_ref, node_ref, hot_ref, heat_ref = refs[:8]
    if last:
        tile_ref, flag_ref, contact_ref, partial_ref, spread, listed, push = refs[8:]
    else:
        contact_ref, total_ref, spread, listed, push = refs[8:]
    extent_z = contact_ref.shape[1]
    rows = contact_ref.shape[0] // 3
    point_rows = own_ref.shape[0] // 24 * 24
    blocks = node_ref.shape[0]
    heats = []

    def store(j, sums):
        for p in range(3):
            push[p : p + 1, j * SEG : (j + 1) * SEG] = PENALTY * jnp.sum(sums[p], axis=0, keepdims=True)
        heats.append(SHORT_GAIN * jnp.sum(sums[3], axis=0, keepdims=True))

    sources = [upper_ref[0:point_rows, extent_z:]] + [far_ref[i, 0:point_rows, :] for i in range(far_ref.shape[0])]
    sums_of = lambda j: tuple(sums_ref[j, q] for q in range(4))
    pair_sums(bins_ref, own_ref, sources, 2 * blocks, bin_count, sums_of, store, spread, listed)
    row, _ = node_split(node_ref, extent_z)
    at_row = lax.broadcasted_iota(jnp.int32, (rows, row.shape[1]), 0) == row
    for p in range(3):
        placed = jnp.where(at_row, push[p : p + 1, :], 0.0)
        contact_ref[p * rows : (p + 1) * rows, :] = sum(
            jnp.dot(piece, hot_ref[...], preferred_element_type=F32) for piece in split_two(placed)
        )
    total = heat_ref[...] + jnp.concatenate(heats, axis=0)
    if not last:
        total_ref[...] = total
        return
    flat = jnp.concatenate([total[j : j + 1, :] for j in range(blocks)], axis=1)
    side, slot = tile_ref[0:1, :], tile_ref[1:2, :]
    hot_slot = one_hot_z(slot, TILE_DEV)
    at_side = lax.broadcasted_iota(jnp.int32, (8, flat.shape[1]), 0) == side
    placed = jnp.where(at_side, flat, 0.0)
    high, low = split_two(placed)
    lowest = (placed - high.astype(F32) - low.astype(F32)).astype(BF16)
    made = sum(lax.dot_general(piece, hot_slot, NT, preferred_element_type=F32) for piece in (high, low, lowest))
    is_odd = flag_ref[4] > 0.5
    to_even = jnp.where(is_odd, made[0:1], made[2:3])
    to_odd = jnp.where(is_odd, made[2:3], made[0:1])
    partial_ref[...] = jnp.concatenate([made[1:2], to_even, to_odd, made[3:]], axis=0)


def turn_body(extent_z, node_ref, out_ref):
    node = node_ref[...]
    column = lax.rem(node, jnp.int32(extent_z)).astype(F32).T
    lane = lax.broadcasted_iota(jnp.int32, (SEG, extent_z), 1).astype(F32)
    for j in range(node.shape[0]):
        out_ref[j * SEG : (j + 1) * SEG, :] = jnp.where(lane == column[:, j : j + 1], 1.0, 0.0).astype(BF16)


def tile_body(own_ref, tiles_ref, node_ref, hot_ref, out_ref):
    extent_x, extent_y, extent_z = tiles_ref.shape
    row, _ = node_split(node_ref, extent_z)
    hot = hot_ref[...]
    tiles = tiles_ref[...].reshape(extent_x * extent_y, extent_z)
    device = lax.div(tiles, jnp.int32(TILE_DEV))
    slot = tiles - device * TILE_DEV
    offset = (device.astype(F32) - own_ref[5]).astype(BF16)
    found = gather_nodes([offset], row, hot)
    side = jnp.where(found < -0.5, 0, jnp.where(found > 0.5, 2, 1))
    found_slot = gather_nodes([slot.astype(F32).astype(BF16)], row, hot).astype(jnp.int32)
    rest = jnp.zeros((6, row.shape[1]), jnp.int32)
    out_ref[...] = jnp.concatenate([side, found_slot, rest], axis=0)


WHICH = ((0, 3, 4), (3, 1, 5), (4, 5, 2))
SCALE = -1.0 / 16.0


def ahead_z(value):
    return pltpu.roll(value, value.shape[1] - 1, 1)


def behind_z(value):
    return pltpu.roll(value, 1, 1)


def ahead_row(value):
    return pltpu.roll(value, value.shape[0] - 1, 0)


def behind_row(value):
    return pltpu.roll(value, 1, 0)


def features(near, far):
    total, change = near + far, far - near
    total_z = ahead_z(total)
    return total + total_z, change + ahead_z(change), total_z - total


def stress_of(along_x, along_y, along_z, volume_modulus, shear):
    volume = volume_modulus * (along_x[0] + along_y[1] + along_z[2])
    twice = shear + shear
    return (
        twice * along_x[0] + volume,
        twice * along_y[1] + volume,
        twice * along_z[2] + volume,
        shear * (along_y[0] + along_x[1]),
        shear * (along_z[0] + along_x[2]),
        shear * (along_z[1] + along_y[2]),
    )


def spread_z(plain, slope):
    return (plain - slope) + behind_z(plain + slope)


def inner_body(disp_ref, moduli_ref, out_ref, feature, stress):
    _, extent_x, extent_y, extent_z = disp_ref.shape

    def fill(x, carry):
        for p in range(3):
            value = disp_ref[p, x]
            for q, part in enumerate(features(value, ahead_row(value))):
                feature[x, 3 * q + p] = part
        return carry

    lax.fori_loop(0, extent_x, fill, 0)
    for c in range(6):
        stress[0, c] = jnp.zeros((extent_y, extent_z), F32)
        stress[extent_x, c] = jnp.zeros((extent_y, extent_z), F32)
    place = lax.broadcasted_iota(jnp.int32, (8, extent_z), 0)

    def load(x, carry):
        for t in range(extent_y // 8):
            rows = slice(t * 8, t * 8 + 8)
            scale = jnp.where(place == 7, 0.0, SCALE) if t == extent_y // 8 - 1 else SCALE
            along_x = [feature[x + 1, p, rows] - feature[x, p, rows] for p in range(3)]
            along_y = [feature[x + 1, 3 + p, rows] + feature[x, 3 + p, rows] for p in range(3)]
            along_z = [feature[x + 1, 6 + p, rows] + feature[x, 6 + p, rows] for p in range(3)]
            found = stress_of(along_x, along_y, along_z, moduli_ref[0, x, rows] * scale, moduli_ref[1, x, rows] * scale)
            for c in range(6):
                stress[x + 1, c, rows] = found[c]
        return carry

    lax.fori_loop(0, extent_x - 1, load, 0)

    def force(x, carry):
        for p in range(3):
            of_x, of_y, of_z = WHICH[p]
            part_x = stress[x, of_x] - stress[x + 1, of_x]
            part_y = stress[x, of_y] + stress[x + 1, of_y]
            part_z = stress[x, of_z] + stress[x + 1, of_z]
            plain = (part_x - part_y) + behind_row(part_x + part_y)
            out_ref[p, x] = spread_z(plain, part_z + behind_row(part_z))
        return carry

    lax.fori_loop(0, extent_x, force, 0)


def update_body(first, last, *refs):
    refs = list(refs)
    take = lambda count: [refs.pop(0) for _ in range(count)]
    flag_ref, disp_ref, vel_ref, mass_ref, inner_ref, contact_ref = take(6)
    own_up_ref, own_down_ref, lower_ref, upper_ref, even_ref, odd_ref, rim_ref = take(7)
    if not last:
        base_ref, node_ref, hot_ref = take(3)
    new_disp_ref, new_vel_ref = take(2)
    if not last:
        up_ref, down_ref, far_ref = take(3)
    if first:
        moduli_ref, rim_ref = rim_ref, take(1)[0]
    (side_low, side_high, face_low, face_high) = take(4)
    _, extent_x, extent_y, extent_z = disp_ref.shape
    has_lower, has_upper, has_back, has_front = [flag_ref[i] for i in range(4)]
    is_odd = flag_ref[4] > 0.5
    place = lax.broadcasted_iota(jnp.int32, (8, extent_z), 0)
    all_but_last = lax.broadcasted_iota(jnp.int32, (extent_y, extent_z), 0) < extent_y - 1
    main = 3 * extent_y

    def back(begin, count):
        rows = slice(begin, begin + count)
        return jnp.where(is_odd, even_ref[rows, :], odd_ref[rows, :]) * has_back

    def front(begin, count):
        rows = slice(begin, begin + count)
        return jnp.where(is_odd, odd_ref[rows, :], even_ref[rows, :]) * has_front

    def ring(tile, above, below):
        return jnp.concatenate([tile, jnp.where(place == 0, above, jnp.where(place == 7, below, 0.0))], axis=0)

    if first:
        for m in range(2):
            at = slice((3 + m) * extent_x, (4 + m) * extent_x)
            begin = main + 8 + m * extent_y
            of_back = back(begin, extent_y)
            high = ring(own_up_ref[at, 0:extent_z], 0.0, of_back[extent_y - 1 :])
            low = ring(lower_ref[at, 0:extent_z] * has_lower, 0.0, back(main + 6 + m, 1))
            rim_ref[m] = high * SCALE
            rim_ref[2 + m] = low * SCALE
            rim_ref[4 + m] = jnp.where(all_but_last, of_back * SCALE, 0.0)
            rim_ref[6 + m] = jnp.where(all_but_last, moduli_ref[m, extent_x - 1] * SCALE, 0.0)

    def rows_of(tile_ref, weight, row, extra):
        made = []
        for p in range(3):
            at = main + extra + p if row is None else p * extent_y + row
            tile = tile_ref[p * extent_x : (p + 1) * extent_x, 0:extent_z]
            tile = tile if weight is None else tile * weight
            made.append(ring(tile, front(at, 1), back(at, 1)))
        return made

    def side(near, far, at, sign, target):
        parts = [features(near[p], far[p]) for p in range(3)]
        along_x = [ahead_row(parts[p][0]) - parts[p][0] for p in range(3)]
        along_y = [ahead_row(parts[p][1]) + parts[p][1] for p in range(3)]
        along_z = [ahead_row(parts[p][2]) + parts[p][2] for p in range(3)]
        found = stress_of(along_x, along_y, along_z, rim_ref[at], rim_ref[at + 1])
        for p in range(3):
            of_x, of_y, of_z = [found[c] for c in WHICH[p]]
            part_x = (behind_row(of_x) - of_x)[:extent_x]
            part_y = (behind_row(of_y) + of_y)[:extent_x]
            part_z = (behind_row(of_z) + of_z)[:extent_x]
            target[p] = spread_z(part_x + sign * part_y, part_z)

    side(rows_of(own_up_ref, None, extent_y - 1, 0), rows_of(upper_ref, has_upper, None, 0), 0, -1.0, side_high)
    side(rows_of(lower_ref, has_lower, None, 3), rows_of(own_down_ref, None, 0, 0), 2, 1.0, side_low)

    def face(near, far, at, sign, target):
        parts_near = [features(value, ahead_row(value)) for value in near]
        parts_far = [features(value, ahead_row(value)) for value in far]
        along_x = [parts_far[p][0] - parts_near[p][0] for p in range(3)]
        along_y = [parts_far[p][1] + parts_near[p][1] for p in range(3)]
        along_z = [parts_far[p][2] + parts_near[p][2] for p in range(3)]
        found = stress_of(along_x, along_y, along_z, rim_ref[at], rim_ref[at + 1])
        for p in range(3):
            of_x, of_y, of_z = [found[c] for c in WHICH[p]]
            of_x = of_x * sign
            plain = (of_x - of_y) + behind_row(of_x + of_y)
            target[p] = spread_z(plain, of_z + behind_row(of_z))

    layer_of = lambda side_of: [side_of(p * extent_y, extent_y) for p in range(3)]
    own_layer = lambda x: [disp_ref[p, x] for p in range(3)]
    face(layer_of(back), own_layer(0), 4, 1.0, face_low)
    face(own_layer(extent_x - 1), layer_of(front), 6, -1.0, face_high)

    for x in range(extent_x):
        step_mass = TIME_STEP / mass_ref[x]
        for p in range(3):
            at = (p * extent_x + x) * extent_y
            load = inner_ref[p, x] + contact_ref[at : at + extent_y, :]
            if x == 0:
                load = load + face_low[p]
            if x == extent_x - 1:
                load = load + face_high[p]
            begin = load[:8] + jnp.where(place == 0, side_low[p, x : x + 1, :], 0.0)
            end = load[extent_y - 8 :] + jnp.where(place == 7, side_high[p, x : x + 1, :], 0.0)
            load = jnp.concatenate([begin, load[8 : extent_y - 8], end] if extent_y > 16 else [begin, end], axis=0)
            speed = vel_ref[p, x] + step_mass * load
            new_vel_ref[p, x] = speed
            new_disp_ref[p, x] = disp_ref[p, x] + TIME_STEP * speed
    if not last:
        store_messages(new_disp_ref, base_ref, node_ref, hot_ref[...], up_ref, down_ref, far_ref)


def per_device(displacement, velocity, moduli, nodal_mass, segment_node, segment_base, contact_bin, element_tile):
    shape = displacement.shape
    _, extent_x, extent_y, extent_z = shape
    steps = contact_bin.shape[0]
    segments = segment_node.shape[0]
    blocks = segments // SEG
    bin_count = lax.axis_size("bin")
    bin_at = lax.axis_index("bin")
    dom_at, dom_count = lax.axis_index("dom"), lax.axis_size("dom")
    own_device = dom_at * bin_count + bin_at
    checks = (bin_at > 0, bin_at < bin_count - 1, dom_at > 0, dom_at < dom_count - 1, (dom_at & 1) == 1)
    flags = jnp.concatenate([jnp.stack(checks).astype(F32), own_device[None].astype(F32)])
    node = segment_node.reshape(blocks, SEG)
    bins = contact_bin[:, :, 0]
    rows = 3 * extent_x
    wide = extent_z + SEG
    struct = lambda *dims: jax.ShapeDtypeStruct(dims, F32)
    layer_rows = 3 * extent_y + 8
    full = lambda *dims: pl.BlockSpec(dims, lambda i: (0,) * len(dims))

    first_outs = [
        struct(rows + 16, wide),
        struct(rows + 8, wide),
        struct(rows + 8, SEG),
        jax.ShapeDtypeStruct((extent_z, segments), BF16),
    ]
    first_args = (flags, displacement, segment_base, node, moduli, bins)
    first_specs = [SCALARS] + [full(*v.shape) for v in first_args[1:]]
    first_specs[4] = pl.BlockSpec((2, extent_x, 8, extent_z), lambda i: (0, 0, extent_y // 8 - 1, 0))
    up, down, far, hot = pl.pallas_call(
        first_body,
        grid=(1,),
        out_shape=first_outs,
        in_specs=first_specs,
        out_specs=[full(*v.shape) for v in first_outs],
        compiler_params=pltpu.CompilerParams(vmem_limit_bytes=60 * 1024 * 1024),
        cost_estimate=pl.CostEstimate(flops=1_000, bytes_accessed=1_000, transcendentals=0),
    )(*first_args)
    (turned,) = call(
        functools.partial(turn_body, extent_z),
        [jax.ShapeDtypeStruct((segments, extent_z), BF16)],
        specs=[WHOLE],
    )(node)
    (tile_places,) = call(
        tile_body, [jax.ShapeDtypeStruct((8, segments), jnp.int32)], specs=[SCALARS] + [WHOLE] * 3
    )(flags, element_tile, node, hot)
    heat = jnp.zeros((blocks, SEG), F32)
    rim = moduli
    for step in range(steps):
        lower = cycled(up, "bin", 1)
        upper = cycled(down, "bin", -1)
        others = jnp.stack([cycled(far, "bin", shift) for shift in range(2, bin_count - 1)])
        first, last = step == 0, step == steps - 1
        (inner,) = call(
            inner_body,
            [struct(*shape)],
            [pltpu.VMEM((extent_x, 9, extent_y, extent_z), F32), pltpu.VMEM((extent_x + 1, 6, extent_y, extent_z), F32)],
            [WHOLE] * 2,
        )(displacement, moduli)
        if first:
            of_bins = [far[rows : rows + steps, :blocks]]
            of_bins += [v[rows : rows + steps, extent_z : extent_z + blocks] for v in (lower, upper)]
            of_bins += [v[rows : rows + steps, :blocks] for v in others]
            all_bins = jnp.concatenate(of_bins, axis=1).astype(jnp.int32)
        layer = lambda at, count=3: pl.BlockSpec((count, 1, extent_y, extent_z), lambda i: (0, at, 0, 0))
        send_rows = layer_rows + (2 * extent_y if first else 0)
        layer_args = [flags, displacement, displacement, lower, upper, inner, others]
        layer_specs = [SCALARS, layer(0), layer(extent_x - 1), full(*lower.shape), full(*upper.shape)]
        layer_specs += [pl.BlockSpec(memory_space=pl.ANY)] * 2
        if first:
            layer_args.append(moduli)
            layer_specs.append(layer(extent_x - 1, 2))
        to_even, to_odd = pl.pallas_call(
            functools.partial(layer_body, first),
            grid=(1,),
            out_shape=[struct(send_rows, extent_z)] * 2,
            in_specs=layer_specs,
            out_specs=[full(send_rows, extent_z)] * 2,
            compiler_params=pltpu.CompilerParams(vmem_limit_bytes=VMEM_BYTES),
            cost_estimate=pl.CostEstimate(flops=1_000, bytes_accessed=1_000, transcendentals=0),
        )(*layer_args)
        relay = swapped(to_odd, "dom")
        near_blocks = 2 * blocks
        far_blocks = blocks * (bin_count - 2)
        pair_scratch = lambda count: [
            pltpu.VMEM((count + 1, 3, SEG, SEG), F32),
            pltpu.SMEM((bin_count * (count + 2),), jnp.int32),
        ]
        (sums,) = call(
            functools.partial(near_body, bin_count),
            [struct(blocks, 4, 8, SEG)],
            pair_scratch(near_blocks),
            [SCALARS, WHOLE, WHOLE, pl.BlockSpec(memory_space=pl.ANY)],
        )(all_bins[step], far, lower, to_odd)
        to_even, sums, relay = lax.optimization_barrier((to_even, sums, relay))
        of_even = swapped(to_even, "dom")
        of_odd = relayed(relay, "dom")
        pair_args = [all_bins[step], far, upper, others, sums, node, turned, heat]
        if last:
            pair_args += [tile_places, flags]
        contact, heat = call(
            functools.partial(rest_body, bin_count, last),
            [struct(3 * extent_x * extent_y, extent_z), struct(8, TILE_DEV) if last else struct(blocks, SEG)],
            pair_scratch(far_blocks) + [pltpu.VMEM((8, segments), F32)],
            [SCALARS] + [WHOLE] * (len(pair_args) - 2) + [SCALARS if last else WHOLE],
        )(*pair_args)
        if last:
            heat, of_even, of_odd = lax.optimization_barrier((heat, of_even, of_odd))
        update_args = [flags, displacement, velocity, nodal_mass, inner, contact, up, down, lower, upper]
        update_args += [of_even, of_odd, rim]
        update_outs = [struct(*shape), struct(*shape)]
        if not last:
            update_args += [segment_base, node, hot]
            update_outs += [struct(rows, wide), struct(rows, wide), struct(rows, SEG)]
        if first:
            update_outs.append(struct(8, extent_y, extent_z))
        made = call(
            functools.partial(update_body, first, last),
            update_outs,
            [pltpu.VMEM((3, extent_x, extent_z), F32)] * 2 + [pltpu.VMEM((3, extent_y, extent_z), F32)] * 2,
            [SCALARS] + [WHOLE] * (len(update_args) - 1),
        )(*update_args)
        displacement, velocity = made[:2]
        if not last:
            up, down, far = made[2:5]
        if first:
            rim = made[-1]
    got = swapped(heat[1:3], "dom")
    got, velocity = lax.optimization_barrier((got, velocity))
    passed = relayed(got[1], "dom")
    tile_heat = heat[0] + got[0] + passed
    return displacement, velocity, tile_heat


def solution(mesh):
    placed = (
        P(None, "dom", "bin", None),
        P(None, "dom", "bin", None),
        P(None, "dom", "bin", None),
        P("dom", "bin", None),
        P(("dom", "bin")),
        P(None, ("dom", "bin")),
        P(None, ("dom", "bin"), None),
        P("dom", "bin", None),
    )
    return jax.shard_map(
        per_device,
        mesh=mesh,
        in_specs=placed,
        out_specs=(P(None, "dom", "bin", None), P(None, "dom", "bin", None), P(("dom", "bin"))),
        check_vma=False,
    )
```
